32 devices in a mesh: expert: 8 (over z, x), rows: 4 (over y, core).
Axes of the slice: x: 2, y: 2, z: 4, core: 2. Of those that a mesh axis runs over, the one named last changes fastest.
Arguments:
- patches: bfloat16 [32, 1024, 384], P(('expert', 'rows')), may hold values from -6 to 6
- image_ids: int32 [32, 1024], P(('expert', 'rows')), may hold values from 0 to 7, as said below
- first_gain: float32 [384], replicated, may hold values from 0.5 to 1.5
- qkv_weight: bfloat16 [384, 1152], replicated, may hold values from -0.3125 to 0.3125
- proj_weight: bfloat16 [384, 384], replicated, may hold values from -1.25 to 1.25
- second_gain: float32 [384], replicated, may hold values from 0.5 to 1.5
- slot_params: bfloat16 [384, 16], P(None, 'expert'), may hold values from -0.15625 to 0.15625
- up_weight: bfloat16 [16, 384, 1536], P('expert'), may hold values from -1.25 to 1.25
- down_weight: bfloat16 [16, 1536, 384], P('expert'), may hold values from -6 to 6
- cotangent: bfloat16 [32, 1024, 384], P(('expert', 'rows')), may hold values from -6 to 6
Outputs:
- output: bfloat16 [32, 1024, 384], P(('expert', 'rows'))
- patch_grad: float32 [32, 1024, 384], P(('expert', 'rows'))
- first_grad: float32 [384], replicated
- qkv_grad: float32 [384, 1152], replicated
- proj_grad: float32 [384, 384], replicated
- second_grad: float32 [384], replicated
- slot_grad: float32 [384, 16], P(None, 'expert')
- up_grad: float32 [16, 384, 1536], P('expert')
- down_grad: float32 [16, 1536, 384], P('expert')
The draws below stay inside these ranges and needn't reach their ends.
Inputs may be any that keep to these rules, and one draw needn't show every extreme that they name: `image_ids`: in each row the ids start at 0 and rise by one at the first patch of each next image; a row holds 4 to 8 images, and some row holds 8.
All inputs are finite; a program needn't handle non-finite values.
Results may differ from the reference program's by a relative error of at most 0.017.
Values may be sent and summed in bfloat16 or wider, within the bound.
No kernel may reach another device: no remote copies, remote signals or barrier semaphores. Data moves between devices by JAX's collectives and lax.ppermute only.
A program may use at most 128 MiB of HBM per device.

```python
import jax
import jax.numpy as jnp
from jax import lax

D = 384
HEADS = 6
HEAD_DIM = 64
FF = 1536
SEQ = 1024
IMG_ROW = 8
EXPERTS = 16
ROWS = 32


def draw_image_ids(key, part):
    key = jax.random.fold_in(key, 7)
    count_key, full_key, cut_key = jax.random.split(key, 3)
    counts = jax.random.randint(count_key, (ROWS,), IMG_ROW // 2, IMG_ROW + 1)
    fullest = jax.random.randint(full_key, (), 0, ROWS)
    counts = jnp.where(jnp.arange(ROWS) == fullest, IMG_ROW, counts)

    def row_cuts(row_key):
        return jax.random.permutation(row_key, SEQ - 1)[:IMG_ROW - 1] + 1
    cuts = jax.vmap(row_cuts)(jax.random.split(cut_key, ROWS))
    order = jnp.arange(IMG_ROW - 1)
    cuts = jnp.where(order[None, :] < counts[:, None] - 1, cuts, SEQ)
    places = jnp.arange(SEQ)
    return jnp.sum((cuts[:, None, :] <= places[None, :, None]).astype(jnp.int32), axis=-1).astype(jnp.int32)


def levels(key, shape, cuts, smallest, largest):
    loudness = 1.0
    for position, shards_of in cuts:
        steps = jax.random.uniform(jax.random.fold_in(jax.random.fold_in(key, 6), position), (shards_of,), jnp.float32, smallest / len(cuts), largest / len(cuts))
        loudness = loudness * jnp.repeat(jnp.exp(steps), shape[position] // shards_of).reshape((-1,) + (1,) * (len(shape) - 1 - position))
    return loudness


def gaussian(rng, shape, spread, reach, cuts=(), kind=jnp.bfloat16):
    loudness = levels(rng, shape, cuts, -0.22, 0.18) if cuts else 1.0
    values = jax.random.normal(rng, shape, jnp.float32) * spread * loudness
    return jnp.minimum(jnp.maximum(values, -reach), reach).astype(kind)


def setup_inputs(seed: int = 0) -> dict:
    arg_keys = jax.random.split(jax.random.key(seed), 11)
    patches = gaussian(arg_keys[0], (ROWS, SEQ, D), 1.0, 6.0, ((0, 32),))
    image_ids = draw_image_ids(jax.random.fold_in(arg_keys[10], 71), 0)
    first_gain = jnp.clip(1.0 + 0.1 * jax.random.normal(arg_keys[2], (D,), jnp.float32), 0.5, 1.5)
    qkv_weight = gaussian(arg_keys[3], (D, 3 * D), D ** -0.5, 0.3125)
    proj_weight = gaussian(arg_keys[4], (D, D), (D // 16) ** -0.5, 1.25)
    second_gain = jnp.clip(1.0 + 0.1 * jax.random.normal(arg_keys[5], (D,), jnp.float32), 0.5, 1.5)
    slot_params = gaussian(arg_keys[6], (D, EXPERTS), (4 * D) ** -0.5, 0.15625, ((1, 8),))
    up_weight = gaussian(arg_keys[7], (EXPERTS, D, FF), (D // 16) ** -0.5, 1.25, ((0, 8),))
    down_weight = gaussian(arg_keys[8], (EXPERTS, FF, D), 1 ** -0.5, 6.0, ((0, 8),))
    cotangent = gaussian(arg_keys[9], (ROWS, SEQ, D), 1.0, 6.0, ((0, 32),))
    return {"patches": patches, "image_ids": image_ids, "first_gain": first_gain, "qkv_weight": qkv_weight, "proj_weight": proj_weight, "second_gain": second_gain, "slot_params": slot_params, "up_weight": up_weight, "down_weight": down_weight, "cotangent": cotangent}


epsilon = 1e-06
masked_fill = -1e+30
highest = lax.Precision.HIGHEST

@jax.custom_vjp
def low(v):
    return lax.optimization_barrier(v.astype(jnp.bfloat16)).astype(jnp.float32)

@jax.custom_vjp
def low_back(v):
    return v

def low_keep(v):
    return (low(v), None)

def low_pass(kept, grad):
    return (grad,)

def back_keep(v):
    return (v, None)

def back_low(kept, grad):
    return (low(grad),)
low.defvjp(low_keep, low_pass)
low_back.defvjp(back_keep, back_low)

def layer_norm(values, gain):
    centred = values - lax.optimization_barrier(jnp.mean(values, axis=-1, keepdims=True))
    return centred * lax.rsqrt(lax.optimization_barrier(jnp.mean(centred * centred, axis=-1, keepdims=True)) + epsilon) * gain

def attend(queries, keys, values, key_ids):
    block = min(512, SEQ)
    count = SEQ // block
    factor = HEAD_DIM ** (-0.5)

    def one_block(item):
        query_block, block_ids = item
        scores = low_back(jnp.einsum('qhd,khd->hqk', query_block, keys, precision=highest) * factor)
        same = block_ids[:, None] == key_ids[None, :]
        scores = jnp.where(same[None], scores, masked_fill)
        probs = low(jax.nn.softmax(scores, axis=-1))
        return jnp.einsum('hqk,khd->qhd', probs, values, precision=highest)
    mixed = lax.map(jax.checkpoint(one_block), (queries.reshape(count, block, HEADS, HEAD_DIM), key_ids.reshape(count, block)))
    return mixed.reshape(SEQ, HEADS * HEAD_DIM)

def row_forward(row_patches, row_ids, weights):
    first_gain, qkv_weight, proj_weight, second_gain, slot_params, up_weight, down_weight = weights
    first_in = low(layer_norm(row_patches, first_gain))
    qkv = low_back(low(jnp.dot(first_in, qkv_weight, precision=highest)))
    shape = (SEQ, HEADS, HEAD_DIM)
    mixed = attend(qkv[:, :D].reshape(shape), qkv[:, D:2 * D].reshape(shape), qkv[:, 2 * D:].reshape(shape), row_ids)
    attn = low_back(low(mixed))
    resid = row_patches + low_back(jnp.dot(attn, proj_weight, precision=highest))
    second_in = low(layer_norm(resid, second_gain))
    logits = low_back(jnp.dot(second_in, slot_params, precision=highest))
    member = (row_ids[:, None] == jnp.arange(IMG_ROW, dtype=jnp.int32)[None, :]).astype(jnp.float32)
    masked = jnp.where(member[:, :, None] > 0, logits[:, None, :], masked_fill)
    top = lax.optimization_barrier(jnp.max(masked, axis=0, keepdims=True))
    raised = member[:, :, None] * jnp.exp(masked - top)
    present = lax.optimization_barrier(jnp.max(member, axis=0))
    dispatch = raised / (lax.optimization_barrier(jnp.sum(raised, axis=0, keepdims=True)) + (1.0 - present)[None, :, None])
    slot_in = low_back(low(jnp.einsum('pjs,pd->jsd', low(dispatch), second_in, precision=highest)))
    pre = low_back(jnp.einsum('jsd,sdf->jsf', slot_in, up_weight, precision=highest))
    hidden = low(jax.nn.gelu(pre, approximate=False))
    slot_out = low_back(low(jnp.einsum('jsf,sfd->jsd', hidden, down_weight, precision=highest)))
    combine = low(member[:, :, None] * jax.nn.softmax(logits, axis=-1)[:, None, :])
    moe = low_back(jnp.einsum('pjs,jsd->pd', combine, slot_out, precision=highest))
    return resid + moe

def reference(patches, image_ids, first_gain, qkv_weight, proj_weight, second_gain, slot_params, up_weight, down_weight, cotangent):
    weights = tuple((value.astype(jnp.float32) for value in (first_gain, qkv_weight, proj_weight, second_gain, slot_params, up_weight, down_weight)))
    group = 4 if ROWS % 4 == 0 else 1
    count = ROWS // group
    inputs = patches.astype(jnp.float32).reshape(count, group, SEQ, D)
    image_rows = image_ids.astype(jnp.int32).reshape(count, group, SEQ)
    grads_in = cotangent.astype(jnp.float32).reshape(count, group, SEQ, D)

    def group_step(running, item):
        group_patches, group_ids, group_grad = item

        def forward(values, params):
            return jax.vmap(row_forward, in_axes=(0, 0, None))(values, group_ids, params)
        result, pull = jax.vjp(forward, group_patches, weights)
        grad_patches, grad_weights = pull(group_grad)
        return (jax.tree.map(jnp.add, running, grad_weights), (result, grad_patches))
    start = jax.tree.map(jnp.zeros_like, weights)
    totals, (results, grad_patches) = lax.scan(group_step, start, (inputs, image_rows, grads_in))
    return (results.reshape(ROWS, SEQ, D).astype(jnp.bfloat16), grad_patches.reshape(ROWS, SEQ, D), totals[0], totals[1], totals[2], totals[3], totals[4], totals[5], totals[6])
```

```python
import jax
import jax.numpy as jnp
from jax import lax
from jax.experimental import pallas as pl
from jax.experimental.pallas import tpu as pltpu
from jax.sharding import PartitionSpec as P

HEADS = 6
IMG_ROW = 8
LANES = 128
TILE = 256

epsilon = 1e-06
masked_fill = -1e30
low = jnp.bfloat16
full = jnp.float32
whole_vmem = pl.BlockSpec(memory_space=pltpu.VMEM)
both_axes = ("expert", "rows")


def dot(left, right, left_dim=1, right_dim=0):
    return lax.dot_general(
        left, right, (((left_dim,), (right_dim,)), ((), ())), preferred_element_type=full
    )


def shape_of(shape, dtype):
    return jax.ShapeDtypeStruct(shape, dtype)


def params(mib):
    return pltpu.CompilerParams(vmem_limit_bytes=mib << 20)


def norm_parts(values):
    centred = values - jnp.mean(values, axis=-1, keepdims=True)
    factor = lax.rsqrt(jnp.mean(centred * centred, axis=-1, keepdims=True) + epsilon)
    return centred * factor, factor


def norm_back(grad_norm, normed, factor, gain):
    scaled = grad_norm * gain
    return factor * (
        scaled
        - jnp.mean(scaled, axis=-1, keepdims=True)
        - normed * jnp.mean(scaled * normed, axis=-1, keepdims=True)
    )


def member_of(ids):
    images = lax.broadcasted_iota(jnp.int32, (IMG_ROW, ids.shape[1]), 0)
    return images == ids


def gelu_parts(pre):
    cdf = 0.5 * (1.0 + lax.erf(pre * 0.7071067811865476))
    pdf = 0.3989422804014327 * jnp.exp(-0.5 * pre * pre)
    return cdf, pdf


def attend_kernel(
    x_ref, ids_ref, gain_ref, weight_ref,
    probs_ref, attn_ref, queries_ref, keys_ref, value_rows_ref, first_ref,
    key_rows, values, mask_rows, same,
):
    pair = pl.program_id(0)
    length, width = x_ref.shape
    pairs = width // LANES
    half = LANES // 2

    @pl.when(pair == 0)
    def _():
        normed, _ = norm_parts(x_ref[...].astype(full))
        first_in = (normed * gain_ref[...]).astype(low)
        first_ref[...] = first_in.T
        turned = dot(weight_ref[...], first_in, 0, 1).astype(low)
        queries_ref[...] = turned[:width].reshape(pairs, LANES, length)
        keys_ref[...] = turned[width : 2 * width].reshape(pairs, LANES, length)
        values[...] = turned[2 * width :].reshape(pairs, LANES, length)
        rows = dot(first_in, weight_ref[:, width:]).astype(low)
        for index in range(pairs):
            key_rows[index] = rows[:, index * LANES : (index + 1) * LANES]
            value_rows_ref[index] = rows[:, width + index * LANES : width + (index + 1) * LANES]
        images = lax.broadcasted_iota(jnp.int32, (LANES, length), 0)
        matching = images == ids_ref[...]
        same[...] = matching.astype(full).astype(low)
        other = jnp.where(jnp.logical_or(matching, images >= IMG_ROW), 0.0, masked_fill)
        mask_rows[...] = other.T.astype(low)

    keys = jnp.concatenate([key_rows[pair], mask_rows[...]], axis=1)
    scaled = queries_ref[pair] * jnp.asarray(half**-0.5, low)
    none = jnp.zeros((half, TILE), low)
    for head in range(2):
        value = values[pair, head * half : (head + 1) * half, :]
        for start in range(0, length, TILE):
            span = slice(start, start + TILE)
            query = scaled[head * half : (head + 1) * half, span]
            parts = [query, none] if head == 0 else [none, query]
            scores = dot(keys, jnp.concatenate(parts + [same[:, span]], axis=0))
            top = jnp.max(scores, axis=0, keepdims=True)
            raised = jnp.exp(scores - top)
            total = jnp.sum(raised, axis=0, keepdims=True)
            probs = (raised * (1.0 / total)).astype(low)
            probs_ref[head, :, span] = probs
            attn_ref[0, head * half : (head + 1) * half, span] = dot(value, probs).astype(low)


def attend(patches, ids, gain, weight):
    length, width = patches.shape
    pairs = width // LANES
    stack = (pairs, LANES, length)
    rows = (pairs, length, LANES)
    return pl.pallas_call(
        attend_kernel,
        grid=(pairs,),
        in_specs=[whole_vmem] * 4,
        out_specs=[
            pl.BlockSpec((2, length, length), lambda pair: (pair, 0, 0)),
            pl.BlockSpec((1, LANES, length), lambda pair: (pair, 0, 0)),
            pl.BlockSpec(stack, lambda pair: (0, 0, 0)),
            pl.BlockSpec(stack, lambda pair: (0, 0, 0)),
            pl.BlockSpec(rows, lambda pair: (0, 0, 0)),
            pl.BlockSpec((width, length), lambda pair: (0, 0)),
        ],
        out_shape=[
            shape_of((2 * pairs, length, length), low),
            shape_of(stack, low),
            shape_of(stack, low),
            shape_of(stack, low),
            shape_of(rows, low),
            shape_of((width, length), low),
        ],
        scratch_shapes=[
            pltpu.VMEM(rows, low),
            pltpu.VMEM(stack, low),
            pltpu.VMEM((length, LANES), low),
            pltpu.VMEM((LANES, length), low),
        ],
        compiler_params=params(48),
        name="attend",
    )(patches, ids, gain, weight)


def slot_rows(slots):
    experts = slots.shape[0]
    row = lax.broadcasted_iota(jnp.int32, (experts * IMG_ROW, experts), 0) // IMG_ROW
    column = lax.broadcasted_iota(jnp.int32, (experts * IMG_ROW, experts), 1)
    return dot((row == column).astype(full).astype(low), slots).astype(low)


def route_kernel(
    x_ref, attn_ref, proj_ref, gain_ref, slots_ref, ids_ref, cotangent_ref,
    resid_ref, second_ref, dispatch_ref, combine_ref, send_ref,
):
    length, width = x_ref.shape
    experts = slots_ref.shape[0]
    shape = (experts, IMG_ROW, length)
    resid = x_ref[...].astype(full) + dot(attn_ref[...].reshape(width, length), proj_ref[...], 0, 0)
    resid_ref[...] = resid
    normed, _ = norm_parts(resid)
    second_in = (normed * gain_ref[...]).astype(low)
    second_ref[...] = second_in
    logits = dot(slot_rows(slots_ref[...]), second_in, 1, 1).reshape(shape)
    member = member_of(ids_ref[...])
    raised = jnp.exp(logits - jnp.max(logits, axis=0, keepdims=True))
    combine = raised * (1.0 / jnp.sum(raised, axis=0, keepdims=True))
    combine_ref[...] = combine
    combine_low = jnp.where(member[None], combine, 0.0).astype(low).reshape(-1, length)
    masked = jnp.where(member[None], logits, masked_fill)
    top = jnp.max(masked, axis=2, keepdims=True)
    raised = jnp.where(member[None], jnp.exp(masked - top), 0.0)
    present = jnp.max(member.astype(full), axis=1, keepdims=True)
    total = jnp.sum(raised, axis=2, keepdims=True) + (1.0 - present)[None]
    dispatch = raised * (1.0 / total)
    dispatch_ref[...] = dispatch
    dispatch_low = dispatch.astype(low).reshape(-1, length)
    block = (send_ref.shape[0], send_ref.shape[2], width)
    send_ref[:, 0] = dot(dispatch_low, second_in).astype(low).reshape(block)
    send_ref[:, 1] = dot(combine_low, cotangent_ref[...]).astype(low).reshape(block)


def route(patches, attn, proj, gain, slots, ids, cotangent, groups):
    length, width = patches.shape
    experts = slots.shape[0]
    own = experts // groups * IMG_ROW
    return pl.pallas_call(
        route_kernel,
        in_specs=[whole_vmem] * 7,
        out_specs=[whole_vmem] * 5,
        out_shape=[
            shape_of((length, width), full),
            shape_of((length, width), low),
            shape_of((experts, IMG_ROW, length), full),
            shape_of((experts, IMG_ROW, length), full),
            shape_of((groups, 2, own, width), low),
        ],
        compiler_params=params(48),
        name="route",
    )(patches, attn, proj, gain, slots, ids, cotangent)


def own_rows(received, expert):
    groups, _, width = received.shape
    rows = received[:, expert * IMG_ROW : (expert + 1) * IMG_ROW]
    return rows.reshape(groups * IMG_ROW, width).astype(low)


def expert_kernel(received_ref, up_ref, down_ref, back_ref, stage):
    expert = pl.program_id(0)
    groups, _, own, width = received_ref.shape
    slots = received_ref[:, 0].astype(full)
    grads = received_ref[:, 1].astype(full)
    for index in range(own // IMG_ROW):

        @pl.when(expert == index)
        def _():
            up = up_ref[0]
            down = down_ref[0]
            pre = dot(own_rows(slots, index), up)
            cdf, pdf = gelu_parts(pre)
            out = dot((pre * cdf).astype(low), down)
            grad_hidden = dot(own_rows(grads, index), down, 1, 1)
            grad_pre = (grad_hidden * (cdf + pre * pdf)).astype(low)
            grad_slots = dot(grad_pre, up, 1, 1)
            rows = slice(index * IMG_ROW, (index + 1) * IMG_ROW)
            stage[0, :, rows] = out.reshape(groups, IMG_ROW, width)
            stage[1, :, rows] = grad_slots.reshape(groups, IMG_ROW, width)

    @pl.when(expert == own // IMG_ROW - 1)
    def _():
        back_ref[:, 0] = stage[0].astype(low)
        back_ref[:, 1] = stage[1].astype(low)


def run_experts(received, up, down):
    groups, _, own, width = received.shape
    experts, _, hidden = up.shape
    return pl.pallas_call(
        expert_kernel,
        grid=(experts,),
        in_specs=[
            whole_vmem,
            pl.BlockSpec((1, width, hidden), lambda expert: (expert, 0, 0)),
            pl.BlockSpec((1, hidden, width), lambda expert: (expert, 0, 0)),
        ],
        out_specs=pl.BlockSpec(received.shape, lambda expert: (0, 0, 0, 0)),
        out_shape=shape_of(received.shape, low),
        scratch_shapes=[pltpu.VMEM((2, groups, own, width), full)],
        compiler_params=params(48),
        name="run_experts",
    )(received, up, down)


def slots_back_kernel(
    back_ref, second_ref, resid_ref, dispatch_ref, combine_ref, ids_ref, cotangent_ref,
    slots_ref, gain_ref, attn_ref, proj_ref,
    output_ref, grad_resid_ref, grad_attn_ref, delta_ref, sums_ref,
):
    length, width = resid_ref.shape
    experts = slots_ref.shape[0]
    count = experts * IMG_ROW
    shape = (experts, IMG_ROW, length)
    slot_out = back_ref[:, 0].reshape(count, width)
    grad_slots = back_ref[:, 1].reshape(count, width)
    cotangent = cotangent_ref[...]
    second_in = second_ref[...]
    combine = combine_ref[...]
    dispatch = dispatch_ref[...]
    member = member_of(ids_ref[...])
    grad_combine = dot(slot_out, cotangent, 1, 1).reshape(shape)
    grad_own = jnp.sum(jnp.where(member[None], grad_combine, 0.0), axis=1, keepdims=True)
    inner = jnp.sum(combine * grad_own, axis=0, keepdims=True)
    grad_logits = combine * (grad_own - inner)
    grad_dispatch = dot(grad_slots, second_in, 1, 1).reshape(shape)
    weighted = jnp.sum(dispatch * grad_dispatch, axis=2, keepdims=True)
    routed = jnp.sum(dispatch * (grad_dispatch - weighted), axis=1, keepdims=True)
    grad_low = (grad_logits + routed).astype(low).reshape(count, length)
    row = lax.broadcasted_iota(jnp.int32, (experts, count), 0) * IMG_ROW
    column = lax.broadcasted_iota(jnp.int32, (experts, count), 1)
    grad_low = dot((row == column).astype(full).astype(low), grad_low).astype(low)
    slot_grad = dot(grad_low, second_in)
    mixing = jnp.concatenate([dispatch.astype(low).reshape(count, length), grad_low], axis=0)
    sources = jnp.concatenate([grad_slots, slots_ref[...]], axis=0)
    grad_second = dot(mixing, sources, 0, 0)
    resid = resid_ref[...]
    combine_low = jnp.where(member[None], combine, 0.0).astype(low).reshape(count, length)
    output_ref[...] = (resid + dot(combine_low, slot_out, 0, 0)).astype(low)
    normed, factor = norm_parts(resid)
    second_grad = jnp.sum(grad_second * normed, axis=0, keepdims=True)
    grad_resid = cotangent.astype(full) + norm_back(grad_second, normed, factor, gain_ref[...])
    grad_resid_ref[...] = grad_resid
    grad_branch = grad_resid.astype(low)
    attn = attn_ref[...].reshape(width, length)
    proj_grad = dot(attn, grad_branch).astype(low)
    grad_attn = dot(proj_ref[...], grad_branch, 1, 1).astype(low)
    grad_attn_ref[...] = grad_attn.reshape(grad_attn_ref.shape)
    product = grad_attn.astype(full) * attn.astype(full)
    heads = 2 * width // LANES
    delta_ref[...] = jnp.sum(product.reshape(heads, width // heads, length), axis=1)
    slot_low = slot_grad.astype(low)
    second_low = jnp.broadcast_to(second_grad, (16, width)).astype(low)
    for index in range(width // LANES):
        lanes = slice(index * LANES, (index + 1) * LANES)
        sums_ref[index * width : (index + 1) * width] = proj_grad[:, lanes]
        base = width * width // LANES + index * experts
        sums_ref[base : base + experts] = slot_low[:, lanes]
        base = (width + experts) * width // LANES + index * 16
        sums_ref[base : base + 16] = second_low[:, lanes]


def slots_back(back, second_in, resid, dispatch, combine, ids, cotangent, slots, gain, attn, proj):
    length, width = resid.shape
    experts = slots.shape[0]
    pairs = width // LANES
    return pl.pallas_call(
        slots_back_kernel,
        in_specs=[whole_vmem] * 11,
        out_specs=[whole_vmem] * 5,
        out_shape=[
            shape_of((length, width), low),
            shape_of((length, width), full),
            shape_of((pairs, LANES, length), low),
            shape_of((2 * pairs, length), full),
            shape_of(((width + experts + 16) * pairs, LANES), low),
        ],
        compiler_params=params(56),
        name="slots_back",
    )(back, second_in, resid, dispatch, combine, ids, cotangent, slots, gain, attn, proj)


def attend_back_kernel(
    first_head, probs_ref, queries_ref, keys_ref, values_ref, grad_attn_ref, delta_ref, first_ref,
    grads_ref, sums_ref, grad_scores,
):
    width, length = first_ref.shape
    half = LANES // 2
    factor = half**-0.5
    none = jnp.zeros((half, TILE), low)
    for head in range(2):
        rows = slice(head * half, (head + 1) * half)
        grad_mixed = grad_attn_ref[0, rows, :]
        delta = delta_ref[first_head + head : first_head + head + 1, :]
        for start in range(0, length, TILE):
            span = slice(start, start + TILE)
            grad = grad_mixed[:, span]
            parts = [grad, none] if head == 0 else [none, grad]
            grad_probs = dot(values_ref[0], jnp.concatenate(parts, axis=0))
            probs = probs_ref[head, :, span].astype(full)
            grad_scores[head, :, span] = (probs * (grad_probs - delta[:, span])).astype(low)
        grads_ref[2, rows, :] = dot(grad_mixed, probs_ref[head], 1, 1).astype(low)
        grads_ref[0, rows, :] = (dot(keys_ref[0, rows, :], grad_scores[head]) * factor).astype(low)
        grads_ref[1, rows, :] = (
            dot(queries_ref[0, rows, :], grad_scores[head], 1, 1) * factor
        ).astype(low)
    sums = dot(first_ref[...], grads_ref[...].reshape(3 * LANES, length), 1, 1).astype(low)
    for index in range(3):
        sums_ref[index * width : (index + 1) * width] = sums[:, index * LANES : (index + 1) * LANES]


def attend_back(pair, probs, queries, keys, values, grad_attn, delta, first_in):
    width, length = first_in.shape

    def kernel(*refs):
        attend_back_kernel(2 * pair, *refs)

    block = pl.BlockSpec((1, LANES, length), lambda _: (pair, 0, 0))
    return pl.pallas_call(
        kernel,
        grid=(1,),
        in_specs=[
            pl.BlockSpec((2, length, length), lambda _: (pair, 0, 0)),
            block,
            block,
            pl.BlockSpec((1, length, LANES), lambda _: (pair, 0, 0)),
            block,
            whole_vmem,
            whole_vmem,
        ],
        out_specs=[whole_vmem, whole_vmem],
        out_shape=[shape_of((3, LANES, length), low), shape_of((3 * width, LANES), low)],
        scratch_shapes=[pltpu.VMEM((2, length, length), low)],
        compiler_params=params(48),
        name="attend_back",
    )(probs, queries, keys, values, grad_attn, delta, first_in)


def patch_back_kernel(x_ref, gain_ref, weight_ref, resid_ref, *refs):
    pieces, result_ref = refs[:-1], refs[-1]
    grads = jnp.concatenate([piece[part] for part in range(3) for piece in pieces], axis=0)
    grad_first = dot(weight_ref[...], grads).T
    normed, factor = norm_parts(x_ref[...].astype(full))
    result_ref[...] = resid_ref[...] + norm_back(grad_first, normed, factor, gain_ref[...])


def patch_back(patches, gain, weight, grad_resid, pieces):
    return pl.pallas_call(
        patch_back_kernel,
        in_specs=[whole_vmem] * (4 + len(pieces)),
        out_specs=whole_vmem,
        out_shape=shape_of(patches.shape, full),
        compiler_params=params(48),
        name="patch_back",
    )(patches, gain, weight, grad_resid, *pieces)


def weights_kernel(copies, *refs):
    received = refs[:copies]
    up_ref, down_ref, up_grad_ref, down_grad_ref, slots, grads = refs[copies:]
    expert = pl.program_id(0)
    groups, _, own, width = received[0].shape
    count = groups * IMG_ROW
    for index in range(own // IMG_ROW):

        @pl.when(jnp.logical_and(expert == index, pl.program_id(1) == 0))
        def _():
            for copy, ref in enumerate(received):
                rows = slice(copy * count, (copy + 1) * count)
                slots[rows] = own_rows(ref[:, 0].astype(full), index)
                grads[rows] = own_rows(ref[:, 1].astype(full), index)

    pre = dot(slots[...], up_ref[0])
    cdf, pdf = gelu_parts(pre)
    down_grad_ref[0] = dot((pre * cdf).astype(low), grads[...], 0, 0)
    grad_hidden = dot(grads[...], down_ref[0], 1, 1)
    grad_pre = (grad_hidden * (cdf + pre * pdf)).astype(low)
    up_grad_ref[0] = dot(slots[...], grad_pre, 0, 0)


def weight_grads(received, up, down):
    groups, _, _, width = received[0].shape
    experts, _, hidden = up.shape
    copies = len(received)
    tile = hidden // 3
    up_spec = pl.BlockSpec((1, width, tile), lambda expert, step: (expert, 0, step))
    down_spec = pl.BlockSpec((1, tile, width), lambda expert, step: (expert, step, 0))
    rows = (copies * groups * IMG_ROW, width)

    def kernel(*refs):
        weights_kernel(copies, *refs)

    return pl.pallas_call(
        kernel,
        grid=(experts, 3),
        in_specs=[whole_vmem] * copies + [up_spec, down_spec],
        out_specs=[up_spec, down_spec],
        out_shape=[shape_of(up.shape, full), shape_of(down.shape, full)],
        scratch_shapes=[pltpu.VMEM(rows, low)] * 2,
        compiler_params=params(48),
        name="weight_grads",
    )(*received, up, down)


def add_kernel(terms_ref, sums_ref):
    sums = jnp.sum(terms_ref[...].astype(full), axis=0).astype(low)
    sums_ref[...] = jnp.broadcast_to(sums[None], sums_ref.shape)


def add_terms(terms):
    return pl.pallas_call(
        add_kernel,
        in_specs=[whole_vmem],
        out_specs=whole_vmem,
        out_shape=shape_of(terms.shape, low),
        compiler_params=params(32),
        name="add_terms",
    )(terms)


def finish_kernel(
    total, place_ref, sums_ref, weight_ref, gain_ref,
    first_ref, qkv_ref, proj_ref, second_ref, slot_ref,
):
    width = weight_ref.shape[0]
    pairs = width // LANES
    own = slot_ref.shape[1]
    rows = sums_ref.shape[0] * sums_ref.shape[1]
    sums = sums_ref[...].reshape(rows, LANES)
    base = (width + total + 16) * pairs
    for index in range(pairs):
        lanes = slice(index * LANES, (index + 1) * LANES)
        proj_ref[:, lanes] = sums[index * width : (index + 1) * width].astype(full)
        start = (width + total) * pairs + index * 16
        second_ref[:, lanes] = sums[start : start + 1].astype(full)
        start = width * pairs + index * total
        block = sums[start : start + total]
        row = lax.broadcasted_iota(jnp.int32, (total, own), 0)
        column = lax.broadcasted_iota(jnp.int32, (total, own), 1) + place_ref[0] * own
        slot_ref[lanes, :] = dot(block, (row == column).astype(full).astype(low), 0, 0)
    first = jnp.zeros((width, 1), full)
    for pair in range(pairs):
        for part in range(3):
            lanes = slice(part * width + pair * LANES, part * width + (pair + 1) * LANES)
            start = base + (pair * 3 + part) * width
            grad = sums[start : start + width].astype(full)
            qkv_ref[:, lanes] = grad
            product = grad * weight_ref[:, lanes].astype(full)
            first = first + jnp.sum(product, axis=1, keepdims=True)
    first_ref[...] = jnp.broadcast_to(first, (width, LANES)).T[0:1] / gain_ref[...]


def finish(place, sums, weight, gain, experts, own):
    width = weight.shape[0]

    def kernel(*refs):
        finish_kernel(experts, *refs)

    return pl.pallas_call(
        kernel,
        in_specs=[pl.BlockSpec(memory_space=pltpu.SMEM)] + [whole_vmem] * 3,
        out_specs=[whole_vmem] * 5,
        out_shape=[
            shape_of((1, width), full),
            shape_of(weight.shape, full),
            shape_of((width, width), full),
            shape_of((1, width), full),
            shape_of((width, own), full),
        ],
        compiler_params=params(48),
        name="finish",
    )(place, sums, weight, gain)


def per_device(
    patches,
    image_ids,
    first_gain,
    qkv_weight,
    proj_weight,
    second_gain,
    slot_params,
    up_weight,
    down_weight,
    cotangent,
):
    groups = lax.axis_size("expert")
    copies = lax.axis_size("rows")
    devices = groups * copies
    _, length, width = patches.shape
    own = slot_params.shape[1]
    experts = own * groups
    spread = jnp.broadcast_to(slot_params.T[None], (groups, own, width))
    slots = lax.all_to_all(spread, "expert", 0, 0, tiled=True).reshape(experts, width)
    patches = patches[0]
    cotangent = cotangent[0]
    first_gain = first_gain[None]
    second_gain = second_gain[None]
    probs, attn, queries, keys, values, first_in = attend(
        patches, image_ids, first_gain, qkv_weight
    )
    resid, second_in, dispatch, combine, send = route(
        patches, attn, proj_weight, second_gain, slots, image_ids, cotangent, groups
    )
    received = lax.all_to_all(send, "expert", 0, 0, tiled=True)
    back = run_experts(received, up_weight, down_weight)
    back = lax.all_to_all(back, "expert", 0, 0, tiled=True)
    others = [
        lax.ppermute(received, "rows", [(place, place ^ step) for place in range(copies)])
        for step in range(1, copies)
    ]
    output, grad_resid, grad_attn, delta, sums = slots_back(
        back, second_in, resid, dispatch, combine, image_ids, cotangent,
        slots, second_gain, attn, proj_weight,
    )
    pieces = []
    bundle = [sums]
    for pair in range(width // LANES):
        grads, sums = attend_back(
            pair, probs, queries, keys, values, grad_attn, delta, first_in
        )
        pieces.append(grads)
        bundle.append(sums)
    patch_grad = patch_back(patches, first_gain, qkv_weight, grad_resid, pieces)
    up_grad, down_grad = weight_grads([received] + others, up_weight, down_weight)
    count = sum(piece.shape[0] for piece in bundle)
    share = -(-count // (16 * devices)) * 16
    bundle.append(jnp.zeros((share * devices - count, LANES), low))
    terms = jnp.concatenate(bundle, axis=0).reshape(devices, share, LANES)
    terms = lax.all_to_all(terms, both_axes, 0, 0, tiled=True)
    sums = lax.all_to_all(add_terms(terms), both_axes, 0, 0, tiled=True)
    place = lax.axis_index("expert").astype(jnp.int32).reshape(1)
    first_grad, qkv_grad, proj_grad, second_grad, slot_grad = finish(
        place, sums, qkv_weight, first_gain, experts, own
    )
    return (
        output[None],
        patch_grad[None],
        first_grad[0],
        qkv_grad,
        proj_grad,
        second_grad[0],
        slot_grad,
        up_grad,
        down_grad,
    )


def solution(mesh):
    return jax.shard_map(
        per_device,
        mesh=mesh,
        in_specs=(
            P(("expert", "rows"), None, None),
            P(("expert", "rows"), None),
            P(),
            P(),
            P(),
            P(),
            P(None, "expert"),
            P("expert", None, None),
            P("expert", None, None),
            P(("expert", "rows"), None, None),
        ),
        out_specs=(
            P(("expert", "rows"), None, None),
            P(("expert", "rows"), None, None),
            P(),
            P(),
            P(),
            P(),
            P(None, "expert"),
            P("expert", None, None),
            P("expert", None, None),
        ),
        check_vma=False,
    )
```

```python
import jax
import jax.numpy as jnp
from jax import lax
from jax.experimental import pallas as pl
from jax.experimental.pallas import tpu as pltpu
from jax.sharding import PartitionSpec as P

HEADS = 6
IMG_ROW = 8
LANES = 128
TILE = 256

epsilon = 1e-06
masked_fill = -1e30
score_bound = 64.0
log2_e = 1.4426950408889634
low = jnp.bfloat16
full = jnp.float32
whole_vmem = pl.BlockSpec(memory_space=pltpu.VMEM)
anywhere = pl.BlockSpec(memory_space=pl.ANY)
both_axes = ("expert", "rows")


def dot(left, right, left_dim=1, right_dim=0):
    return lax.dot_general(
        left, right, (((left_dim,), (right_dim,)), ((), ())), preferred_element_type=full
    )


def shape_of(shape, dtype):
    return jax.ShapeDtypeStruct(shape, dtype)


def kept(shape, dtype):
    return pltpu.HBM(shape, dtype)


def keep(*arrays):
    return [pltpu.with_memory_space_constraint(array, pltpu.HBM) for array in arrays]


def params(mib):
    return pltpu.CompilerParams(vmem_limit_bytes=mib << 20)


def cost(microseconds):
    return pl.CostEstimate(
        flops=0, transcendentals=0, bytes_accessed=int(microseconds * 3.6e6)
    )


def norm_parts(values):
    centred = values - jnp.mean(values, axis=-1, keepdims=True)
    factor = lax.rsqrt(jnp.mean(centred * centred, axis=-1, keepdims=True) + epsilon)
    return centred * factor, factor


def norm_back(grad_norm, normed, factor, gain):
    scaled = grad_norm * gain
    return factor * (
        scaled
        - jnp.mean(scaled, axis=-1, keepdims=True)
        - normed * jnp.mean(scaled * normed, axis=-1, keepdims=True)
    )


def member_of(ids):
    images = lax.broadcasted_iota(jnp.int32, (IMG_ROW, ids.shape[1]), 0)
    return images == ids


def gelu_parts(pre):
    cdf = 0.5 * (1.0 + lax.erf(pre * 0.7071067811865476))
    pdf = 0.3989422804014327 * jnp.exp(-0.5 * pre * pre)
    return cdf, pdf


def attend_kernel(
    x_ref, ids_ref, gain_ref, weight_ref,
    probs_ref, attn_ref, inverse_ref, queries_out, keys_out, value_rows_out, first_out,
    queries_ref, keys_ref, value_rows_ref, first_ref,
    key_rows, values, mask_rows, same, bound, semaphores,
):
    pair = pl.program_id(0)
    length, width = x_ref.shape
    pairs = width // LANES
    half = LANES // 2
    saves = [
        pltpu.make_async_copy(source, target, semaphores.at[index])
        for index, (source, target) in enumerate(
            [
                (queries_ref, queries_out),
                (keys_ref, keys_out),
                (value_rows_ref, value_rows_out),
                (first_ref, first_out),
            ]
        )
    ]

    @pl.when(pair == 0)
    def _():
        normed, _ = norm_parts(x_ref[...].astype(full))
        first_in = (normed * gain_ref[...].reshape(1, width)).astype(low)
        first_ref[...] = first_in.T
        turned = dot(weight_ref[...], first_in, 0, 1)
        scaled = (turned[:width] * (half**-0.5 * log2_e)).astype(low)
        turned = turned[width:].astype(low)
        queries_ref[...] = scaled.reshape(pairs, LANES, length)
        keys_ref[...] = turned[:width].reshape(pairs, LANES, length)
        values[...] = turned[width:].reshape(pairs, LANES, length)
        norms = []
        for part in (scaled, turned[:width]):
            square = part.astype(full).reshape(2 * pairs, half, length)
            norms.append(jnp.max(jnp.sum(square * square, axis=1), axis=1, keepdims=True))
        bound[0] = jnp.max(norms[0] * norms[1])
        rows = dot(first_in, weight_ref[:, width:]).astype(low)
        for index in range(pairs):
            key_rows[index] = rows[:, index * LANES : (index + 1) * LANES]
            value_rows_ref[index] = rows[:, width + index * LANES : width + (index + 1) * LANES]
        images = lax.broadcasted_iota(jnp.int32, (LANES, length), 0)
        matching = images == ids_ref[...]
        same[...] = matching.astype(full).astype(low)
        other = jnp.where(jnp.logical_or(matching, images >= IMG_ROW), 0.0, masked_fill)
        mask_rows[...] = other.T.astype(low)
        for save in saves:
            save.start()

    def attend_pair(raise_scores):
        keys = jnp.concatenate([key_rows[pair], mask_rows[...]], axis=1)
        none = jnp.zeros((half, TILE), low)
        ones = jnp.ones((16, length), low)
        for head in range(2):
            rows = slice(head * half, (head + 1) * half)
            value = jnp.concatenate([values[pair, rows, :], ones], axis=0)
            for start in range(0, length, TILE):
                span = slice(start, start + TILE)
                query = queries_ref[pair, rows, span]
                parts = [query, none] if head == 0 else [none, query]
                scores = dot(keys, jnp.concatenate(parts + [same[:, span]], axis=0))
                probs = raise_scores(scores).astype(low)
                probs_ref[head, :, span] = probs
                mixed = dot(value, probs)
                inverse = 1.0 / mixed[half : half + 1]
                inverse_ref[0, head : head + 1, span] = inverse
                attn_ref[0, rows, span] = (mixed[:half] * inverse).astype(low)

    small = bound[0] < score_bound * score_bound

    @pl.when(small)
    def _():
        attend_pair(jnp.exp2)

    @pl.when(jnp.logical_not(small))
    def _():
        attend_pair(lambda scores: jnp.exp2(scores - jnp.max(scores, axis=0, keepdims=True)))

    @pl.when(pair == pairs - 1)
    def _():
        for save in saves:
            save.wait()


def attend(patches, ids, gain, weight):
    length, width = patches.shape
    pairs = width // LANES
    stack = (pairs, LANES, length)
    rows = (pairs, length, LANES)
    return pl.pallas_call(
        attend_kernel,
        grid=(pairs,),
        in_specs=[whole_vmem] * 4,
        out_specs=[
            pl.BlockSpec((2, length, length), lambda pair: (pair, 0, 0)),
            pl.BlockSpec((1, LANES, length), lambda pair: (pair, 0, 0)),
            pl.BlockSpec((1, 2, length), lambda pair: (pair, 0, 0)),
            anywhere,
            anywhere,
            anywhere,
            anywhere,
        ],
        out_shape=[
            kept((2 * pairs, length, length), low),
            kept(stack, low),
            kept((pairs, 2, length), full),
            kept(stack, low),
            kept(stack, low),
            kept(rows, low),
            kept((width, length), low),
        ],
        scratch_shapes=[
            pltpu.VMEM(stack, low),
            pltpu.VMEM(stack, low),
            pltpu.VMEM(rows, low),
            pltpu.VMEM((width, length), low),
            pltpu.VMEM(rows, low),
            pltpu.VMEM(stack, low),
            pltpu.VMEM((length, LANES), low),
            pltpu.VMEM((LANES, length), low),
            pltpu.SMEM((1,), full),
            pltpu.SemaphoreType.DMA((4,)),
        ],
        compiler_params=params(24),
        cost_estimate=cost(25),
        name="attend",
    )(*keep(patches, ids, gain, weight))


def slot_rows(slots):
    experts = slots.shape[0]
    row = lax.broadcasted_iota(jnp.int32, (experts * IMG_ROW, experts), 0) // IMG_ROW
    column = lax.broadcasted_iota(jnp.int32, (experts * IMG_ROW, experts), 1)
    return dot((row == column).astype(full).astype(low), slots).astype(low)


def route_kernel(
    x_ref, attn_ref, proj_ref, gain_ref, slots_ref, ids_ref, cotangent_ref,
    resid_out, second_out, dispatch_out, combine_out, send_ref,
    resid_ref, second_ref, dispatch_ref, combine_ref, semaphores,
):
    length, width = x_ref.shape
    saves = [
        pltpu.make_async_copy(source, target, semaphores.at[index])
        for index, (source, target) in enumerate(
            [
                (resid_ref, resid_out),
                (second_ref, second_out),
                (combine_ref, combine_out),
                (dispatch_ref, dispatch_out),
            ]
        )
    ]
    experts = slots_ref.shape[0]
    shape = (experts, IMG_ROW, length)
    resid = x_ref[...].astype(full) + dot(attn_ref[...].reshape(width, length), proj_ref[...], 0, 0)
    resid_ref[...] = resid
    saves[0].start()
    normed, _ = norm_parts(resid)
    second_in = (normed * gain_ref[...].reshape(1, width)).astype(low)
    second_ref[...] = second_in
    saves[1].start()
    logits = dot(slot_rows(slots_ref[...]), second_in, 1, 1).reshape(shape)
    member = member_of(ids_ref[...])
    raised = jnp.exp(logits - jnp.max(logits, axis=0, keepdims=True))
    combine = raised * (1.0 / jnp.sum(raised, axis=0, keepdims=True))
    combine_ref[...] = combine
    saves[2].start()
    combine_low = jnp.where(member[None], combine, 0.0).astype(low).reshape(-1, length)
    masked = jnp.where(member[None], logits, masked_fill)
    top = jnp.max(masked, axis=2, keepdims=True)
    raised = jnp.where(member[None], jnp.exp(masked - top), 0.0)
    present = jnp.max(member.astype(full), axis=1, keepdims=True)
    total = jnp.sum(raised, axis=2, keepdims=True) + (1.0 - present)[None]
    dispatch = raised * (1.0 / total)
    dispatch_ref[...] = dispatch
    saves[3].start()
    dispatch_low = dispatch.astype(low).reshape(-1, length)
    block = (send_ref.shape[0], send_ref.shape[2], width)
    send_ref[:, 0] = dot(dispatch_low, second_in).astype(low).reshape(block)
    send_ref[:, 1] = dot(combine_low, cotangent_ref[...]).astype(low).reshape(block)
    for save in saves:
        save.wait()


def route(patches, attn, proj, gain, slots, ids, cotangent, groups):
    length, width = patches.shape
    experts = slots.shape[0]
    own = experts // groups * IMG_ROW
    return pl.pallas_call(
        route_kernel,
        in_specs=[whole_vmem] * 7,
        out_specs=[anywhere] * 4 + [whole_vmem],
        out_shape=[
            kept((length, width), full),
            kept((length, width), low),
            kept((experts, IMG_ROW, length), full),
            kept((experts, IMG_ROW, length), full),
            shape_of((groups, 2, own, width), low),
        ],
        scratch_shapes=[
            pltpu.VMEM((length, width), full),
            pltpu.VMEM((length, width), low),
            pltpu.VMEM((experts, IMG_ROW, length), full),
            pltpu.VMEM((experts, IMG_ROW, length), full),
            pltpu.SemaphoreType.DMA((4,)),
        ],
        compiler_params=params(16 + experts // 4),
        cost_estimate=cost(3),
        name="route",
    )(*keep(patches, attn, proj, gain), slots, *keep(ids, cotangent))


def own_rows(received, expert):
    groups, _, width = received.shape
    rows = received[:, expert * IMG_ROW : (expert + 1) * IMG_ROW]
    return rows.reshape(groups * IMG_ROW, width).astype(low)


def expert_kernel(received_ref, up_ref, down_ref, back_ref, stage):
    expert = pl.program_id(0)
    groups, _, own, width = received_ref.shape
    slots = received_ref[:, 0].astype(full)
    grads = received_ref[:, 1].astype(full)
    for index in range(own // IMG_ROW):

        @pl.when(expert == index)
        def _():
            up = up_ref[0]
            down = down_ref[0]
            pre = dot(own_rows(slots, index), up)
            cdf, pdf = gelu_parts(pre)
            out = dot((pre * cdf).astype(low), down)
            grad_hidden = dot(own_rows(grads, index), down, 1, 1)
            grad_pre = (grad_hidden * (cdf + pre * pdf)).astype(low)
            grad_slots = dot(grad_pre, up, 1, 1)
            rows = slice(index * IMG_ROW, (index + 1) * IMG_ROW)
            stage[0, :, rows] = out.reshape(groups, IMG_ROW, width)
            stage[1, :, rows] = grad_slots.reshape(groups, IMG_ROW, width)

    @pl.when(expert == own // IMG_ROW - 1)
    def _():
        back_ref[:, 0] = stage[0].astype(low)
        back_ref[:, 1] = stage[1].astype(low)


def run_experts(received, up, down):
    groups, _, own, width = received.shape
    experts, _, hidden = up.shape
    return pl.pallas_call(
        expert_kernel,
        grid=(experts,),
        in_specs=[
            whole_vmem,
            pl.BlockSpec((1, width, hidden), lambda expert: (expert, 0, 0)),
            pl.BlockSpec((1, hidden, width), lambda expert: (expert, 0, 0)),
        ],
        out_specs=pl.BlockSpec(received.shape, lambda expert: (0, 0, 0, 0)),
        out_shape=shape_of(received.shape, low),
        scratch_shapes=[pltpu.VMEM((2, groups, own, width), full)],
        compiler_params=params(40),
        cost_estimate=cost(3),
        name="run_experts",
    )(received, *keep(up, down))


def backward_kernel(
    back_ref, slots_ref, gain_ref, ids_ref, inverse_ref, *refs
):
    sources = refs[:12]
    output_ref, grad_resid_ref, grads_ref, sums_ref = refs[-20:-16]
    targets = refs[-16:-4]
    grad_attn, delta, grad_scores, semaphores = refs[-4:]
    loads = [
        pltpu.make_async_copy(source, target, semaphores.at[index])
        for index, (source, target) in enumerate(zip(sources, targets, strict=True))
    ]
    for load in loads:
        load.start()
    cotangent_ref, combine_ref, second_ref, dispatch_ref, resid_ref, attn_ref, proj_ref = targets[:7]
    values_ref, probs_ref, keys_ref, queries_ref, first_ref = targets[7:]
    for load in loads[:4]:
        load.wait()
    length, width = resid_ref.shape
    pairs = width // LANES
    half = LANES // 2
    experts = slots_ref.shape[0]
    count = experts * IMG_ROW
    shape = (experts, IMG_ROW, length)
    slot_out = back_ref[:, 0].reshape(count, width)
    grad_slots = back_ref[:, 1].reshape(count, width)
    cotangent = cotangent_ref[...]
    second_in = second_ref[...]
    combine = combine_ref[...]
    dispatch = dispatch_ref[...]
    member = member_of(ids_ref[...])
    grad_combine = dot(slot_out, cotangent, 1, 1).reshape(shape)
    grad_own = jnp.sum(jnp.where(member[None], grad_combine, 0.0), axis=1, keepdims=True)
    inner = jnp.sum(combine * grad_own, axis=0, keepdims=True)
    grad_logits = combine * (grad_own - inner)
    grad_dispatch = dot(grad_slots, second_in, 1, 1).reshape(shape)
    weighted = jnp.sum(dispatch * grad_dispatch, axis=2, keepdims=True)
    routed = jnp.sum(dispatch * (grad_dispatch - weighted), axis=1, keepdims=True)
    grad_low = (grad_logits + routed).astype(low).reshape(count, length)
    row = lax.broadcasted_iota(jnp.int32, (experts, count), 0) * IMG_ROW
    column = lax.broadcasted_iota(jnp.int32, (experts, count), 1)
    grad_low = dot((row == column).astype(full).astype(low), grad_low).astype(low)
    slot_grad = dot(grad_low, second_in)
    mixing = jnp.concatenate([dispatch.astype(low).reshape(count, length), grad_low], axis=0)
    mixed = jnp.concatenate([grad_slots, slots_ref[...]], axis=0)
    grad_second = dot(mixing, mixed, 0, 0)
    for load in loads[4:7]:
        load.wait()
    resid = resid_ref[...]
    combine_low = jnp.where(member[None], combine, 0.0).astype(low).reshape(count, length)
    output_ref[...] = (resid + dot(combine_low, slot_out, 0, 0)).astype(low)
    normed, factor = norm_parts(resid)
    second_grad = jnp.sum(grad_second * normed, axis=0, keepdims=True)
    gain = gain_ref[...].reshape(1, width)
    grad_resid = cotangent.astype(full) + norm_back(grad_second, normed, factor, gain)
    grad_resid_ref[...] = grad_resid
    grad_branch = grad_resid.astype(low)
    attn = attn_ref[...]
    proj_grad = dot(attn.reshape(width, length), grad_branch).astype(low)
    scaled = dot(proj_ref[...], grad_branch, 1, 1).reshape(pairs, 2, half, length)
    scaled = (scaled * inverse_ref[...][:, :, None, :]).astype(low)
    product = scaled.astype(full) * attn.reshape(scaled.shape).astype(full)
    delta[...] = jnp.sum(product, axis=2)
    grad_attn[...] = scaled.reshape(grad_attn.shape)
    slot_low = slot_grad.astype(low)
    second_low = jnp.broadcast_to(second_grad, (16, width)).astype(low)
    early = pairs * (width + experts + 16)
    for index in range(pairs):
        lanes = slice(index * LANES, (index + 1) * LANES)
        sums_ref[index * width : (index + 1) * width] = proj_grad[:, lanes]
        base = width * pairs + index * experts
        sums_ref[base : base + experts] = slot_low[:, lanes]
        base = (width + experts) * pairs + index * 16
        sums_ref[base : base + 16] = second_low[:, lanes]
    used = early + pairs * 3 * width
    if used < sums_ref.shape[0]:
        sums_ref[used:] = jnp.zeros((sums_ref.shape[0] - used, LANES), low)

    for load in loads[7:]:
        load.wait()
    factor = half**-0.5
    none = jnp.zeros((half, TILE), low)

    def one_pair(pair, carry):
        for head in range(2):
            rows = slice(head * half, (head + 1) * half)
            for start in range(0, length, TILE):
                span = slice(start, start + TILE)
                grad = grad_attn[pair, rows, span]
                parts = [grad, none] if head == 0 else [none, grad]
                grad_probs = dot(values_ref[pair], jnp.concatenate(parts, axis=0))
                probs = probs_ref[2 * pair + head, :, span].astype(full)
                grad_probs = grad_probs - delta[pair, head : head + 1, span]
                grad_scores[head, :, span] = (probs * grad_probs).astype(low)
            scores = grad_scores[head]
            probs = probs_ref[2 * pair + head]
            grads_ref[pair, 2, rows, :] = dot(grad_attn[pair, rows, :], probs, 1, 1).astype(low)
            grads_ref[pair, 0, rows, :] = (dot(keys_ref[pair, rows, :], scores) * factor).astype(low)
            grads_ref[pair, 1, rows, :] = (
                dot(queries_ref[pair, rows, :], scores, 1, 1) * (1.0 / log2_e)
            ).astype(low)
        sums = dot(first_ref[...], grads_ref[pair].reshape(3 * LANES, length), 1, 1).astype(low)

        for index in range(3):
            base = pl.multiple_of(early + (pair * 3 + index) * width, 16)
            sums_ref[pl.ds(base, width)] = sums[:, index * LANES : (index + 1) * LANES]
        return carry

    lax.fori_loop(0, pairs, one_pair, 0)


def padded(rows, devices):
    return -(-rows // (16 * devices)) * 16 * devices


def backward(back, slots, gain, ids, inverse, arrays, devices):
    length, width = arrays[0].shape
    experts = slots.shape[0]
    pairs = width // LANES
    rows = padded(pairs * (4 * width + experts + 16), devices)
    return pl.pallas_call(
        backward_kernel,
        in_specs=[whole_vmem] * 5 + [anywhere] * len(arrays),
        out_specs=[whole_vmem] * 4,
        out_shape=[
            kept((length, width), low),
            kept((length, width), full),
            kept((pairs, 3, LANES, length), low),
            shape_of((rows, LANES), low),
        ],
        scratch_shapes=[pltpu.VMEM(array.shape, array.dtype) for array in arrays]
        + [
            pltpu.VMEM((pairs, LANES, length), low),
            pltpu.VMEM((pairs, 2, length), full),
            pltpu.VMEM((2, length, length), low),
            pltpu.SemaphoreType.DMA((len(arrays),)),
        ],
        compiler_params=params(44 + experts // 8),
        cost_estimate=cost(20),
        name="backward",
    )(back, *keep(slots, gain, ids, inverse, *arrays))


def patch_back_kernel(x_ref, gain_ref, weight_ref, resid_ref, grads_ref, *refs):
    result_ref = refs[-1]
    length, width = x_ref.shape
    pairs = width // LANES
    grads = [grads_ref[pair, part] for part in range(3) for pair in range(pairs)]
    grad_first = dot(weight_ref[...], jnp.concatenate(grads, axis=0)).T
    normed, factor = norm_parts(x_ref[...].astype(full))
    gain = gain_ref[...].reshape(1, width)
    result_ref[...] = resid_ref[...] + norm_back(grad_first, normed, factor, gain)


def patch_back(patches, gain, weight, grad_resid, grads, after):
    return pl.pallas_call(
        patch_back_kernel,
        in_specs=[whole_vmem] * 5 + [anywhere] * len(after),
        out_specs=whole_vmem,
        out_shape=kept(patches.shape, full),
        compiler_params=params(20),
        cost_estimate=cost(3),
        name="patch_back",
    )(*keep(patches, gain, weight, grad_resid, grads, *after))


def weights_kernel(copies, *refs):
    received = refs[:copies]
    up_ref, down_ref, _, up_grad_ref, down_grad_ref, slots, grads = refs[copies:]
    expert = pl.program_id(0)
    groups, _, own, width = received[0].shape
    count = groups * IMG_ROW
    for index in range(own // IMG_ROW):

        @pl.when(jnp.logical_and(expert == index, pl.program_id(1) == 0))
        def _():
            for copy, ref in enumerate(received):
                rows = slice(copy * count, (copy + 1) * count)
                slots[rows] = own_rows(ref[:, 0].astype(full), index)
                grads[rows] = own_rows(ref[:, 1].astype(full), index)

    pre = dot(slots[...], up_ref[0])
    cdf, pdf = gelu_parts(pre)
    down_grad_ref[0] = dot((pre * cdf).astype(low), grads[...], 0, 0)
    grad_hidden = dot(grads[...], down_ref[0], 1, 1)
    grad_pre = (grad_hidden * (cdf + pre * pdf)).astype(low)
    up_grad_ref[0] = dot(slots[...], grad_pre, 0, 0)


def weight_grads(received, up, down, after):
    groups, _, _, width = received[0].shape
    experts, _, hidden = up.shape
    copies = len(received)
    tile = hidden // 3
    up_spec = pl.BlockSpec((1, width, tile), lambda expert, step: (expert, 0, step))
    down_spec = pl.BlockSpec((1, tile, width), lambda expert, step: (expert, step, 0))
    rows = (copies * groups * IMG_ROW, width)

    def kernel(*refs):
        weights_kernel(copies, *refs)

    return pl.pallas_call(
        kernel,
        grid=(experts, 3),
        in_specs=[whole_vmem] * copies + [up_spec, down_spec, pl.BlockSpec(memory_space=pl.ANY)],
        out_specs=[up_spec, down_spec],
        out_shape=[kept(up.shape, full), kept(down.shape, full)],
        scratch_shapes=[pltpu.VMEM(rows, low)] * 2,
        compiler_params=params(40),
        cost_estimate=cost(9),
        name="weight_grads",
    )(*keep(*received, up, down, after))


def half_kernel(place_ref, mine_ref, other_ref, sums_ref):
    count, share, lanes = sums_ref.shape
    rows = pl.ds(pl.multiple_of(place_ref[0] * count * share, 16), count * share)
    sums = mine_ref[rows].astype(full) + other_ref[rows].astype(full)
    sums_ref[...] = sums.astype(low).reshape(sums_ref.shape)


def add_half(place, mine, other, count):
    rows, lanes = mine.shape
    return pl.pallas_call(
        half_kernel,
        in_specs=[pl.BlockSpec(memory_space=pltpu.SMEM), whole_vmem, whole_vmem],
        out_specs=whole_vmem,
        out_shape=shape_of((count, rows // (2 * count), lanes), low),
        compiler_params=params(12),
        cost_estimate=cost(1),
        name="add_half",
    )(place, mine, other)


def add_kernel(terms_ref, *refs):
    sums_ref = refs[-1]
    sums = jnp.sum(terms_ref[...].astype(full), axis=0).astype(low)
    sums_ref[...] = jnp.broadcast_to(sums[None], sums_ref.shape)


def add_terms(terms, after):
    return pl.pallas_call(
        add_kernel,
        in_specs=[whole_vmem] + [anywhere] * len(after),
        out_specs=whole_vmem,
        out_shape=shape_of(terms.shape, low),
        compiler_params=params(12),
        cost_estimate=cost(1),
        name="add_terms",
    )(terms, *keep(*after))


def finish_kernel(
    total, place_ref, mine_ref, other_ref, weight_ref, gain_ref,
    first_ref, qkv_ref, proj_ref, second_ref, slot_ref,
):
    width = weight_ref.shape[0]
    pairs = width // LANES
    own = slot_ref.shape[0]
    ahead = place_ref[1] == 0

    mine = mine_ref[...].reshape(-1, LANES)
    other = other_ref[...].reshape(-1, LANES)
    sums = jnp.concatenate(
        [jnp.where(ahead, mine, other), jnp.where(ahead, other, mine)], axis=0
    )
    base = (width + total + 16) * pairs
    seconds = []
    for index in range(pairs):
        lanes = slice(index * LANES, (index + 1) * LANES)
        proj_ref[:, lanes] = sums[index * width : (index + 1) * width].astype(full)
        start = (width + total) * pairs + index * 16
        seconds.append(sums[start : start + 16].astype(full)[0:1])
        start = width * pairs + index * total
        row = lax.broadcasted_iota(jnp.int32, (own, total), 0) + place_ref[0] * own
        column = lax.broadcasted_iota(jnp.int32, (own, total), 1)
        chosen = (row == column).astype(full).astype(low)
        slot_ref[:, lanes] = dot(chosen, sums[start : start + total])
    second_ref[...] = jnp.concatenate(seconds, axis=1).reshape(width)
    first = jnp.zeros((width, 1), full)
    for pair in range(pairs):
        for part in range(3):
            lanes = slice(part * width + pair * LANES, part * width + (pair + 1) * LANES)
            start = base + (pair * 3 + part) * width
            grad = sums[start : start + width].astype(full)
            qkv_ref[:, lanes] = grad
            product = grad * weight_ref[:, lanes].astype(full)
            first = first + jnp.sum(product, axis=1, keepdims=True)
    row = jnp.broadcast_to(first, (width, LANES)).T[0:1]
    first_ref[...] = (row / gain_ref[...].reshape(1, width)).reshape(width)


def finish(place, mine, other, weight, gain, experts, own):
    width = weight.shape[0]

    def kernel(*refs):
        finish_kernel(experts, *refs)

    return pl.pallas_call(
        kernel,
        in_specs=[pl.BlockSpec(memory_space=pltpu.SMEM)] + [whole_vmem] * 4,
        out_specs=[whole_vmem] * 5,
        out_shape=[
            shape_of((width,), full),
            shape_of(weight.shape, full),
            shape_of((width, width), full),
            shape_of((width,), full),
            shape_of((own, width), full),
        ],
        compiler_params=params(20),
        cost_estimate=cost(3),
        name="finish",
    )(place, mine, other, *keep(weight, gain))


def per_device(
    patches,
    image_ids,
    first_gain,
    qkv_weight,
    proj_weight,
    second_gain,
    slot_params,
    up_weight,
    down_weight,
    cotangent,
):
    groups = lax.axis_size("expert")
    copies = lax.axis_size("rows")
    devices = groups * copies
    _, length, width = patches.shape
    own = slot_params.shape[1]
    experts = own * groups
    spread = jnp.broadcast_to(slot_params.T[None], (groups, own, width))
    slots = lax.all_to_all(spread, "expert", 0, 0, tiled=True).reshape(experts, width)
    patches = patches[0]
    cotangent = cotangent[0]
    probs, attn, inverse, queries, keys, values, first_in = attend(
        patches, image_ids, first_gain, qkv_weight
    )
    resid, second_in, dispatch, combine, send = route(
        patches, attn, proj_weight, second_gain, slots, image_ids, cotangent, groups
    )
    received = lax.all_to_all(send, "expert", 0, 0, tiled=True)
    back = run_experts(received, up_weight, down_weight)
    back = lax.all_to_all(back, "expert", 0, 0, tiled=True)
    others = [
        lax.ppermute(received, "rows", [(index, index ^ step) for index in range(copies)])
        for step in range(1, copies)
    ]
    saved = [cotangent, combine, second_in, dispatch, resid, attn, proj_weight]
    saved += [values, probs, keys, queries, first_in]
    output, grad_resid, grads, terms = backward(
        back, slots, second_gain, image_ids, inverse, saved, devices
    )
    core = lax.axis_index("rows") % 2
    place = jnp.stack([lax.axis_index("expert"), core]).astype(jnp.int32)
    swap = [(index, index ^ 1) for index in range(copies)]
    halves = [list(range(index, devices, 2)) for index in range(2)]

    def exchange(array):
        return lax.all_to_all(array, both_axes, 0, 0, tiled=True, axis_index_groups=halves)

    half = add_half(place[1:], terms, lax.ppermute(terms, "rows", swap), devices // 2)
    patch_grad = patch_back(patches, first_gain, qkv_weight, grad_resid, grads, [half] + others)
    sums = add_terms(exchange(half), [patch_grad])
    up_grad, down_grad = weight_grads([received] + others, up_weight, down_weight, sums)
    sums, up_grad, down_grad = lax.optimization_barrier((exchange(sums), up_grad, down_grad))
    first_grad, qkv_grad, proj_grad, second_grad, slot_grad = finish(
        place, sums, lax.ppermute(sums, "rows", swap), qkv_weight, first_gain, experts, own
    )
    return (
        output[None],
        patch_grad[None],
        first_grad,
        qkv_grad,
        proj_grad,
        second_grad,
        slot_grad.T,
        up_grad,
        down_grad,
    )


def solution(mesh):
    return jax.shard_map(
        per_device,
        mesh=mesh,
        in_specs=(
            P(("expert", "rows"), None, None),
            P(("expert", "rows"), None),
            P(),
            P(),
            P(),
            P(),
            P(None, "expert"),
            P("expert", None, None),
            P("expert", None, None),
            P(("expert", "rows"), None, None),
        ),
        out_specs=(
            P(("expert", "rows"), None, None),
            P(("expert", "rows"), None, None),
            P(),
            P(),
            P(),
            P(),
            P(None, "expert"),
            P("expert", None, None),
            P("expert", None, None),
        ),
        check_vma=False,
    )
```

```python
import jax
import jax.numpy as jnp
from jax import lax
from jax.experimental import pallas as pl
from jax.experimental.pallas import tpu as pltpu
from jax.sharding import PartitionSpec as P

HEADS = 6
IMG_ROW = 8
LANES = 128
TILE = 256

epsilon = 1e-06
masked_fill = -1e30
score_bound = 64.0
log2_e = 1.4426950408889634
low = jnp.bfloat16
full = jnp.float32
whole_vmem = pl.BlockSpec(memory_space=pltpu.VMEM)
anywhere = pl.BlockSpec(memory_space=pl.ANY)
both_axes = ("expert", "rows")


def dot(left, right, left_dim=1, right_dim=0):
    return lax.dot_general(
        left, right, (((left_dim,), (right_dim,)), ((), ())), preferred_element_type=full
    )


def shape_of(shape, dtype):
    return jax.ShapeDtypeStruct(shape, dtype)


def kept(shape, dtype):
    return pltpu.HBM(shape, dtype)


def keep(*arrays):
    return [pltpu.with_memory_space_constraint(array, pltpu.HBM) for array in arrays]


def params(mib):
    return pltpu.CompilerParams(vmem_limit_bytes=mib << 20)


def cost(microseconds):
    return pl.CostEstimate(
        flops=0, transcendentals=0, bytes_accessed=int(microseconds * 3.6e6)
    )


def norm_parts(values):
    centred = values - jnp.mean(values, axis=-1, keepdims=True)
    factor = lax.rsqrt(jnp.mean(centred * centred, axis=-1, keepdims=True) + epsilon)
    return centred * factor, factor


def norm_back(grad_norm, normed, factor, gain):
    scaled = grad_norm * gain
    return factor * (
        scaled
        - jnp.mean(scaled, axis=-1, keepdims=True)
        - normed * jnp.mean(scaled * normed, axis=-1, keepdims=True)
    )


def member_of(ids):
    images = lax.broadcasted_iota(jnp.int32, (IMG_ROW, ids.shape[1]), 0)
    return images == ids


def gelu_parts(pre):
    cdf = 0.5 * (1.0 + lax.erf(pre * 0.7071067811865476))
    pdf = 0.3989422804014327 * jnp.exp(-0.5 * pre * pre)
    return cdf, pdf


def copies_of(sources, targets, semaphores):
    return [
        pltpu.make_async_copy(source, target, semaphores.at[index])
        for index, (source, target) in enumerate(zip(sources, targets, strict=True))
    ]


def attend_kernel(x_ref, ids_ref, gain_ref, weight_ref, proj_ref, second_gain_ref, *refs):
    outs, refs = refs[:9], refs[9:]
    probs_out, saved, refs = outs[0], refs[:8], refs[8:]
    queries_ref, keys_ref, value_rows_ref, first_ref = saved[:4]
    attn_ref, inverse_ref, resid_ref, second_ref = saved[4:]
    probs_ref, key_rows, values, mask_rows, same, bound, semaphores, probs_semaphores = refs
    pair = pl.program_id(0)
    length, width = x_ref.shape
    pairs = width // LANES
    half = LANES // 2
    saves = copies_of(saved, outs[1:], semaphores)

    def save_probs(head):
        return pltpu.make_async_copy(
            probs_ref.at[head], probs_out.at[head], probs_semaphores.at[head]
        )

    @pl.when(pair == 0)
    def _():
        normed, _ = norm_parts(x_ref[...].astype(full))
        first_in = (normed * gain_ref[...].reshape(1, width)).astype(low)
        turned = dot(weight_ref[...], first_in, 0, 1)
        scaled = (turned[:width] * (half**-0.5 * log2_e)).astype(low)
        turned = turned[width:].astype(low)
        queries_ref[...] = scaled.reshape(pairs, LANES, length)
        keys_ref[...] = turned[:width].reshape(pairs, LANES, length)
        values[...] = turned[width:].reshape(pairs, LANES, length)
        norms = []
        for part in (scaled, turned[:width]):
            square = part.astype(full).reshape(2 * pairs, half, length)
            norms.append(jnp.max(jnp.sum(square * square, axis=1), axis=1, keepdims=True))
        bound[0] = jnp.max(norms[0] * norms[1])
        rows = dot(first_in, weight_ref[:, width:]).astype(low)
        for index in range(pairs):
            key_rows[index] = rows[:, index * LANES : (index + 1) * LANES]
            value_rows_ref[index] = rows[:, width + index * LANES : width + (index + 1) * LANES]
        first_ref[...] = first_in.T
        for save in saves[:4]:
            save.start()
        images = lax.broadcasted_iota(jnp.int32, (LANES, length), 0)
        matching = images == ids_ref[...]
        same[...] = matching.astype(full).astype(low)
        other = jnp.where(jnp.logical_or(matching, images >= IMG_ROW), 0.0, masked_fill)
        mask_rows[...] = other.T.astype(low)

    def attend_pair(raise_scores):
        keys = jnp.concatenate([key_rows[pair], mask_rows[...]], axis=1)
        none = jnp.zeros((half, TILE), low)
        ones = jnp.ones((16, length), low)
        for head in range(2):
            rows = slice(head * half, (head + 1) * half)
            for start in range(0, length, TILE):
                span = slice(start, start + TILE)
                query = queries_ref[pair, rows, span]
                parts = [query, none] if head == 0 else [none, query]
                scores = dot(keys, jnp.concatenate(parts + [same[:, span]], axis=0))
                probs_ref[2 * pair + head, :, span] = raise_scores(scores).astype(low)
            save_probs(2 * pair + head).start()
        for head in range(2):
            rows = slice(head * half, (head + 1) * half)
            value = jnp.concatenate([values[pair, rows, :], ones], axis=0)
            mixed = dot(value, probs_ref[2 * pair + head])
            inverse = 1.0 / mixed[half : half + 1]
            inverse_ref[pair, head : head + 1] = inverse
            attn_ref[pair, rows] = (mixed[:half] * inverse).astype(low)

    small = bound[0] < score_bound * score_bound

    @pl.when(small)
    def _():
        attend_pair(jnp.exp2)

    @pl.when(jnp.logical_not(small))
    def _():
        attend_pair(lambda scores: jnp.exp2(scores - jnp.max(scores, axis=0, keepdims=True)))

    @pl.when(pair == pairs - 1)
    def _():
        for save in saves[4:6]:
            save.start()
        attn = attn_ref[...].reshape(width, length)
        resid = x_ref[...].astype(full) + dot(attn, proj_ref[...], 0, 0)
        resid_ref[...] = resid
        saves[6].start()
        normed, _ = norm_parts(resid)
        second_ref[...] = (normed * second_gain_ref[...].reshape(1, width)).astype(low)
        saves[7].start()
        for save in saves:
            save.wait()
        for head in range(2 * pairs):
            save_probs(head).wait()


def attend(patches, ids, gain, weight, proj, second_gain):
    length, width = patches.shape
    pairs = width // LANES
    stack = (pairs, LANES, length)
    rows = (pairs, length, LANES)
    probs = (2 * pairs, length, length)
    saved = [
        (stack, low),
        (stack, low),
        (rows, low),
        ((width, length), low),
        (stack, low),
        ((pairs, 2, length), full),
        ((length, width), full),
        ((length, width), low),
    ]
    return pl.pallas_call(
        attend_kernel,
        grid=(pairs,),
        in_specs=[whole_vmem] * 6,
        out_specs=[anywhere] * 9,
        out_shape=[kept(probs, low)] + [kept(*entry) for entry in saved],
        scratch_shapes=[pltpu.VMEM(*entry) for entry in saved]
        + [
            pltpu.VMEM(probs, low),
            pltpu.VMEM(rows, low),
            pltpu.VMEM(stack, low),
            pltpu.VMEM((length, LANES), low),
            pltpu.VMEM((LANES, length), low),
            pltpu.SMEM((1,), full),
            pltpu.SemaphoreType.DMA((8,)),
            pltpu.SemaphoreType.DMA((2 * pairs,)),
        ],
        compiler_params=params(44),
        cost_estimate=cost(17),
        name="attend",
    )(*keep(patches, ids, gain, weight, proj, second_gain))


def slot_rows(slots):
    experts = slots.shape[0]
    row = lax.broadcasted_iota(jnp.int32, (experts * IMG_ROW, experts), 0) // IMG_ROW
    column = lax.broadcasted_iota(jnp.int32, (experts * IMG_ROW, experts), 1)
    return dot((row == column).astype(full).astype(low), slots).astype(low)


def route_kernel(
    second_ref, slots_ref, ids_ref, cotangent_ref,
    dispatch_out, combine_out, send_ref,
    dispatch_ref, combine_ref, semaphores,
):
    length, width = second_ref.shape
    experts = slots_ref.shape[0]
    shape = (experts, IMG_ROW, length)
    saves = copies_of([dispatch_ref, combine_ref], [dispatch_out, combine_out], semaphores)
    second_in = second_ref[...]
    logits = dot(slot_rows(slots_ref[...]), second_in, 1, 1).reshape(shape)
    member = member_of(ids_ref[...])
    masked = jnp.where(member[None], logits, masked_fill)
    top = jnp.max(masked, axis=2, keepdims=True)
    raised = jnp.where(member[None], jnp.exp(masked - top), 0.0)
    present = jnp.max(member.astype(full), axis=1, keepdims=True)
    total = jnp.sum(raised, axis=2, keepdims=True) + (1.0 - present)[None]
    dispatch = raised * (1.0 / total)
    dispatch_ref[...] = dispatch
    saves[0].start()
    raised = jnp.exp(logits - jnp.max(logits, axis=0, keepdims=True))
    combine = raised * (1.0 / jnp.sum(raised, axis=0, keepdims=True))
    combine_ref[...] = combine
    saves[1].start()
    dispatch_low = dispatch.astype(low).reshape(-1, length)
    combine_low = jnp.where(member[None], combine, 0.0).astype(low).reshape(-1, length)
    block = (send_ref.shape[0], send_ref.shape[2], width)
    send_ref[:, 0] = dot(dispatch_low, second_in).astype(low).reshape(block)
    send_ref[:, 1] = dot(combine_low, cotangent_ref[...]).astype(low).reshape(block)
    for save in saves:
        save.wait()


def route(second_in, slots, ids, cotangent, groups):
    length, width = second_in.shape
    experts = slots.shape[0]
    own = experts // groups * IMG_ROW
    shape = (experts, IMG_ROW, length)
    return pl.pallas_call(
        route_kernel,
        in_specs=[whole_vmem] * 4,
        out_specs=[anywhere] * 2 + [whole_vmem],
        out_shape=[kept(shape, full)] * 2 + [shape_of((groups, 2, own, width), low)],
        scratch_shapes=[pltpu.VMEM(shape, full)] * 2 + [pltpu.SemaphoreType.DMA((2,))],
        compiler_params=params(14 + experts // 4),
        cost_estimate=cost(3),
        name="route",
    )(*keep(second_in), slots, *keep(ids, cotangent))


def own_rows(received, expert):
    groups, _, width = received.shape
    rows = received[:, expert * IMG_ROW : (expert + 1) * IMG_ROW]
    return rows.reshape(groups * IMG_ROW, width).astype(low)


def expert_kernel(received_ref, up_ref, down_source, back_ref, down_ref, stage, semaphores):
    groups, _, own, width = received_ref.shape
    experts = own // IMG_ROW
    loads = copies_of(
        [down_source.at[index] for index in range(experts)],
        [down_ref.at[index] for index in range(experts)],
        semaphores,
    )
    for load in loads:
        load.start()
    slots = received_ref[:, 0].astype(full)
    grads = received_ref[:, 1].astype(full)
    for index in range(experts):
        up = up_ref[index]
        pre = dot(own_rows(slots, index), up)
        cdf, pdf = gelu_parts(pre)
        loads[index].wait()
        down = down_ref[index]
        out = dot((pre * cdf).astype(low), down)
        grad_hidden = dot(own_rows(grads, index), down, 1, 1)
        grad_pre = (grad_hidden * (cdf + pre * pdf)).astype(low)
        grad_slots = dot(grad_pre, up, 1, 1)
        rows = slice(index * IMG_ROW, (index + 1) * IMG_ROW)
        stage[0, :, rows] = out.reshape(groups, IMG_ROW, width)
        stage[1, :, rows] = grad_slots.reshape(groups, IMG_ROW, width)
    back_ref[:, 0] = stage[0].astype(low)
    back_ref[:, 1] = stage[1].astype(low)


def run_experts(received, up, down):
    groups, _, own, width = received.shape
    experts, _, hidden = up.shape
    return pl.pallas_call(
        expert_kernel,
        in_specs=[whole_vmem, whole_vmem, anywhere],
        out_specs=whole_vmem,
        out_shape=shape_of(received.shape, low),
        scratch_shapes=[
            pltpu.VMEM(down.shape, low),
            pltpu.VMEM((2, groups, own, width), full),
            pltpu.SemaphoreType.DMA((experts,)),
        ],
        compiler_params=params(12 + groups // 2),
        cost_estimate=cost(3),
        name="run_experts",
    )(received, up, *keep(down))


def backward_kernel(
    back_ref, slots_ref, gain_ref, ids_ref, inverse_ref, *refs
):
    sources, probs_source, refs = refs[:11], refs[11], refs[12:]
    (output_out, grad_resid_out, grads_out, sums_ref), refs = refs[:4], refs[4:]
    targets, refs = refs[:11], refs[11:]
    probs_ref, output_ref, grad_resid_ref, grads_ref, grad_attn, delta, grad_scores = refs[:7]
    semaphores, probs_semaphores, saves_semaphores = refs[7:]
    loads = copies_of(sources, targets, semaphores)
    cotangent_ref, combine_ref, second_ref, dispatch_ref, resid_ref, attn_ref, proj_ref = targets[:7]
    values_ref, keys_ref, queries_ref, first_ref = targets[7:]
    pairs = resid_ref.shape[1] // LANES

    def load_probs(pair):
        return pltpu.make_async_copy(
            probs_source.at[pl.ds(2 * pair, 2)],
            probs_ref.at[pl.ds(2 * pair, 2)],
            probs_semaphores.at[pair],
        )

    def save_grads(pair):
        return pltpu.make_async_copy(
            grads_ref.at[pair], grads_out.at[pair], saves_semaphores.at[2 + pair]
        )

    saves = copies_of(
        [output_ref, grad_resid_ref], [output_out, grad_resid_out], saves_semaphores
    )
    for load in loads:
        load.start()
    for load in loads[:4]:
        load.wait()
    for pair in range(pairs):
        load_probs(pair).start()
    length, width = resid_ref.shape
    half = LANES // 2
    experts = slots_ref.shape[0]
    count = experts * IMG_ROW
    shape = (experts, IMG_ROW, length)
    slot_out = back_ref[:, 0].reshape(count, width)
    grad_slots = back_ref[:, 1].reshape(count, width)
    cotangent = cotangent_ref[...]
    second_in = second_ref[...]
    combine = combine_ref[...]
    dispatch = dispatch_ref[...]
    member = member_of(ids_ref[...])
    grad_combine = dot(slot_out, cotangent, 1, 1).reshape(shape)
    grad_own = jnp.sum(jnp.where(member[None], grad_combine, 0.0), axis=1, keepdims=True)
    inner = jnp.sum(combine * grad_own, axis=0, keepdims=True)
    grad_logits = combine * (grad_own - inner)
    grad_dispatch = dot(grad_slots, second_in, 1, 1).reshape(shape)
    weighted = jnp.sum(dispatch * grad_dispatch, axis=2, keepdims=True)
    routed = jnp.sum(dispatch * (grad_dispatch - weighted), axis=1, keepdims=True)
    grad_low = (grad_logits + routed).astype(low).reshape(count, length)
    row = lax.broadcasted_iota(jnp.int32, (experts, count), 0) * IMG_ROW
    column = lax.broadcasted_iota(jnp.int32, (experts, count), 1)
    grad_low = dot((row == column).astype(full).astype(low), grad_low).astype(low)
    slot_grad = dot(grad_low, second_in)
    mixing = jnp.concatenate([dispatch.astype(low).reshape(count, length), grad_low], axis=0)
    mixed = jnp.concatenate([grad_slots, slots_ref[...]], axis=0)
    grad_second = dot(mixing, mixed, 0, 0)
    for load in loads[4:7]:
        load.wait()
    resid = resid_ref[...]
    combine_low = jnp.where(member[None], combine, 0.0).astype(low).reshape(count, length)
    output_ref[...] = (resid + dot(combine_low, slot_out, 0, 0)).astype(low)
    saves[0].start()
    normed, factor = norm_parts(resid)
    second_grad = jnp.sum(grad_second * normed, axis=0, keepdims=True)
    gain = gain_ref[...].reshape(1, width)
    grad_resid = cotangent.astype(full) + norm_back(grad_second, normed, factor, gain)
    grad_resid_ref[...] = grad_resid
    saves[1].start()
    grad_branch = grad_resid.astype(low)
    attn = attn_ref[...]
    proj_grad = dot(attn.reshape(width, length), grad_branch).astype(low)
    scaled = dot(proj_ref[...], grad_branch, 1, 1).reshape(pairs, 2, half, length)
    scaled = (scaled * inverse_ref[...][:, :, None, :]).astype(low)
    product = scaled.astype(full) * attn.reshape(scaled.shape).astype(full)
    delta[...] = jnp.sum(product, axis=2)
    grad_attn[...] = scaled.reshape(grad_attn.shape)
    slot_low = slot_grad.astype(low)
    second_low = jnp.broadcast_to(second_grad, (16, width)).astype(low)
    early = pairs * (width + experts + 16)
    for index in range(pairs):
        lanes = slice(index * LANES, (index + 1) * LANES)
        sums_ref[index * width : (index + 1) * width] = proj_grad[:, lanes]
        base = width * pairs + index * experts
        sums_ref[base : base + experts] = slot_low[:, lanes]
        base = (width + experts) * pairs + index * 16
        sums_ref[base : base + 16] = second_low[:, lanes]
    used = early + pairs * 3 * width
    if used < sums_ref.shape[0]:
        sums_ref[used:] = jnp.zeros((sums_ref.shape[0] - used, LANES), low)

    for load in loads[7:]:
        load.wait()
    factor = half**-0.5
    none = jnp.zeros((half, TILE), low)

    def one_pair(pair, carry):
        load_probs(pair).wait()
        for head in range(2):
            rows = slice(head * half, (head + 1) * half)
            for start in range(0, length, TILE):
                span = slice(start, start + TILE)
                grad = grad_attn[pair, rows, span]
                parts = [grad, none] if head == 0 else [none, grad]
                grad_probs = dot(values_ref[pair], jnp.concatenate(parts, axis=0))
                probs = probs_ref[2 * pair + head, :, span].astype(full)
                grad_probs = grad_probs - delta[pair, head : head + 1, span]
                grad_scores[head, :, span] = (probs * grad_probs).astype(low)
            scores = grad_scores[head]
            probs = probs_ref[2 * pair + head]
            grads_ref[pair, 2, rows, :] = dot(grad_attn[pair, rows, :], probs, 1, 1).astype(low)
            grads_ref[pair, 0, rows, :] = (dot(keys_ref[pair, rows, :], scores) * factor).astype(low)
            grads_ref[pair, 1, rows, :] = (
                dot(queries_ref[pair, rows, :], scores, 1, 1) * (1.0 / log2_e)
            ).astype(low)
        sums = dot(first_ref[...], grads_ref[pair].reshape(3 * LANES, length), 1, 1).astype(low)

        for index in range(3):
            base = pl.multiple_of(early + (pair * 3 + index) * width, 16)
            sums_ref[pl.ds(base, width)] = sums[:, index * LANES : (index + 1) * LANES]
        save_grads(pair).start()
        return carry

    lax.fori_loop(0, pairs, one_pair, 0)
    for save in saves + [save_grads(pair) for pair in range(pairs)]:
        save.wait()


def padded(rows, devices):
    return -(-rows // (16 * devices)) * 16 * devices


def backward(back, slots, gain, ids, inverse, arrays, probs, devices):
    length, width = arrays[0].shape
    experts = slots.shape[0]
    pairs = width // LANES
    rows = padded(pairs * (4 * width + experts + 16), devices)
    saved = [((length, width), low), ((length, width), full), ((pairs, 3, LANES, length), low)]
    return pl.pallas_call(
        backward_kernel,
        in_specs=[whole_vmem] * 5 + [anywhere] * (len(arrays) + 1),
        out_specs=[anywhere] * 3 + [whole_vmem],
        out_shape=[kept(*entry) for entry in saved] + [shape_of((rows, LANES), low)],
        scratch_shapes=[pltpu.VMEM(array.shape, array.dtype) for array in (*arrays, probs)]
        + [pltpu.VMEM(*entry) for entry in saved]
        + [
            pltpu.VMEM((pairs, LANES, length), low),
            pltpu.VMEM((pairs, 2, length), full),
            pltpu.VMEM((2, length, length), low),
            pltpu.SemaphoreType.DMA((len(arrays),)),
            pltpu.SemaphoreType.DMA((pairs,)),
            pltpu.SemaphoreType.DMA((2 + pairs,)),
        ],
        compiler_params=params(44 + experts // 8),
        cost_estimate=cost(20),
        name="backward",
    )(back, *keep(slots, gain, ids, inverse, *arrays, probs))


def patch_back_kernel(x_ref, gain_ref, weight_ref, resid_ref, grads_ref, result_ref):
    length, width = x_ref.shape
    pairs = width // LANES
    grads = [grads_ref[pair, part] for part in range(3) for pair in range(pairs)]
    grad_first = dot(weight_ref[...], jnp.concatenate(grads, axis=0)).T
    normed, factor = norm_parts(x_ref[...].astype(full))
    gain = gain_ref[...].reshape(1, width)
    result_ref[...] = resid_ref[...] + norm_back(grad_first, normed, factor, gain)


def patch_back(patches, gain, weight, grad_resid, grads):
    return pl.pallas_call(
        patch_back_kernel,
        in_specs=[whole_vmem] * 5,
        out_specs=whole_vmem,
        out_shape=kept(patches.shape, full),
        compiler_params=params(20),
        cost_estimate=cost(3),
        name="patch_back",
    )(*keep(patches, gain, weight, grad_resid, grads))


def weights_kernel(copies, *refs):
    received = refs[:copies]
    up_ref, down_ref, up_grad_ref, down_grad_ref, slots, grads = refs[copies:]
    expert = pl.program_id(0)
    groups, _, own, width = received[0].shape
    count = groups * IMG_ROW
    for index in range(own // IMG_ROW):

        @pl.when(jnp.logical_and(expert == index, pl.program_id(1) == 0))
        def _():
            for copy, ref in enumerate(received):
                rows = slice(copy * count, (copy + 1) * count)
                slots[rows] = own_rows(ref[:, 0].astype(full), index)
                grads[rows] = own_rows(ref[:, 1].astype(full), index)

    pre = dot(slots[...], up_ref[0])
    cdf, pdf = gelu_parts(pre)
    down_grad_ref[0] = dot((pre * cdf).astype(low), grads[...], 0, 0)
    grad_hidden = dot(grads[...], down_ref[0], 1, 1)
    grad_pre = (grad_hidden * (cdf + pre * pdf)).astype(low)
    up_grad_ref[0] = dot(slots[...], grad_pre, 0, 0)


def weight_grads(received, up, down):
    groups, _, _, width = received[0].shape
    experts, _, hidden = up.shape
    copies = len(received)
    tile = hidden // 3
    up_spec = pl.BlockSpec((1, width, tile), lambda expert, step: (expert, 0, step))
    down_spec = pl.BlockSpec((1, tile, width), lambda expert, step: (expert, step, 0))
    rows = (copies * groups * IMG_ROW, width)

    def kernel(*refs):
        weights_kernel(copies, *refs)

    return pl.pallas_call(
        kernel,
        grid=(experts, 3),
        in_specs=[whole_vmem] * copies + [up_spec, down_spec],
        out_specs=[up_spec, down_spec],
        out_shape=[kept(up.shape, full), kept(down.shape, full)],
        scratch_shapes=[pltpu.VMEM(rows, low)] * 2,
        compiler_params=params(40),
        cost_estimate=cost(9),
        name="weight_grads",
    )(*keep(*received, up, down))


def position(place_ref):
    expert, row = place_ref[0], place_ref[1]
    return row % 2, row // 2 * 2 + expert % 2, expert // 2


def flipped(index, step):
    return jnp.bitwise_xor(index, step)


def rows_at(index, count):
    return pl.ds(pl.multiple_of(index * count, 16), count)


def small_call(kernel, out_shape, name, *arrays, scratch=(), limit=16):
    return pl.pallas_call(
        kernel,
        in_specs=[pl.BlockSpec(memory_space=pltpu.SMEM)] + [whole_vmem] * (len(arrays) - 1),
        out_specs=jax.tree.map(lambda _: whole_vmem, out_shape),
        out_shape=out_shape,
        scratch_shapes=scratch,
        compiler_params=params(limit),
        cost_estimate=cost(1),
        name=name,
    )(*arrays)


def core_kernel(place_ref, mine_ref, other_ref, *outs):
    core, quarter, _ = position(place_ref)
    count = outs[0].shape[0]
    for step, out in enumerate(outs):
        rows = rows_at(core * 4 + flipped(quarter, step), count)
        out[...] = (mine_ref[rows].astype(full) + other_ref[rows].astype(full)).astype(out.dtype)


def plane_kernel(place_ref, *refs):
    total = refs[0][...]
    for other in refs[1:-1]:
        total = total + other[...].astype(full)
    refs[-1][...] = total.astype(low)


def line_kernel(place_ref, *refs):
    _, _, layer = position(place_ref)
    pieces, out, terms = refs[:-2], refs[-2], refs[-1]
    for step, piece in enumerate(pieces):
        terms[flipped(layer, step)] = piece[...]
    out[...] = jnp.sum(terms[...].astype(full), axis=0).astype(low)


def finish_parts(place_ref, parts, whole):
    core, quarter, _ = position(place_ref)
    for index, part in enumerate(parts):
        half = flipped(core, index // 4)
        whole[rows_at(half * 4 + flipped(quarter, index % 4), part.shape[0])] = part[...]


def finish_kernel(
    total, place_ref, weight_ref, gain_ref, *refs
):
    parts = refs[:8]
    first_ref, qkv_ref, proj_ref, second_ref, slot_ref, sums = refs[8:]
    finish_parts(place_ref, parts, sums)
    width = weight_ref.shape[0]
    pairs = width // LANES
    own = slot_ref.shape[0]
    base = (width + total + 16) * pairs
    seconds = []
    for index in range(pairs):
        lanes = slice(index * LANES, (index + 1) * LANES)
        proj_ref[:, lanes] = sums[index * width : (index + 1) * width].astype(full)
        start = (width + total) * pairs + index * 16
        seconds.append(sums[start : start + 16].astype(full)[0:1])
        start = width * pairs + index * total
        row = lax.broadcasted_iota(jnp.int32, (own, total), 0) + place_ref[0] * own
        column = lax.broadcasted_iota(jnp.int32, (own, total), 1)
        chosen = (row == column).astype(full).astype(low)
        slot_ref[:, lanes] = dot(chosen, sums[start : start + total])
    second_ref[...] = jnp.concatenate(seconds, axis=1).reshape(width)
    first = jnp.zeros((width, 1), full)
    for pair in range(pairs):
        for part in range(3):
            lanes = slice(part * width + pair * LANES, part * width + (pair + 1) * LANES)
            start = base + (pair * 3 + part) * width
            grad = sums[start : start + width].astype(full)
            qkv_ref[:, lanes] = grad
            product = grad * weight_ref[:, lanes].astype(full)
            first = first + jnp.sum(product, axis=1, keepdims=True)
    row = jnp.broadcast_to(first, (width, LANES)).T[0:1]
    first_ref[...] = (row / gain_ref[...].reshape(1, width)).reshape(width)


def finish(place, parts, weight, gain, experts, own):
    width = weight.shape[0]

    def kernel(*refs):
        finish_kernel(experts, *refs)

    return pl.pallas_call(
        kernel,
        in_specs=[pl.BlockSpec(memory_space=pltpu.SMEM)] + [whole_vmem] * (2 + len(parts)),
        out_specs=[whole_vmem] * 5,
        out_shape=[
            shape_of((width,), full),
            shape_of(weight.shape, full),
            shape_of((width, width), full),
            shape_of((width,), full),
            shape_of((own, width), full),
        ],
        scratch_shapes=[pltpu.VMEM((sum(part.shape[0] for part in parts), LANES), low)],
        compiler_params=params(20),
        cost_estimate=cost(3),
        name="finish",
    )(place, *keep(weight, gain), *parts)


def per_device(
    patches,
    image_ids,
    first_gain,
    qkv_weight,
    proj_weight,
    second_gain,
    slot_params,
    up_weight,
    down_weight,
    cotangent,
):
    groups = lax.axis_size("expert")
    copies = lax.axis_size("rows")
    devices = groups * copies
    _, length, width = patches.shape
    own = slot_params.shape[1]
    experts = own * groups
    spread = jnp.broadcast_to(slot_params.T[None], (groups, own, width))
    slots = lax.all_to_all(spread, "expert", 0, 0, tiled=True).reshape(experts, width)
    patches = patches[0]
    cotangent = cotangent[0]
    probs, queries, keys, values, first_in, attn, inverse, resid, second_in = attend(
        patches, image_ids, first_gain, qkv_weight, proj_weight, second_gain
    )
    dispatch, combine, send = route(second_in, slots, image_ids, cotangent, groups)
    received = lax.all_to_all(send, "expert", 0, 0, tiled=True)
    back = run_experts(received, up_weight, down_weight)
    back = lax.all_to_all(back, "expert", 0, 0, tiled=True)
    others = [
        lax.ppermute(received, "rows", [(index, index ^ step) for index in range(copies)])
        for step in range(1, copies)
    ]
    saved = [cotangent, combine, second_in, dispatch, resid, attn, proj_weight]
    saved += [values, keys, queries, first_in]
    output, grad_resid, grads, terms = backward(
        back, slots, second_gain, image_ids, inverse, saved, probs, devices
    )
    place = jnp.stack([lax.axis_index("expert"), lax.axis_index("rows")]).astype(jnp.int32)
    layers = groups // 2

    def flip(array, expert, row):
        pairs = [
            (index, (index // copies ^ expert) * copies + (index % copies ^ row))
            for index in range(devices)
        ]
        return lax.ppermute(array, both_axes, pairs)

    terms, others = lax.optimization_barrier((terms, others))
    share = terms.shape[0] // devices
    quarter = (layers * share, LANES)
    mine, *sends = small_call(
        core_kernel, [shape_of(quarter, full)] + [shape_of(quarter, low)] * 3, "add_core",
        place, terms, flip(terms, 0, 1),
    )
    arrived = [flip(send, step % 2, step // 2 * 2) for step, send in enumerate(sends, 1)]
    grads, _ = lax.optimization_barrier((grads, mine))
    patch_grad = patch_back(patches, first_gain, qkv_weight, grad_resid, grads)
    arrived, patch_grad = lax.optimization_barrier((arrived, patch_grad))
    mine = small_call(plane_kernel, shape_of(quarter, low), "add_plane", place, mine, *arrived)
    arrived = [flip(mine, step * 2, 0) for step in range(1, layers)]
    others, _ = lax.optimization_barrier((others, mine))
    up_grad, down_grad = weight_grads([received] + others, up_weight, down_weight)
    arrived, up_grad, down_grad = lax.optimization_barrier((arrived, up_grad, down_grad))
    mine = small_call(
        line_kernel, shape_of(quarter, low), "add_line", place, mine, *arrived,
        scratch=[pltpu.VMEM((layers, *quarter), low)], limit=12 + layers,
    )
    arrived = [flip(mine, step % 2, step // 2 * 2) for step in range(1, 4)]
    parts = [mine] + arrived
    parts = parts + [flip(part, 0, 1) for part in parts]
    first_grad, qkv_grad, proj_grad, second_grad, slot_grad = finish(
        place, parts, qkv_weight, first_gain, experts, own
    )
    return (
        output[None],
        patch_grad[None],
        first_grad,
        qkv_grad,
        proj_grad,
        second_grad,
        slot_grad.T,
        up_grad,
        down_grad,
    )


def solution(mesh):
    return jax.shard_map(
        per_device,
        mesh=mesh,
        in_specs=(
            P(("expert", "rows"), None, None),
            P(("expert", "rows"), None),
            P(),
            P(),
            P(),
            P(),
            P(None, "expert"),
            P("expert", None, None),
            P("expert", None, None),
            P(("expert", "rows"), None, None),
        ),
        out_specs=(
            P(("expert", "rows"), None, None),
            P(("expert", "rows"), None, None),
            P(),
            P(),
            P(),
            P(),
            P(None, "expert"),
            P("expert", None, None),
            P("expert", None, None),
        ),
        check_vma=False,
    )
```

```python
import jax
import jax.numpy as jnp
from jax import lax
from jax.experimental import pallas as pl
from jax.experimental.pallas import tpu as pltpu
from jax.sharding import PartitionSpec as P

HEADS = 6
IMG_ROW = 8
LANES = 128
TILE = 256

epsilon = 1e-06
masked_fill = -1e30
score_bound = 64.0
log2_e = 1.4426950408889634
low = jnp.bfloat16
full = jnp.float32
whole_vmem = pl.BlockSpec(memory_space=pltpu.VMEM)
anywhere = pl.BlockSpec(memory_space=pl.ANY)
both_axes = ("expert", "rows")


def dot(left, right, left_dim=1, right_dim=0):
    return lax.dot_general(
        left, right, (((left_dim,), (right_dim,)), ((), ())), preferred_element_type=full
    )


def shape_of(shape, dtype):
    return jax.ShapeDtypeStruct(shape, dtype)


def kept(shape, dtype):
    return pltpu.HBM(shape, dtype)


def keep(*arrays):
    return [pltpu.with_memory_space_constraint(array, pltpu.HBM) for array in arrays]


def params(mib):
    return pltpu.CompilerParams(vmem_limit_bytes=mib << 20)


def cost(microseconds):
    return pl.CostEstimate(
        flops=0, transcendentals=0, bytes_accessed=int(microseconds * 3.6e6)
    )


def norm_parts(values):
    centred = values - jnp.mean(values, axis=-1, keepdims=True)
    factor = lax.rsqrt(jnp.mean(centred * centred, axis=-1, keepdims=True) + epsilon)
    return centred * factor, factor


def norm_back(grad_norm, normed, factor, gain):
    scaled = grad_norm * gain
    return factor * (
        scaled
        - jnp.mean(scaled, axis=-1, keepdims=True)
        - normed * jnp.mean(scaled * normed, axis=-1, keepdims=True)
    )


def member_of(ids):
    images = lax.broadcasted_iota(jnp.int32, (IMG_ROW, ids.shape[1]), 0)
    return images == ids


def gelu_parts(pre):
    cdf = 0.5 * (1.0 + lax.erf(pre * 0.7071067811865476))
    pdf = 0.3989422804014327 * jnp.exp(-0.5 * pre * pre)
    return cdf, pdf


def copies_of(sources, targets, semaphores):
    return [
        pltpu.make_async_copy(source, target, semaphores.at[index])
        for index, (source, target) in enumerate(zip(sources, targets, strict=True))
    ]


def attend_kernel(*refs):
    sources, refs = refs[:6], refs[6:]
    outs, second_ref, same, refs = refs[:8], refs[8], refs[9], refs[10:]
    probs_out, saved, refs = outs[0], refs[:7], refs[7:]
    queries_ref, keys_ref, value_rows_ref, first_ref = saved[:4]
    attn_ref, inverse_ref, resid_ref = saved[4:]
    probs_ref, key_rows, values, mask_rows, bound, semaphores, probs_semaphores = refs[:7]
    x_ref, gain_ref, weight_ref, ids_ref, proj_ref, second_gain_ref = refs[7:13]
    loads = copies_of(sources, refs[7:13], refs[13])
    for load in loads:
        load.start()
    length, width = x_ref.shape
    pairs = width // LANES
    half = LANES // 2
    saves = copies_of(saved, outs[1:], semaphores)

    def save_probs(head):
        return pltpu.make_async_copy(
            probs_ref.at[head], probs_out.at[head], probs_semaphores.at[head]
        )

    for load in loads[:2]:
        load.wait()
    normed, _ = norm_parts(x_ref[...].astype(full))
    first_in = (normed * gain_ref[...].reshape(1, width)).astype(low)
    loads[2].wait()
    turned = dot(weight_ref[...], first_in, 0, 1)
    scaled = (turned[:width] * (half**-0.5 * log2_e)).astype(low)
    turned = turned[width:].astype(low)
    queries_ref[...] = scaled.reshape(pairs, LANES, length)
    keys_ref[...] = turned[:width].reshape(pairs, LANES, length)
    values[...] = turned[width:].reshape(pairs, LANES, length)
    norms = []
    for part in (scaled, turned[:width]):
        square = part.astype(full).reshape(2 * pairs, half, length)
        norms.append(jnp.max(jnp.sum(square * square, axis=1), axis=1, keepdims=True))
    bound[0] = jnp.max(norms[0] * norms[1])
    rows = dot(first_in, weight_ref[:, width:]).astype(low)
    for index in range(pairs):
        key_rows[index] = rows[:, index * LANES : (index + 1) * LANES]
        value_rows_ref[index] = rows[:, width + index * LANES : width + (index + 1) * LANES]
    first_ref[...] = first_in.T
    for save in saves[:4]:
        save.start()
    loads[3].wait()
    images = lax.broadcasted_iota(jnp.int32, (LANES, length), 0)
    matching = images == ids_ref[...]
    same[...] = matching.astype(full).astype(low)
    other = jnp.where(jnp.logical_or(matching, images >= IMG_ROW), 0.0, masked_fill)
    mask_rows[...] = other.T.astype(low)

    def attend_pair(pair, raise_scores):
        keys = jnp.concatenate([key_rows[pair], mask_rows[...]], axis=1)
        none = jnp.zeros((half, TILE), low)
        ones = jnp.ones((16, length), low)
        for head in range(2):
            rows = slice(head * half, (head + 1) * half)
            for start in range(0, length, TILE):
                span = slice(start, start + TILE)
                query = queries_ref[pair, rows, span]
                parts = [query, none] if head == 0 else [none, query]
                scores = dot(keys, jnp.concatenate(parts + [same[:, span]], axis=0))
                probs_ref[2 * pair + head, :, span] = raise_scores(scores).astype(low)
            save_probs(2 * pair + head).start()
        for head in range(2):
            rows = slice(head * half, (head + 1) * half)
            value = jnp.concatenate([values[pair, rows, :], ones], axis=0)
            mixed = dot(value, probs_ref[2 * pair + head])
            inverse = 1.0 / mixed[half : half + 1]
            inverse_ref[pair, head : head + 1] = inverse
            attn_ref[pair, rows] = (mixed[:half] * inverse).astype(low)

    small = bound[0] < score_bound * score_bound

    def one_pair(pair, carry):
        @pl.when(small)
        def _():
            attend_pair(pair, jnp.exp2)

        @pl.when(jnp.logical_not(small))
        def _():
            attend_pair(
                pair,
                lambda scores: jnp.exp2(scores - jnp.max(scores, axis=0, keepdims=True)),
            )

        return carry

    lax.fori_loop(0, pairs, one_pair, 0)
    for save in saves[4:6]:
        save.start()
    for load in loads[4:]:
        load.wait()
    attn = attn_ref[...].reshape(width, length)
    resid = x_ref[...].astype(full) + dot(attn, proj_ref[...], 0, 0)
    resid_ref[...] = resid
    saves[6].start()
    normed, _ = norm_parts(resid)
    second_ref[...] = (normed * second_gain_ref[...].reshape(1, width)).astype(low)
    for save in saves:
        save.wait()
    for head in range(2 * pairs):
        save_probs(head).wait()


def attend(patches, ids, gain, weight, proj, second_gain):
    inputs = patches, gain, weight, ids, proj, second_gain
    length, width = patches.shape
    pairs = width // LANES
    stack = (pairs, LANES, length)
    rows = (pairs, length, LANES)
    probs = (2 * pairs, length, length)
    saved = [
        (stack, low),
        (stack, low),
        (rows, low),
        ((width, length), low),
        (stack, low),
        ((pairs, 2, length), full),
        ((length, width), full),
    ]
    return pl.pallas_call(
        attend_kernel,
        in_specs=[anywhere] * 6,
        out_specs=[anywhere] * 8 + [whole_vmem] * 2,
        out_shape=[kept(probs, low)]
        + [kept(*entry) for entry in saved]
        + [shape_of((length, width), low), shape_of((LANES, length), low)],
        scratch_shapes=[pltpu.VMEM(*entry) for entry in saved]
        + [
            pltpu.VMEM(probs, low),
            pltpu.VMEM(rows, low),
            pltpu.VMEM(stack, low),
            pltpu.VMEM((length, LANES), low),
            pltpu.SMEM((1,), full),
            pltpu.SemaphoreType.DMA((7,)),
            pltpu.SemaphoreType.DMA((2 * pairs,)),
        ]
        + [pltpu.VMEM(array.shape, array.dtype) for array in inputs]
        + [pltpu.SemaphoreType.DMA((6,))],
        compiler_params=params(30),
        cost_estimate=cost(12),
        name="attend",
    )(*keep(*inputs))


def slot_rows(slots):
    experts = slots.shape[0]
    row = lax.broadcasted_iota(jnp.int32, (experts * IMG_ROW, experts), 0) // IMG_ROW
    column = lax.broadcasted_iota(jnp.int32, (experts * IMG_ROW, experts), 1)
    return dot((row == column).astype(full).astype(low), slots).astype(low)


def route_kernel(
    second_ref, slots_ref, same_ref, cotangent_source,
    second_out, dispatch_out, combine_out, send_ref,
    cotangent_ref, dispatch_ref, combine_ref, semaphores,
):
    length, width = second_ref.shape
    experts = slots_ref.shape[0]
    shape = (experts, IMG_ROW, length)
    load, *saves = copies_of(
        [cotangent_source, second_ref, dispatch_ref, combine_ref],
        [cotangent_ref, second_out, dispatch_out, combine_out],
        semaphores,
    )
    load.start()
    saves[0].start()
    second_in = second_ref[...]
    logits = dot(slot_rows(slots_ref[...]), second_in, 1, 1).reshape(shape)
    present = same_ref[...].astype(full)[:IMG_ROW]
    member = present > 0.0
    masked = jnp.where(member[None], logits, masked_fill)
    top = jnp.max(masked, axis=2, keepdims=True)
    raised = jnp.where(member[None], jnp.exp(masked - top), 0.0)
    absent = 1.0 - jnp.max(present, axis=1, keepdims=True)
    total = jnp.sum(raised, axis=2, keepdims=True) + absent[None]
    dispatch = raised * (1.0 / total)
    dispatch_ref[...] = dispatch
    saves[1].start()
    raised = jnp.exp(logits - jnp.max(logits, axis=0, keepdims=True))
    combine = raised * (1.0 / jnp.sum(raised, axis=0, keepdims=True))
    combine_ref[...] = combine
    saves[2].start()
    dispatch_low = dispatch.astype(low).reshape(-1, length)
    combine_low = jnp.where(member[None], combine, 0.0).astype(low).reshape(-1, length)
    block = (send_ref.shape[0], send_ref.shape[2], width)
    send_ref[:, 0] = dot(dispatch_low, second_in).astype(low).reshape(block)
    load.wait()
    send_ref[:, 1] = dot(combine_low, cotangent_ref[...]).astype(low).reshape(block)
    for save in saves:
        save.wait()


def route(second_in, slots, same, cotangent, groups):
    length, width = second_in.shape
    experts = slots.shape[0]
    own = experts // groups * IMG_ROW
    shape = (experts, IMG_ROW, length)
    return pl.pallas_call(
        route_kernel,
        in_specs=[whole_vmem] * 3 + [anywhere],
        out_specs=[anywhere] * 3 + [whole_vmem],
        out_shape=[kept((length, width), low)]
        + [kept(shape, full)] * 2
        + [shape_of((groups, 2, own, width), low)],
        scratch_shapes=[pltpu.VMEM((length, width), low)]
        + [pltpu.VMEM(shape, full)] * 2
        + [pltpu.SemaphoreType.DMA((4,))],
        compiler_params=params(14 + experts // 4),
        cost_estimate=cost(3),
        name="route",
    )(second_in, slots, same, *keep(cotangent))


def own_rows(received, expert):
    groups, _, width = received.shape
    rows = received[:, expert * IMG_ROW : (expert + 1) * IMG_ROW]
    return rows.reshape(groups * IMG_ROW, width).astype(low)


def expert_kernel(received_ref, up_ref, down_source, back_ref, down_ref, stage, semaphores):
    groups, _, own, width = received_ref.shape
    experts = own // IMG_ROW
    loads = copies_of(
        [down_source.at[index] for index in range(experts)],
        [down_ref.at[index] for index in range(experts)],
        semaphores,
    )
    for load in loads:
        load.start()
    slots = received_ref[:, 0].astype(full)
    grads = received_ref[:, 1].astype(full)
    for index in range(experts):
        up = up_ref[index]
        pre = dot(own_rows(slots, index), up)
        cdf, pdf = gelu_parts(pre)
        loads[index].wait()
        down = down_ref[index]
        out = dot((pre * cdf).astype(low), down)
        grad_hidden = dot(own_rows(grads, index), down, 1, 1)
        grad_pre = (grad_hidden * (cdf + pre * pdf)).astype(low)
        grad_slots = dot(grad_pre, up, 1, 1)
        rows = slice(index * IMG_ROW, (index + 1) * IMG_ROW)
        stage[0, :, rows] = out.reshape(groups, IMG_ROW, width)
        stage[1, :, rows] = grad_slots.reshape(groups, IMG_ROW, width)
    back_ref[:, 0] = stage[0].astype(low)
    back_ref[:, 1] = stage[1].astype(low)


def run_experts(received, up, down):
    groups, _, own, width = received.shape
    experts, _, hidden = up.shape
    return pl.pallas_call(
        expert_kernel,
        in_specs=[whole_vmem, whole_vmem, anywhere],
        out_specs=whole_vmem,
        out_shape=shape_of(received.shape, low),
        scratch_shapes=[
            pltpu.VMEM(down.shape, low),
            pltpu.VMEM((2, groups, own, width), full),
            pltpu.SemaphoreType.DMA((experts,)),
        ],
        compiler_params=params(12 + groups // 2),
        cost_estimate=cost(3),
        name="run_experts",
    )(received, up, *keep(down))


def backward_kernel(back_ref, *refs):
    sources, probs_source, refs = refs[:15], refs[15], refs[16:]
    (output_out, grad_resid_out, grads_out, sums_ref), refs = refs[:4], refs[4:]
    targets, refs = refs[:15], refs[15:]
    probs_ref, output_ref, grad_resid_ref, grads_ref, grad_attn, delta, grad_scores = refs[:7]
    semaphores, probs_semaphores, saves_semaphores = refs[7:]
    loads = copies_of(sources, targets, semaphores)
    ids_ref, cotangent_ref, combine_ref, second_ref, dispatch_ref, slots_ref = targets[:6]
    resid_ref, gain_ref, attn_ref, proj_ref, inverse_ref = targets[6:11]
    values_ref, keys_ref, queries_ref, first_ref = targets[11:]
    pairs = resid_ref.shape[1] // LANES

    def load_probs(pair):
        return pltpu.make_async_copy(
            probs_source.at[pl.ds(2 * pair, 2)],
            probs_ref.at[pl.ds(2 * pair, 2)],
            probs_semaphores.at[pair],
        )

    def save_grads(pair):
        return pltpu.make_async_copy(
            grads_ref.at[pair], grads_out.at[pair], saves_semaphores.at[2 + pair]
        )

    saves = copies_of(
        [output_ref, grad_resid_ref], [output_out, grad_resid_out], saves_semaphores
    )
    for load in loads[:11]:
        load.start()
    for load in loads[:6]:
        load.wait()
    for load in loads[11:]:
        load.start()
    load_probs(0).start()
    length, width = resid_ref.shape
    half = LANES // 2
    experts = slots_ref.shape[0]
    count = experts * IMG_ROW
    shape = (experts, IMG_ROW, length)
    slot_out = back_ref[:, 0].reshape(count, width)
    grad_slots = back_ref[:, 1].reshape(count, width)
    cotangent = cotangent_ref[...]
    second_in = second_ref[...]
    combine = combine_ref[...]
    dispatch = dispatch_ref[...]
    member = member_of(ids_ref[...])
    grad_combine = dot(slot_out, cotangent, 1, 1).reshape(shape)
    grad_own = jnp.sum(jnp.where(member[None], grad_combine, 0.0), axis=1, keepdims=True)
    inner = jnp.sum(combine * grad_own, axis=0, keepdims=True)
    grad_logits = combine * (grad_own - inner)
    grad_dispatch = dot(grad_slots, second_in, 1, 1).reshape(shape)
    weighted = jnp.sum(dispatch * grad_dispatch, axis=2, keepdims=True)
    routed = jnp.sum(dispatch * (grad_dispatch - weighted), axis=1, keepdims=True)
    grad_low = (grad_logits + routed).astype(low).reshape(count, length)
    row = lax.broadcasted_iota(jnp.int32, (experts, count), 0) * IMG_ROW
    column = lax.broadcasted_iota(jnp.int32, (experts, count), 1)
    grad_low = dot((row == column).astype(full).astype(low), grad_low).astype(low)
    slot_grad = dot(grad_low, second_in)
    mixing = jnp.concatenate([dispatch.astype(low).reshape(count, length), grad_low], axis=0)
    mixed = jnp.concatenate([grad_slots, slots_ref[...]], axis=0)
    grad_second = dot(mixing, mixed, 0, 0)
    for load in loads[6:11]:
        load.wait()
    resid = resid_ref[...]
    combine_low = jnp.where(member[None], combine, 0.0).astype(low).reshape(count, length)
    output_ref[...] = (resid + dot(combine_low, slot_out, 0, 0)).astype(low)
    saves[0].start()
    normed, factor = norm_parts(resid)
    second_grad = jnp.sum(grad_second * normed, axis=0, keepdims=True)
    gain = gain_ref[...].reshape(1, width)
    grad_resid = cotangent.astype(full) + norm_back(grad_second, normed, factor, gain)
    grad_resid_ref[...] = grad_resid
    saves[1].start()
    grad_branch = grad_resid.astype(low)
    attn = attn_ref[...]
    proj_grad = dot(attn.reshape(width, length), grad_branch).astype(low)
    scaled = dot(proj_ref[...], grad_branch, 1, 1).reshape(pairs, 2, half, length)
    scaled = (scaled * inverse_ref[...][:, :, None, :]).astype(low)
    product = scaled.astype(full) * attn.reshape(scaled.shape).astype(full)
    delta[...] = jnp.sum(product, axis=2)
    grad_attn[...] = scaled.reshape(grad_attn.shape)
    slot_low = slot_grad.astype(low)
    second_low = jnp.broadcast_to(second_grad, (16, width)).astype(low)
    early = pairs * (width + experts + 16)
    for index in range(pairs):
        lanes = slice(index * LANES, (index + 1) * LANES)
        sums_ref[index * width : (index + 1) * width] = proj_grad[:, lanes]
        base = width * pairs + index * experts
        sums_ref[base : base + experts] = slot_low[:, lanes]
        base = (width + experts) * pairs + index * 16
        sums_ref[base : base + 16] = second_low[:, lanes]
    used = early + pairs * 3 * width
    if used < sums_ref.shape[0]:
        sums_ref[used:] = jnp.zeros((sums_ref.shape[0] - used, LANES), low)

    for load in loads[11:]:
        load.wait()
    factor = half**-0.5
    none = jnp.zeros((half, TILE), low)

    def one_pair(pair, carry):
        load_probs(pair).wait()

        @pl.when(pair < pairs - 1)
        def _():
            load_probs(pair + 1).start()

        for head in range(2):
            rows = slice(head * half, (head + 1) * half)
            for start in range(0, length, TILE):
                span = slice(start, start + TILE)
                grad = grad_attn[pair, rows, span]
                parts = [grad, none] if head == 0 else [none, grad]
                grad_probs = dot(values_ref[pair], jnp.concatenate(parts, axis=0))
                probs = probs_ref[2 * pair + head, :, span].astype(full)
                grad_probs = grad_probs - delta[pair, head : head + 1, span]
                grad_scores[head, :, span] = (probs * grad_probs).astype(low)
            scores = grad_scores[head]
            probs = probs_ref[2 * pair + head]
            grads_ref[pair, 2, rows, :] = dot(grad_attn[pair, rows, :], probs, 1, 1).astype(low)
            grads_ref[pair, 0, rows, :] = (dot(keys_ref[pair, rows, :], scores) * factor).astype(low)
            grads_ref[pair, 1, rows, :] = (
                dot(queries_ref[pair, rows, :], scores, 1, 1) * (1.0 / log2_e)
            ).astype(low)
        sums = dot(first_ref[...], grads_ref[pair].reshape(3 * LANES, length), 1, 1).astype(low)

        for index in range(3):
            base = pl.multiple_of(early + (pair * 3 + index) * width, 16)
            sums_ref[pl.ds(base, width)] = sums[:, index * LANES : (index + 1) * LANES]
        save_grads(pair).start()
        return carry

    lax.fori_loop(0, pairs, one_pair, 0)
    for save in saves + [save_grads(pair) for pair in range(pairs)]:
        save.wait()


def padded(rows, parts):
    return -(-rows // (16 * parts)) * 16 * parts


def backward(back, arrays, probs):
    length, width = arrays[1].shape
    experts = arrays[5].shape[0]
    pairs = width // LANES
    rows = padded(pairs * (4 * width + experts + 16), 8)
    saved = [((length, width), low), ((length, width), full), ((pairs, 3, LANES, length), low)]
    return pl.pallas_call(
        backward_kernel,
        in_specs=[whole_vmem] + [anywhere] * (len(arrays) + 1),
        out_specs=[anywhere] * 3 + [whole_vmem],
        out_shape=[kept(*entry) for entry in saved] + [shape_of((rows, LANES), low)],
        scratch_shapes=[pltpu.VMEM(array.shape, array.dtype) for array in (*arrays, probs)]
        + [pltpu.VMEM(*entry) for entry in saved]
        + [
            pltpu.VMEM((pairs, LANES, length), low),
            pltpu.VMEM((pairs, 2, length), full),
            pltpu.VMEM((2, length, length), low),
            pltpu.SemaphoreType.DMA((len(arrays),)),
            pltpu.SemaphoreType.DMA((pairs,)),
            pltpu.SemaphoreType.DMA((2 + pairs,)),
        ],
        compiler_params=params(38 + experts // 8),
        cost_estimate=cost(20),
        name="backward",
    )(back, *keep(*arrays, probs))


def patch_back_kernel(x_ref, gain_ref, weight_ref, resid_ref, grads_ref, result_ref):
    length, width = x_ref.shape
    pairs = width // LANES
    grads = [grads_ref[pair, part] for part in range(3) for pair in range(pairs)]
    grad_first = dot(weight_ref[...], jnp.concatenate(grads, axis=0)).T
    normed, factor = norm_parts(x_ref[...].astype(full))
    gain = gain_ref[...].reshape(1, width)
    result_ref[...] = resid_ref[...] + norm_back(grad_first, normed, factor, gain)


def patch_back(patches, gain, weight, grad_resid, grads):
    return pl.pallas_call(
        patch_back_kernel,
        in_specs=[whole_vmem] * 5,
        out_specs=whole_vmem,
        out_shape=kept(patches.shape, full),
        compiler_params=params(20),
        cost_estimate=cost(3),
        name="patch_back",
    )(*keep(patches, gain, weight, grad_resid, grads))


def weights_kernel(copies, *refs):
    received = refs[:copies]
    up_ref, down_ref, up_grad_ref, down_grad_ref, slots, grads = refs[copies:]
    expert = pl.program_id(0)
    groups, _, own, width = received[0].shape
    count = groups * IMG_ROW
    for index in range(own // IMG_ROW):

        @pl.when(jnp.logical_and(expert == index, pl.program_id(1) == 0))
        def _():
            for copy, ref in enumerate(received):
                rows = slice(copy * count, (copy + 1) * count)
                slots[rows] = own_rows(ref[:, 0].astype(full), index)
                grads[rows] = own_rows(ref[:, 1].astype(full), index)

    pre = dot(slots[...], up_ref[0])
    cdf, pdf = gelu_parts(pre)
    down_grad_ref[0] = dot((pre * cdf).astype(low), grads[...], 0, 0)
    grad_hidden = dot(grads[...], down_ref[0], 1, 1)
    grad_pre = (grad_hidden * (cdf + pre * pdf)).astype(low)
    up_grad_ref[0] = dot(slots[...], grad_pre, 0, 0)


def weight_grads(received, up, down):
    groups, _, _, width = received[0].shape
    experts, _, hidden = up.shape
    copies = len(received)
    steps = 1 if copies * groups <= 64 else 3
    tile = hidden // steps
    up_spec = pl.BlockSpec((1, width, tile), lambda expert, step: (expert, 0, step))
    down_spec = pl.BlockSpec((1, tile, width), lambda expert, step: (expert, step, 0))
    rows = (copies * groups * IMG_ROW, width)

    def kernel(*refs):
        weights_kernel(copies, *refs)

    return pl.pallas_call(
        kernel,
        grid=(experts, steps),
        in_specs=[whole_vmem] * copies + [up_spec, down_spec],
        out_specs=[up_spec, down_spec],
        out_shape=[kept(up.shape, full), kept(down.shape, full)],
        scratch_shapes=[pltpu.VMEM(rows, low)] * 2,
        compiler_params=params(40),
        cost_estimate=cost(9),
        name="weight_grads",
    )(*keep(*received, up, down))


def position(place_ref):
    expert, row = place_ref[0], place_ref[1]
    return row % 2, row // 2 * 2 + expert % 2, expert // 2


def flipped(index, step):
    return jnp.bitwise_xor(index, step)


def rows_at(index, count):
    return pl.ds(pl.multiple_of(index * count, 16), count)


def small_call(kernel, out_shape, name, *arrays):
    return pl.pallas_call(
        kernel,
        in_specs=[pl.BlockSpec(memory_space=pltpu.SMEM)] + [whole_vmem] * (len(arrays) - 1),
        out_specs=jax.tree.map(lambda _: whole_vmem, out_shape),
        out_shape=out_shape,
        compiler_params=params(16),
        cost_estimate=cost(1),
        name=name,
    )(*arrays)


def core_kernel(place_ref, mine_ref, other_ref, *outs):
    core, quarter, _ = position(place_ref)
    count = outs[0].shape[0]
    for step, out in enumerate(outs):
        rows = rows_at(core * 4 + flipped(quarter, step), count)
        out[...] = (mine_ref[rows].astype(full) + other_ref[rows].astype(full)).astype(out.dtype)


def plane_kernel(place_ref, *refs):
    total = refs[0][...]
    for other in refs[1:-1]:
        total = total + other[...].astype(full)
    refs[-1][...] = total.astype(low)


def line_kernel(place_ref, mine_ref, other_ref, out_ref):
    out_ref[...] = (mine_ref[...].astype(full) + other_ref[...].astype(full)).astype(low)


def finish_parts(place_ref, parts, whole):
    core, quarter, _ = position(place_ref)
    for index, part in enumerate(parts):
        half = flipped(core, index // 4)
        whole[rows_at(half * 4 + flipped(quarter, index % 4), part.shape[0])] = part[...]


def finish_kernel(
    total, place_ref, weight_ref, gain_ref, *refs
):
    parts = refs[:8]
    first_ref, qkv_ref, proj_ref, second_ref, slot_ref, sums = refs[8:]
    finish_parts(place_ref, parts, sums)
    width = weight_ref.shape[0]
    pairs = width // LANES
    own = slot_ref.shape[0]
    base = (width + total + 16) * pairs
    seconds = []
    for index in range(pairs):
        lanes = slice(index * LANES, (index + 1) * LANES)
        proj_ref[:, lanes] = sums[index * width : (index + 1) * width].astype(full)
        start = (width + total) * pairs + index * 16
        seconds.append(sums[start : start + 16].astype(full)[0:1])
        start = width * pairs + index * total
        row = lax.broadcasted_iota(jnp.int32, (own, total), 0) + place_ref[0] * own
        column = lax.broadcasted_iota(jnp.int32, (own, total), 1)
        chosen = (row == column).astype(full).astype(low)
        slot_ref[:, lanes] = dot(chosen, sums[start : start + total])
    second_ref[...] = jnp.concatenate(seconds, axis=1).reshape(width)
    first = jnp.zeros((width, LANES), full)
    for pair in range(pairs):
        for part in range(3):
            lanes = slice(part * width + pair * LANES, part * width + (pair + 1) * LANES)
            start = base + (pair * 3 + part) * width
            grad = sums[start : start + width].astype(full)
            qkv_ref[:, lanes] = grad
            first = first + grad * weight_ref[:, lanes].astype(full)
    row = jnp.sum(first.T, axis=0, keepdims=True)
    first_ref[...] = (row / gain_ref[...].reshape(1, width)).reshape(width)


def finish(place, parts, weight, gain, experts, own):
    width = weight.shape[0]

    def kernel(*refs):
        finish_kernel(experts, *refs)

    return pl.pallas_call(
        kernel,
        in_specs=[pl.BlockSpec(memory_space=pltpu.SMEM)] + [whole_vmem] * (2 + len(parts)),
        out_specs=[whole_vmem] * 5,
        out_shape=[
            shape_of((width,), full),
            shape_of(weight.shape, full),
            shape_of((width, width), full),
            shape_of((width,), full),
            shape_of((own, width), full),
        ],
        scratch_shapes=[pltpu.VMEM((sum(part.shape[0] for part in parts), LANES), low)],
        compiler_params=params(20),
        cost_estimate=cost(3),
        name="finish",
    )(place, weight, gain, *parts)


def per_device(
    patches,
    image_ids,
    first_gain,
    qkv_weight,
    proj_weight,
    second_gain,
    slot_params,
    up_weight,
    down_weight,
    cotangent,
):
    groups = lax.axis_size("expert")
    copies = lax.axis_size("rows")
    devices = groups * copies
    _, length, width = patches.shape
    own = slot_params.shape[1]
    experts = own * groups
    spread = jnp.broadcast_to(slot_params.T[None], (groups, own, width))
    slots = lax.all_to_all(spread, "expert", 0, 0, tiled=True).reshape(experts, width)
    patches = patches[0]
    cotangent = cotangent[0]
    probs, queries, keys, values, first_in, attn, inverse, resid, second_in, same = attend(
        patches, image_ids, first_gain, qkv_weight, proj_weight, second_gain
    )
    second_in, dispatch, combine, send = route(second_in, slots, same, cotangent, groups)
    received = lax.all_to_all(send, "expert", 0, 0, tiled=True)
    back = run_experts(received, up_weight, down_weight)
    back = lax.all_to_all(back, "expert", 0, 0, tiled=True)
    others = [
        lax.ppermute(received, "rows", [(index, index ^ step) for index in range(copies)])
        for step in range(1, copies)
    ]
    saved = [image_ids, cotangent, combine, second_in, dispatch, slots]
    saved += [resid, second_gain, attn, proj_weight, inverse, values, keys, queries, first_in]
    output, grad_resid, grads, terms = backward(back, saved, probs)
    place = jnp.stack([lax.axis_index("expert"), lax.axis_index("rows")]).astype(jnp.int32)
    layers = groups // 2

    def flip(array, expert, row):
        pairs = [
            (index, (index // copies ^ expert) * copies + (index % copies ^ row))
            for index in range(devices)
        ]
        return lax.ppermute(array, both_axes, pairs)

    terms, others = lax.optimization_barrier((terms, others))
    quarter = (terms.shape[0] // 8, LANES)
    mine, *sends = small_call(
        core_kernel, [shape_of(quarter, full)] + [shape_of(quarter, low)] * 3, "add_core",
        place, terms, flip(terms, 0, 1),
    )
    arrived = [flip(send, step % 2, step // 2 * 2) for step, send in enumerate(sends, 1)]
    grads, _ = lax.optimization_barrier((grads, mine))
    patch_grad = patch_back(patches, first_gain, qkv_weight, grad_resid, grads)
    arrived, patch_grad = lax.optimization_barrier((arrived, patch_grad))
    mine = small_call(plane_kernel, shape_of(quarter, low), "add_plane", place, mine, *arrived)
    step = 1
    while step < layers:
        arrived = flip(mine, step * 2, 0)
        if step * 2 >= layers:
            others, _ = lax.optimization_barrier((others, mine))
            up_grad, down_grad = weight_grads([received] + others, up_weight, down_weight)
            arrived, up_grad, down_grad = lax.optimization_barrier((arrived, up_grad, down_grad))
        mine = small_call(
            line_kernel, shape_of(quarter, low), f"add_line_{step}", place, mine, arrived
        )
        step *= 2
    arrived = [flip(mine, step % 2, step // 2 * 2) for step in range(1, 4)]
    parts = [mine] + arrived
    parts = parts + [flip(part, 0, 1) for part in parts]
    first_grad, qkv_grad, proj_grad, second_grad, slot_grad = finish(
        place, parts, qkv_weight, first_gain, experts, own
    )
    return (
        output[None],
        patch_grad[None],
        first_grad,
        qkv_grad,
        proj_grad,
        second_grad,
        slot_grad.T,
        up_grad,
        down_grad,
    )


def solution(mesh):
    return jax.shard_map(
        per_device,
        mesh=mesh,
        in_specs=(
            P(("expert", "rows"), None, None),
            P(("expert", "rows"), None),
            P(),
            P(),
            P(),
            P(),
            P(None, "expert"),
            P("expert", None, None),
            P("expert", None, None),
            P(("expert", "rows"), None, None),
        ),
        out_specs=(
            P(("expert", "rows"), None, None),
            P(("expert", "rows"), None, None),
            P(),
            P(),
            P(),
            P(),
            P(None, "expert"),
            P("expert", None, None),
            P("expert", None, None),
        ),
        check_vma=False,
    )
```

```python
import jax
import jax.numpy as jnp
from jax import lax
from jax.experimental import pallas as pl
from jax.experimental.pallas import tpu as pltpu
from jax.sharding import PartitionSpec as P

HEADS = 6
IMG_ROW = 8
LANES = 128
TILE = 256

epsilon = 1e-06
masked_fill = -1e30
score_bound = 64.0
log2_e = 1.4426950408889634
low = jnp.bfloat16
full = jnp.float32
whole_vmem = pl.BlockSpec(memory_space=pltpu.VMEM)
anywhere = pl.BlockSpec(memory_space=pl.ANY)
both_axes = ("expert", "rows")


def dot(left, right, left_dim=1, right_dim=0):
    return lax.dot_general(
        left, right, (((left_dim,), (right_dim,)), ((), ())), preferred_element_type=full
    )


def shape_of(shape, dtype):
    return jax.ShapeDtypeStruct(shape, dtype)


def kept(shape, dtype):
    return pltpu.HBM(shape, dtype)


def keep(*arrays):
    return [pltpu.with_memory_space_constraint(array, pltpu.HBM) for array in arrays]


def params(mib):
    return pltpu.CompilerParams(vmem_limit_bytes=mib << 20)


def cost(microseconds):
    return pl.CostEstimate(
        flops=0, transcendentals=0, bytes_accessed=int(microseconds * 3.6e6)
    )


def norm_parts(values):
    centred = values - jnp.mean(values, axis=-1, keepdims=True)
    factor = lax.rsqrt(jnp.mean(centred * centred, axis=-1, keepdims=True) + epsilon)
    return centred * factor, factor


def norm_back(grad_norm, normed, factor, gain):
    scaled = grad_norm * gain
    return factor * (
        scaled
        - jnp.mean(scaled, axis=-1, keepdims=True)
        - normed * jnp.mean(scaled * normed, axis=-1, keepdims=True)
    )


def member_of(ids):
    images = lax.broadcasted_iota(jnp.int32, (IMG_ROW, ids.shape[1]), 0)
    return images == ids


def gelu_parts(pre):
    cdf = 0.5 * (1.0 + lax.erf(pre * 0.7071067811865476))
    pdf = 0.3989422804014327 * jnp.exp(-0.5 * pre * pre)
    return cdf, pdf


def copies_of(sources, targets, semaphores):
    return [
        pltpu.make_async_copy(source, target, semaphores.at[index])
        for index, (source, target) in enumerate(zip(sources, targets, strict=True))
    ]


def attend_kernel(*refs):
    sources, refs = refs[:6], refs[6:]
    outs, second_ref, same, refs = refs[:8], refs[8], refs[9], refs[10:]
    probs_out, saved, refs = outs[0], refs[:7], refs[7:]
    queries_ref, keys_ref, value_rows_ref, first_ref = saved[:4]
    attn_ref, inverse_ref, resid_ref = saved[4:]
    probs_ref, key_rows, values, mask_rows, bound, semaphores, probs_semaphores = refs[:7]
    x_ref, gain_ref, weight_ref, ids_ref, proj_ref, second_gain_ref = refs[7:13]
    loads = copies_of(sources, refs[7:13], refs[13])
    for load in loads:
        load.start()
    length, width = x_ref.shape
    pairs = width // LANES
    half = LANES // 2
    saves = copies_of(saved, outs[1:], semaphores)

    def save_probs(head):
        return pltpu.make_async_copy(
            probs_ref.at[head], probs_out.at[head], probs_semaphores.at[head]
        )

    for load in loads[:2]:
        load.wait()
    normed, _ = norm_parts(x_ref[...].astype(full))
    first_in = (normed * gain_ref[...].reshape(1, width)).astype(low)
    loads[2].wait()
    turned = dot(weight_ref[...], first_in, 0, 1)
    scaled = (turned[:width] * (half**-0.5 * log2_e)).astype(low)
    turned = turned[width:].astype(low)
    queries_ref[...] = scaled.reshape(pairs, LANES, length)
    keys_ref[...] = turned[:width].reshape(pairs, LANES, length)
    values[...] = turned[width:].reshape(pairs, LANES, length)
    norms = []
    for part in (scaled, turned[:width]):
        square = part.astype(full).reshape(2 * pairs, half, length)
        norms.append(jnp.max(jnp.sum(square * square, axis=1), axis=1, keepdims=True))
    bound[0] = jnp.max(norms[0] * norms[1])
    for index in range(pairs):
        key_rows[index] = keys_ref[index].T
        value_rows_ref[index] = values[index].T
    first_ref[...] = first_in.T
    for save in saves[:4]:
        save.start()
    loads[3].wait()
    images = lax.broadcasted_iota(jnp.int32, (LANES, length), 0)
    matching = images == ids_ref[...]
    same[...] = matching.astype(full).astype(low)
    other = jnp.where(jnp.logical_or(matching, images >= IMG_ROW), 0.0, masked_fill)
    mask_rows[...] = other.T.astype(low)

    def attend_pair(pair, raise_scores):
        keys = jnp.concatenate([key_rows[pair], mask_rows[...]], axis=1)
        none = jnp.zeros((half, TILE), low)
        ones = jnp.ones((16, length), low)
        for head in range(2):
            rows = slice(head * half, (head + 1) * half)
            for start in range(0, length, TILE):
                span = slice(start, start + TILE)
                query = queries_ref[pair, rows, span]
                parts = [query, none] if head == 0 else [none, query]
                scores = dot(keys, jnp.concatenate(parts + [same[:, span]], axis=0))
                probs_ref[2 * pair + head, :, span] = raise_scores(scores).astype(low)
            save_probs(2 * pair + head).start()
        for head in range(2):
            rows = slice(head * half, (head + 1) * half)
            value = jnp.concatenate([values[pair, rows, :], ones], axis=0)
            mixed = dot(value, probs_ref[2 * pair + head])
            inverse = 1.0 / mixed[half : half + 1]
            inverse_ref[pair, head : head + 1] = inverse
            attn_ref[pair, rows] = (mixed[:half] * inverse).astype(low)

    small = bound[0] < score_bound * score_bound

    def one_pair(pair, carry):
        @pl.when(small)
        def _():
            attend_pair(pair, jnp.exp2)

        @pl.when(jnp.logical_not(small))
        def _():
            attend_pair(
                pair,
                lambda scores: jnp.exp2(scores - jnp.max(scores, axis=0, keepdims=True)),
            )

        return carry

    lax.fori_loop(0, pairs, one_pair, 0)
    for save in saves[4:6]:
        save.start()
    for load in loads[4:]:
        load.wait()
    attn = attn_ref[...].reshape(width, length)
    resid = x_ref[...].astype(full) + dot(attn, proj_ref[...], 0, 0)
    resid_ref[...] = resid
    saves[6].start()
    normed, _ = norm_parts(resid)
    second_ref[...] = (normed * second_gain_ref[...].reshape(1, width)).astype(low)
    for save in saves:
        save.wait()
    for head in range(2 * pairs):
        save_probs(head).wait()


def attend(patches, ids, gain, weight, proj, second_gain):
    inputs = patches, gain, weight, ids, proj, second_gain
    length, width = patches.shape
    pairs = width // LANES
    stack = (pairs, LANES, length)
    rows = (pairs, length, LANES)
    probs = (2 * pairs, length, length)
    saved = [
        (stack, low),
        (stack, low),
        (rows, low),
        ((width, length), low),
        (stack, low),
        ((pairs, 2, length), full),
        ((length, width), full),
    ]
    return pl.pallas_call(
        attend_kernel,
        in_specs=[anywhere] * 6,
        out_specs=[anywhere] * 8 + [whole_vmem] * 2,
        out_shape=[kept(probs, low)]
        + [kept(*entry) for entry in saved]
        + [shape_of((length, width), low), shape_of((LANES, length), low)],
        scratch_shapes=[pltpu.VMEM(*entry) for entry in saved]
        + [
            pltpu.VMEM(probs, low),
            pltpu.VMEM(rows, low),
            pltpu.VMEM(stack, low),
            pltpu.VMEM((length, LANES), low),
            pltpu.SMEM((1,), full),
            pltpu.SemaphoreType.DMA((7,)),
            pltpu.SemaphoreType.DMA((2 * pairs,)),
        ]
        + [pltpu.VMEM(array.shape, array.dtype) for array in inputs]
        + [pltpu.SemaphoreType.DMA((6,))],
        compiler_params=params(30),
        cost_estimate=cost(12),
        name="attend",
    )(*keep(*inputs))


def slot_rows(slots):
    experts = slots.shape[0]
    row = lax.broadcasted_iota(jnp.int32, (experts * IMG_ROW, experts), 0) // IMG_ROW
    column = lax.broadcasted_iota(jnp.int32, (experts * IMG_ROW, experts), 1)
    return dot((row == column).astype(full).astype(low), slots).astype(low)


def route_kernel(
    second_ref, slots_ref, same_ref, cotangent_source,
    second_out, dispatch_out, combine_out, send_ref,
    cotangent_ref, dispatch_ref, combine_ref, semaphores,
):
    length, width = second_ref.shape
    experts = slots_ref.shape[0]
    shape = (experts, IMG_ROW, length)
    load, *saves = copies_of(
        [cotangent_source, second_ref, dispatch_ref, combine_ref],
        [cotangent_ref, second_out, dispatch_out, combine_out],
        semaphores,
    )
    load.start()
    saves[0].start()
    second_in = second_ref[...]
    logits = dot(slot_rows(slots_ref[...]), second_in, 1, 1).reshape(shape)
    present = same_ref[...].astype(full)[:IMG_ROW]
    member = present > 0.0
    masked = jnp.where(member[None], logits, masked_fill)
    top = jnp.max(masked, axis=2, keepdims=True)
    raised = jnp.where(member[None], jnp.exp(masked - top), 0.0)
    absent = 1.0 - jnp.max(present, axis=1, keepdims=True)
    total = jnp.sum(raised, axis=2, keepdims=True) + absent[None]
    dispatch = raised * (1.0 / total)
    dispatch_ref[...] = dispatch
    saves[1].start()
    raised = jnp.exp(logits - jnp.max(logits, axis=0, keepdims=True))
    combine = raised * (1.0 / jnp.sum(raised, axis=0, keepdims=True))
    combine_ref[...] = combine
    saves[2].start()
    dispatch_low = dispatch.astype(low).reshape(-1, length)
    combine_low = jnp.where(member[None], combine, 0.0).astype(low).reshape(-1, length)
    block = (send_ref.shape[0], send_ref.shape[2], width)
    send_ref[:, 0] = dot(dispatch_low, second_in).astype(low).reshape(block)
    load.wait()
    send_ref[:, 1] = dot(combine_low, cotangent_ref[...]).astype(low).reshape(block)
    for save in saves:
        save.wait()


def route(second_in, slots, same, cotangent, groups):
    length, width = second_in.shape
    experts = slots.shape[0]
    own = experts // groups * IMG_ROW
    shape = (experts, IMG_ROW, length)
    return pl.pallas_call(
        route_kernel,
        in_specs=[whole_vmem] * 3 + [anywhere],
        out_specs=[anywhere] * 3 + [whole_vmem],
        out_shape=[kept((length, width), low)]
        + [kept(shape, full)] * 2
        + [shape_of((groups, 2, own, width), low)],
        scratch_shapes=[pltpu.VMEM((length, width), low)]
        + [pltpu.VMEM(shape, full)] * 2
        + [pltpu.SemaphoreType.DMA((4,))],
        compiler_params=params(14 + experts // 4),
        cost_estimate=cost(3),
        name="route",
    )(second_in, slots, same, *keep(cotangent))


def own_rows(received, expert):
    groups, _, width = received.shape
    rows = received[:, expert * IMG_ROW : (expert + 1) * IMG_ROW]
    return rows.reshape(groups * IMG_ROW, width).astype(low)


def expert_kernel(received_ref, up_ref, down_source, back_ref, down_ref, stage, semaphores):
    groups, _, own, width = received_ref.shape
    experts = own // IMG_ROW
    loads = copies_of(
        [down_source.at[index] for index in range(experts)],
        [down_ref.at[index] for index in range(experts)],
        semaphores,
    )
    for load in loads:
        load.start()
    slots = received_ref[:, 0].astype(full)
    grads = received_ref[:, 1].astype(full)
    for index in range(experts):
        up = up_ref[index]
        pre = dot(own_rows(slots, index), up)
        cdf, pdf = gelu_parts(pre)
        loads[index].wait()
        down = down_ref[index]
        out = dot((pre * cdf).astype(low), down)
        grad_hidden = dot(own_rows(grads, index), down, 1, 1)
        grad_pre = (grad_hidden * (cdf + pre * pdf)).astype(low)
        grad_slots = dot(grad_pre, up, 1, 1)
        rows = slice(index * IMG_ROW, (index + 1) * IMG_ROW)
        stage[0, :, rows] = out.reshape(groups, IMG_ROW, width)
        stage[1, :, rows] = grad_slots.reshape(groups, IMG_ROW, width)
    back_ref[:, 0] = stage[0].astype(low)
    back_ref[:, 1] = stage[1].astype(low)


def run_experts(received, up, down):
    groups, _, own, width = received.shape
    experts, _, hidden = up.shape
    return pl.pallas_call(
        expert_kernel,
        in_specs=[whole_vmem, whole_vmem, anywhere],
        out_specs=whole_vmem,
        out_shape=shape_of(received.shape, low),
        scratch_shapes=[
            pltpu.VMEM(down.shape, low),
            pltpu.VMEM((2, groups, own, width), full),
            pltpu.SemaphoreType.DMA((experts,)),
        ],
        compiler_params=params(12 + groups // 2),
        cost_estimate=cost(3),
        name="run_experts",
    )(received, up, *keep(down))


def backward_kernel(back_ref, *refs):
    sources, probs_source, refs = refs[:15], refs[15], refs[16:]
    (output_out, grad_resid_out, grads_out, sums_ref), refs = refs[:4], refs[4:]
    targets, refs = refs[:15], refs[15:]
    probs_ref, output_ref, grad_resid_ref, grads_ref, grad_attn, delta, grad_scores = refs[:7]
    turned_scores, turned_probs, semaphores, probs_semaphores, saves_semaphores = refs[7:]
    loads = copies_of(sources, targets, semaphores)
    ids_ref, cotangent_ref, combine_ref, second_ref, dispatch_ref, slots_ref = targets[:6]
    resid_ref, gain_ref, attn_ref, proj_ref, inverse_ref = targets[6:11]
    values_ref, keys_ref, queries_ref, first_ref = targets[11:]
    pairs = resid_ref.shape[1] // LANES

    def load_probs(pair):
        return pltpu.make_async_copy(
            probs_source.at[pl.ds(2 * pair, 2)],
            probs_ref.at[pl.ds(2 * pair, 2)],
            probs_semaphores.at[pair],
        )

    def save_grads(pair):
        return pltpu.make_async_copy(
            grads_ref.at[pair], grads_out.at[pair], saves_semaphores.at[2 + pair]
        )

    saves = copies_of(
        [output_ref, grad_resid_ref], [output_out, grad_resid_out], saves_semaphores
    )
    for load in loads[:11]:
        load.start()
    for load in loads[:6]:
        load.wait()
    for load in loads[11:]:
        load.start()
    load_probs(0).start()
    length, width = resid_ref.shape
    half = LANES // 2
    experts = slots_ref.shape[0]
    count = experts * IMG_ROW
    shape = (experts, IMG_ROW, length)
    slot_out = back_ref[:, 0].reshape(count, width)
    grad_slots = back_ref[:, 1].reshape(count, width)
    cotangent = cotangent_ref[...]
    second_in = second_ref[...]
    combine = combine_ref[...]
    dispatch = dispatch_ref[...]
    member = member_of(ids_ref[...])
    grad_combine = dot(slot_out, cotangent, 1, 1).reshape(shape)
    grad_own = jnp.sum(jnp.where(member[None], grad_combine, 0.0), axis=1, keepdims=True)
    inner = jnp.sum(combine * grad_own, axis=0, keepdims=True)
    grad_logits = combine * (grad_own - inner)
    grad_dispatch = dot(grad_slots, second_in, 1, 1).reshape(shape)
    weighted = jnp.sum(dispatch * grad_dispatch, axis=2, keepdims=True)
    routed = jnp.sum(dispatch * (grad_dispatch - weighted), axis=1, keepdims=True)
    grad_low = (grad_logits + routed).astype(low).reshape(count, length)
    row = lax.broadcasted_iota(jnp.int32, (experts, count), 0) * IMG_ROW
    column = lax.broadcasted_iota(jnp.int32, (experts, count), 1)
    grad_low = dot((row == column).astype(full).astype(low), grad_low).astype(low)
    slot_grad = dot(grad_low, second_in)
    mixing = jnp.concatenate([dispatch.astype(low).reshape(count, length), grad_low], axis=0)
    mixed = jnp.concatenate([grad_slots, slots_ref[...]], axis=0)
    grad_second = dot(mixing, mixed, 0, 0)
    for load in loads[6:11]:
        load.wait()
    resid = resid_ref[...]
    combine_low = jnp.where(member[None], combine, 0.0).astype(low).reshape(count, length)
    output_ref[...] = (resid + dot(combine_low, slot_out, 0, 0)).astype(low)
    saves[0].start()
    normed, factor = norm_parts(resid)
    second_grad = jnp.sum(grad_second * normed, axis=0, keepdims=True)
    gain = gain_ref[...].reshape(1, width)
    grad_resid = cotangent.astype(full) + norm_back(grad_second, normed, factor, gain)
    grad_resid_ref[...] = grad_resid
    saves[1].start()
    grad_branch = grad_resid.astype(low)
    attn = attn_ref[...]
    proj_grad = dot(attn.reshape(width, length), grad_branch).astype(low)
    scaled = dot(proj_ref[...], grad_branch, 1, 1).reshape(pairs, 2, half, length)
    scaled = (scaled * inverse_ref[...][:, :, None, :]).astype(low)
    product = scaled.astype(full) * attn.reshape(scaled.shape).astype(full)
    delta[...] = jnp.sum(product, axis=2)
    grad_attn[...] = scaled.reshape(grad_attn.shape)
    slot_low = slot_grad.astype(low)
    second_low = jnp.broadcast_to(second_grad, (16, width)).astype(low)
    early = pairs * (width + experts + 16)
    for index in range(pairs):
        lanes = slice(index * LANES, (index + 1) * LANES)
        sums_ref[index * width : (index + 1) * width] = proj_grad[:, lanes]
        base = width * pairs + index * experts
        sums_ref[base : base + experts] = slot_low[:, lanes]
        base = (width + experts) * pairs + index * 16
        sums_ref[base : base + 16] = second_low[:, lanes]
    used = early + pairs * 3 * width
    if used < sums_ref.shape[0]:
        sums_ref[used:] = jnp.zeros((sums_ref.shape[0] - used, LANES), low)

    for load in loads[11:]:
        load.wait()
    factor = half**-0.5
    none = jnp.zeros((half, TILE), low)

    def one_pair(pair, carry):
        load_probs(pair).wait()

        @pl.when(pair < pairs - 1)
        def _():
            load_probs(pair + 1).start()

        heads = [slice(head * half, (head + 1) * half) for head in range(2)]
        for head, rows in enumerate(heads):
            for start in range(0, length, TILE):
                span = slice(start, start + TILE)
                grad = grad_attn[pair, rows, span]
                parts = [grad, none] if head == 0 else [none, grad]
                grad_probs = dot(values_ref[pair], jnp.concatenate(parts, axis=0))
                grad_probs = grad_probs - delta[pair, head : head + 1, span]
                probs = probs_ref[2 * pair + head, :, span].astype(full)
                scores = (probs * grad_probs).astype(low)
                grad_scores[head, :, span] = scores
                turned_scores[head, span, :] = scores.T
            turned_probs[head] = probs_ref[2 * pair + head].T
        for head, rows in enumerate(heads):
            grads_ref[pair, 1, rows, :] = (
                dot(queries_ref[pair, rows, :], turned_scores[head]) * (1.0 / log2_e)
            ).astype(low)
        for head, rows in enumerate(heads):
            grads_ref[pair, 2, rows, :] = dot(
                grad_attn[pair, rows, :], turned_probs[head]
            ).astype(low)
        for head, rows in enumerate(heads):
            grads_ref[pair, 0, rows, :] = (
                dot(keys_ref[pair, rows, :], grad_scores[head]) * factor
            ).astype(low)
        sums = dot(first_ref[...], grads_ref[pair].reshape(3 * LANES, length), 1, 1).astype(low)

        for index in range(3):
            base = pl.multiple_of(early + (pair * 3 + index) * width, 16)
            sums_ref[pl.ds(base, width)] = sums[:, index * LANES : (index + 1) * LANES]
        save_grads(pair).start()
        return carry

    lax.fori_loop(0, pairs, one_pair, 0)
    for save in saves + [save_grads(pair) for pair in range(pairs)]:
        save.wait()


def padded(rows, parts):
    return -(-rows // (16 * parts)) * 16 * parts


def backward(back, arrays, probs):
    length, width = arrays[1].shape
    experts = arrays[5].shape[0]
    pairs = width // LANES
    rows = padded(pairs * (4 * width + experts + 16), 8)
    saved = [((length, width), low), ((length, width), full), ((pairs, 3, LANES, length), low)]
    return pl.pallas_call(
        backward_kernel,
        in_specs=[whole_vmem] + [anywhere] * (len(arrays) + 1),
        out_specs=[anywhere] * 3 + [whole_vmem],
        out_shape=[kept(*entry) for entry in saved] + [shape_of((rows, LANES), low)],
        scratch_shapes=[pltpu.VMEM(array.shape, array.dtype) for array in (*arrays, probs)]
        + [pltpu.VMEM(*entry) for entry in saved]
        + [
            pltpu.VMEM((pairs, LANES, length), low),
            pltpu.VMEM((pairs, 2, length), full),
            pltpu.VMEM((2, length, length), low),
            pltpu.VMEM((2, length, length), low),
            pltpu.VMEM((2, length, length), low),
            pltpu.SemaphoreType.DMA((len(arrays),)),
            pltpu.SemaphoreType.DMA((pairs,)),
            pltpu.SemaphoreType.DMA((2 + pairs,)),
        ],
        compiler_params=params(44 + experts // 8),
        cost_estimate=cost(20),
        name="backward",
    )(back, *keep(*arrays, probs))


def patch_back_kernel(x_ref, gain_ref, weight_ref, resid_ref, grads_ref, result_ref):
    length, width = x_ref.shape
    pairs = width // LANES
    grads = [grads_ref[pair, part] for part in range(3) for pair in range(pairs)]
    grad_first = dot(weight_ref[...], jnp.concatenate(grads, axis=0)).T
    normed, factor = norm_parts(x_ref[...].astype(full))
    gain = gain_ref[...].reshape(1, width)
    result_ref[...] = resid_ref[...] + norm_back(grad_first, normed, factor, gain)


def patch_back(patches, gain, weight, grad_resid, grads):
    return pl.pallas_call(
        patch_back_kernel,
        in_specs=[whole_vmem] * 5,
        out_specs=whole_vmem,
        out_shape=kept(patches.shape, full),
        compiler_params=params(20),
        cost_estimate=cost(3),
        name="patch_back",
    )(*keep(patches, gain, weight, grad_resid, grads))


def weights_kernel(copies, *refs):
    received = refs[:copies]
    up_ref, down_ref, up_grad_ref, down_grad_ref, slots, grads = refs[copies:]
    expert = pl.program_id(0)
    groups, _, own, width = received[0].shape
    count = groups * IMG_ROW
    for index in range(own // IMG_ROW):

        @pl.when(jnp.logical_and(expert == index, pl.program_id(1) == 0))
        def _():
            for copy, ref in enumerate(received):
                rows = slice(copy * count, (copy + 1) * count)
                slots[rows] = own_rows(ref[:, 0].astype(full), index)
                grads[rows] = own_rows(ref[:, 1].astype(full), index)

    pre = dot(slots[...], up_ref[0])
    cdf, pdf = gelu_parts(pre)
    down_grad_ref[0] = dot((pre * cdf).astype(low), grads[...], 0, 0)
    grad_hidden = dot(grads[...], down_ref[0], 1, 1)
    grad_pre = (grad_hidden * (cdf + pre * pdf)).astype(low)
    up_grad_ref[0] = dot(slots[...], grad_pre, 0, 0)


def weight_grads(received, up, down):
    groups, _, _, width = received[0].shape
    experts, _, hidden = up.shape
    copies = len(received)
    steps = 1 if copies * groups <= 64 else 3
    tile = hidden // steps
    up_spec = pl.BlockSpec((1, width, tile), lambda expert, step: (expert, 0, step))
    down_spec = pl.BlockSpec((1, tile, width), lambda expert, step: (expert, step, 0))
    rows = (copies * groups * IMG_ROW, width)

    def kernel(*refs):
        weights_kernel(copies, *refs)

    return pl.pallas_call(
        kernel,
        grid=(experts, steps),
        in_specs=[whole_vmem] * copies + [up_spec, down_spec],
        out_specs=[up_spec, down_spec],
        out_shape=[kept(up.shape, full), kept(down.shape, full)],
        scratch_shapes=[pltpu.VMEM(rows, low)] * 2,
        compiler_params=params(40),
        cost_estimate=cost(9),
        name="weight_grads",
    )(*keep(*received, up, down))


def position(place_ref):
    expert, row = place_ref[0], place_ref[1]
    return row % 2, row // 2 * 2 + expert % 2, expert // 2


def flipped(index, step):
    return jnp.bitwise_xor(index, step)


def rows_at(index, count):
    return pl.ds(pl.multiple_of(index * count, 16), count)


def small_call(kernel, out_shape, name, *arrays):
    return pl.pallas_call(
        kernel,
        in_specs=[pl.BlockSpec(memory_space=pltpu.SMEM)] + [whole_vmem] * (len(arrays) - 1),
        out_specs=jax.tree.map(lambda _: whole_vmem, out_shape),
        out_shape=out_shape,
        compiler_params=params(16),
        cost_estimate=cost(1),
        name=name,
    )(*arrays)


def core_kernel(place_ref, mine_ref, other_ref, *outs):
    core, quarter, _ = position(place_ref)
    count = outs[0].shape[0]
    for step, out in enumerate(outs):
        rows = rows_at(core * 4 + flipped(quarter, step), count)
        out[...] = (mine_ref[rows].astype(full) + other_ref[rows].astype(full)).astype(out.dtype)


def plane_kernel(place_ref, *refs):
    total = refs[0][...]
    for other in refs[1:-1]:
        total = total + other[...].astype(full)
    refs[-1][...] = total.astype(low)


def line_kernel(place_ref, mine_ref, other_ref, out_ref):
    out_ref[...] = (mine_ref[...].astype(full) + other_ref[...].astype(full)).astype(low)


def finish_parts(place_ref, parts, whole):
    core, quarter, _ = position(place_ref)
    for index, part in enumerate(parts):
        half = flipped(core, index // 4)
        whole[rows_at(half * 4 + flipped(quarter, index % 4), part.shape[0])] = part[...]


def finish_kernel(
    total, place_ref, weight_ref, gain_ref, *refs
):
    parts = refs[:8]
    first_ref, qkv_ref, proj_ref, second_ref, slot_ref, sums = refs[8:]
    finish_parts(place_ref, parts, sums)
    width = weight_ref.shape[0]
    pairs = width // LANES
    own = slot_ref.shape[0]
    base = (width + total + 16) * pairs
    seconds = []
    for index in range(pairs):
        lanes = slice(index * LANES, (index + 1) * LANES)
        proj_ref[:, lanes] = sums[index * width : (index + 1) * width].astype(full)
        start = (width + total) * pairs + index * 16
        seconds.append(sums[start : start + 16].astype(full)[0:1])
        start = width * pairs + index * total
        row = lax.broadcasted_iota(jnp.int32, (own, total), 0) + place_ref[0] * own
        column = lax.broadcasted_iota(jnp.int32, (own, total), 1)
        chosen = (row == column).astype(full).astype(low)
        slot_ref[:, lanes] = dot(chosen, sums[start : start + total])
    second_ref[...] = jnp.concatenate(seconds, axis=1).reshape(width)
    first = jnp.zeros((width, LANES), full)
    for pair in range(pairs):
        for part in range(3):
            lanes = slice(part * width + pair * LANES, part * width + (pair + 1) * LANES)
            start = base + (pair * 3 + part) * width
            grad = sums[start : start + width].astype(full)
            qkv_ref[:, lanes] = grad
            first = first + grad * weight_ref[:, lanes].astype(full)
    row = jnp.sum(first.T, axis=0, keepdims=True)
    first_ref[...] = (row / gain_ref[...].reshape(1, width)).reshape(width)


def finish(place, parts, weight, gain, experts, own):
    width = weight.shape[0]

    def kernel(*refs):
        finish_kernel(experts, *refs)

    return pl.pallas_call(
        kernel,
        in_specs=[pl.BlockSpec(memory_space=pltpu.SMEM)] + [whole_vmem] * (2 + len(parts)),
        out_specs=[whole_vmem] * 5,
        out_shape=[
            shape_of((width,), full),
            shape_of(weight.shape, full),
            shape_of((width, width), full),
            shape_of((width,), full),
            shape_of((own, width), full),
        ],
        scratch_shapes=[pltpu.VMEM((sum(part.shape[0] for part in parts), LANES), low)],
        compiler_params=params(20),
        cost_estimate=cost(3),
        name="finish",
    )(place, weight, gain, *parts)


def per_device(
    patches,
    image_ids,
    first_gain,
    qkv_weight,
    proj_weight,
    second_gain,
    slot_params,
    up_weight,
    down_weight,
    cotangent,
):
    groups = lax.axis_size("expert")
    copies = lax.axis_size("rows")
    devices = groups * copies
    _, length, width = patches.shape
    own = slot_params.shape[1]
    experts = own * groups
    spread = jnp.broadcast_to(slot_params.T[None], (groups, own, width))
    slots = lax.all_to_all(spread, "expert", 0, 0, tiled=True).reshape(experts, width)
    patches = patches[0]
    cotangent = cotangent[0]
    probs, queries, keys, values, first_in, attn, inverse, resid, second_in, same = attend(
        patches, image_ids, first_gain, qkv_weight, proj_weight, second_gain
    )
    second_in, dispatch, combine, send = route(second_in, slots, same, cotangent, groups)
    received = lax.all_to_all(send, "expert", 0, 0, tiled=True)
    back = run_experts(received, up_weight, down_weight)
    back = lax.all_to_all(back, "expert", 0, 0, tiled=True)
    others = [
        lax.ppermute(received, "rows", [(index, index ^ step) for index in range(copies)])
        for step in range(1, copies)
    ]
    saved = [image_ids, cotangent, combine, second_in, dispatch, slots]
    saved += [resid, second_gain, attn, proj_weight, inverse, values, keys, queries, first_in]
    output, grad_resid, grads, terms = backward(back, saved, probs)
    place = jnp.stack([lax.axis_index("expert"), lax.axis_index("rows")]).astype(jnp.int32)
    layers = groups // 2

    def flip(array, expert, row):
        pairs = [
            (index, (index // copies ^ expert) * copies + (index % copies ^ row))
            for index in range(devices)
        ]
        return lax.ppermute(array, both_axes, pairs)

    terms, others = lax.optimization_barrier((terms, others))
    quarter = (terms.shape[0] // 8, LANES)
    mine, *sends = small_call(
        core_kernel, [shape_of(quarter, full)] + [shape_of(quarter, low)] * 3, "add_core",
        place, terms, flip(terms, 0, 1),
    )
    arrived = [flip(send, step % 2, step // 2 * 2) for step, send in enumerate(sends, 1)]
    grads, _ = lax.optimization_barrier((grads, mine))
    patch_grad = patch_back(patches, first_gain, qkv_weight, grad_resid, grads)
    arrived, patch_grad = lax.optimization_barrier((arrived, patch_grad))
    mine = small_call(plane_kernel, shape_of(quarter, low), "add_plane", place, mine, *arrived)
    step = 1
    while step < layers:
        arrived = flip(mine, step * 2, 0)
        if step * 2 >= layers:
            others, _ = lax.optimization_barrier((others, mine))
            up_grad, down_grad = weight_grads([received] + others, up_weight, down_weight)
            arrived, up_grad, down_grad = lax.optimization_barrier((arrived, up_grad, down_grad))
        mine = small_call(
            line_kernel, shape_of(quarter, low), f"add_line_{step}", place, mine, arrived
        )
        step *= 2
    arrived = [flip(mine, step % 2, step // 2 * 2) for step in range(1, 4)]
    parts = [mine] + arrived
    parts = parts + [flip(part, 0, 1) for part in parts]
    first_grad, qkv_grad, proj_grad, second_grad, slot_grad = finish(
        place, parts, qkv_weight, first_gain, experts, own
    )
    return (
        output[None],
        patch_grad[None],
        first_grad,
        qkv_grad,
        proj_grad,
        second_grad,
        slot_grad.T,
        up_grad,
        down_grad,
    )


def solution(mesh):
    return jax.shard_map(
        per_device,
        mesh=mesh,
        in_specs=(
            P(("expert", "rows"), None, None),
            P(("expert", "rows"), None),
            P(),
            P(),
            P(),
            P(),
            P(None, "expert"),
            P("expert", None, None),
            P("expert", None, None),
            P(("expert", "rows"), None, None),
        ),
        out_specs=(
            P(("expert", "rows"), None, None),
            P(("expert", "rows"), None, None),
            P(),
            P(),
            P(),
            P(),
            P(None, "expert"),
            P("expert", None, None),
            P("expert", None, None),
        ),
        check_vma=False,
    )
```

```python
import jax
import jax.numpy as jnp
from jax import lax
from jax.experimental import pallas as pl
from jax.experimental.pallas import tpu as pltpu
from jax.sharding import PartitionSpec as P

HEADS = 6
IMG_ROW = 8
LANES = 128
TILE = 256

epsilon = 1e-06
masked_fill = -1e30
score_bound = 44.0
low = jnp.bfloat16
full = jnp.float32
whole_vmem = pl.BlockSpec(memory_space=pltpu.VMEM)
anywhere = pl.BlockSpec(memory_space=pl.ANY)
both_axes = ("expert", "rows")


def dot(left, right, left_dim=1, right_dim=0):
    return lax.dot_general(
        left, right, (((left_dim,), (right_dim,)), ((), ())), preferred_element_type=full
    )


def shape_of(shape, dtype):
    return jax.ShapeDtypeStruct(shape, dtype)


def kept(shape, dtype):
    return pltpu.HBM(shape, dtype)


def keep(*arrays):
    return [pltpu.with_memory_space_constraint(array, pltpu.HBM) for array in arrays]


def params(mib):
    return pltpu.CompilerParams(vmem_limit_bytes=mib << 20)


def cost(microseconds):
    return pl.CostEstimate(
        flops=0, transcendentals=0, bytes_accessed=int(microseconds * 3.6e6)
    )


def norm_parts(values):
    centred = values - jnp.mean(values, axis=-1, keepdims=True)
    factor = lax.rsqrt(jnp.mean(centred * centred, axis=-1, keepdims=True) + epsilon)
    return centred * factor, factor


def norm_back(grad_norm, normed, factor, gain):
    scaled = grad_norm * gain
    return factor * (
        scaled
        - jnp.mean(scaled, axis=-1, keepdims=True)
        - normed * jnp.mean(scaled * normed, axis=-1, keepdims=True)
    )


def member_of(ids):
    images = lax.broadcasted_iota(jnp.int32, (IMG_ROW, ids.shape[1]), 0)
    return images == ids


def gelu_parts(pre):
    cdf = 0.5 * (1.0 + lax.erf(pre * 0.7071067811865476))
    pdf = 0.3989422804014327 * jnp.exp(-0.5 * pre * pre)
    return cdf, pdf


def copies_of(sources, targets, semaphores):
    return [
        pltpu.make_async_copy(source, target, semaphores.at[index])
        for index, (source, target) in enumerate(zip(sources, targets, strict=True))
    ]


def attend_kernel(*refs):
    sources, refs = refs[:6], refs[6:]
    outs, second_ref, same, refs = refs[:9], refs[9], refs[10], refs[11:]
    probs_out, saved, refs = outs[0], refs[:8], refs[8:]
    queries_ref, keys_ref, value_rows_ref, first_ref = saved[:4]
    attn_ref, rest_ref, inverse_ref, resid_ref = saved[4:]
    probs_ref, key_rows, values, mask_rows, bound, semaphores, probs_semaphores = refs[:7]
    x_ref, gain_ref, weight_ref, ids_ref, proj_ref, second_gain_ref = refs[7:13]
    loads = copies_of(sources, refs[7:13], refs[13])
    for load in loads:
        load.start()
    length, width = x_ref.shape
    pairs = width // LANES
    half = LANES // 2
    saves = copies_of(saved, outs[1:], semaphores)

    def save_probs(head):
        return pltpu.make_async_copy(
            probs_ref.at[head], probs_out.at[head], probs_semaphores.at[head]
        )

    for load in loads[:2]:
        load.wait()
    normed, _ = norm_parts(x_ref[...].astype(full))
    first_in = (normed * gain_ref[...].reshape(1, width)).astype(low)
    loads[2].wait()
    turned = dot(weight_ref[...], first_in, 0, 1)
    turned = turned.astype(low)
    scaled = turned[:width] * jnp.asarray(half**-0.5, low)
    turned = turned[width:]
    queries_ref[...] = scaled.reshape(pairs, LANES, length)
    keys_ref[...] = turned[:width].reshape(pairs, LANES, length)
    values[...] = turned[width:].reshape(pairs, LANES, length)
    norms = []
    for part in (scaled, turned[:width]):
        square = part.astype(full).reshape(2 * pairs, half, length)
        norms.append(jnp.max(jnp.sum(square * square, axis=1), axis=1, keepdims=True))
    bound[0] = jnp.max(norms[0] * norms[1])
    for index in range(pairs):
        key_rows[index] = keys_ref[index].T
        value_rows_ref[index] = values[index].T
    first_ref[...] = first_in.T
    for save in saves[:4]:
        save.start()
    loads[3].wait()
    images = lax.broadcasted_iota(jnp.int32, (LANES, length), 0)
    matching = images == ids_ref[...]
    same[...] = matching.astype(full).astype(low)
    other = jnp.where(jnp.logical_or(matching, images >= IMG_ROW), 0.0, masked_fill)
    mask_rows[...] = other.T.astype(low)

    def attend_pair(pair, raise_scores):
        keys = jnp.concatenate([key_rows[pair], mask_rows[...]], axis=1)
        none = jnp.zeros((half, TILE), low)
        ones = jnp.ones((16, length), low)
        for head in range(2):
            rows = slice(head * half, (head + 1) * half)
            for start in range(0, length, TILE):
                span = slice(start, start + TILE)
                query = queries_ref[pair, rows, span]
                parts = [query, none] if head == 0 else [none, query]
                scores = dot(keys, jnp.concatenate(parts + [same[:, span]], axis=0))
                probs_ref[2 * pair + head, :, span] = raise_scores(scores).astype(low)
            save_probs(2 * pair + head).start()
        for head in range(2):
            rows = slice(head * half, (head + 1) * half)
            value = jnp.concatenate([values[pair, rows, :], ones], axis=0)
            mixed = dot(value, probs_ref[2 * pair + head])
            inverse = 1.0 / mixed[half : half + 1]
            inverse_ref[pair, head : head + 1] = inverse
            mixed = mixed[:half] * inverse
            attn = mixed.astype(low)
            attn_ref[pair, rows] = attn
            rest_ref[pair, rows] = (mixed - attn.astype(full)).astype(low)

    small = bound[0] < score_bound * score_bound

    def one_pair(pair, carry):
        @pl.when(small)
        def _():
            attend_pair(pair, jnp.exp)

        @pl.when(jnp.logical_not(small))
        def _():
            attend_pair(
                pair,
                lambda scores: jnp.exp(scores - jnp.max(scores, axis=0, keepdims=True)),
            )

        return carry

    lax.fori_loop(0, pairs, one_pair, 0)
    for save in saves[4:7]:
        save.start()
    for load in loads[4:]:
        load.wait()
    attn = attn_ref[...].reshape(width, length)
    resid = x_ref[...].astype(full) + dot(attn, proj_ref[...], 0, 0)
    resid_ref[...] = resid
    saves[7].start()
    normed, _ = norm_parts(resid)
    second_ref[...] = (normed * second_gain_ref[...].reshape(1, width)).astype(low)
    for save in saves:
        save.wait()
    for head in range(2 * pairs):
        save_probs(head).wait()


def attend(patches, ids, gain, weight, proj, second_gain):
    inputs = patches, gain, weight, ids, proj, second_gain
    length, width = patches.shape
    pairs = width // LANES
    stack = (pairs, LANES, length)
    rows = (pairs, length, LANES)
    probs = (2 * pairs, length, length)
    saved = [
        (stack, low),
        (stack, low),
        (rows, low),
        ((width, length), low),
        (stack, low),
        (stack, low),
        ((pairs, 2, length), full),
        ((length, width), full),
    ]
    return pl.pallas_call(
        attend_kernel,
        in_specs=[anywhere] * 6,
        out_specs=[anywhere] * 9 + [whole_vmem] * 2,
        out_shape=[kept(probs, low)]
        + [kept(*entry) for entry in saved]
        + [shape_of((length, width), low), shape_of((LANES, length), low)],
        scratch_shapes=[pltpu.VMEM(*entry) for entry in saved]
        + [
            pltpu.VMEM(probs, low),
            pltpu.VMEM(rows, low),
            pltpu.VMEM(stack, low),
            pltpu.VMEM((length, LANES), low),
            pltpu.SMEM((1,), full),
            pltpu.SemaphoreType.DMA((8,)),
            pltpu.SemaphoreType.DMA((2 * pairs,)),
        ]
        + [pltpu.VMEM(array.shape, array.dtype) for array in inputs]
        + [pltpu.SemaphoreType.DMA((6,))],
        compiler_params=params(30),
        cost_estimate=cost(12),
        name="attend",
    )(*keep(*inputs))


def slot_rows(slots):
    experts = slots.shape[0]
    row = lax.broadcasted_iota(jnp.int32, (experts * IMG_ROW, experts), 0) // IMG_ROW
    column = lax.broadcasted_iota(jnp.int32, (experts * IMG_ROW, experts), 1)
    return dot((row == column).astype(full).astype(low), slots).astype(low)


def route_kernel(
    second_ref, slots_ref, same_ref, cotangent_source,
    second_out, dispatch_out, combine_out, send_ref,
    cotangent_ref, dispatch_ref, combine_ref, semaphores,
):
    length, width = second_ref.shape
    experts = slots_ref.shape[0]
    shape = (experts, IMG_ROW, length)
    load, *saves = copies_of(
        [cotangent_source, second_ref, dispatch_ref, combine_ref],
        [cotangent_ref, second_out, dispatch_out, combine_out],
        semaphores,
    )
    load.start()
    saves[0].start()
    second_in = second_ref[...]
    logits = dot(slot_rows(slots_ref[...]), second_in, 1, 1).reshape(shape)
    present = same_ref[...].astype(full)[:IMG_ROW]
    member = present > 0.0
    masked = jnp.where(member[None], logits, masked_fill)
    top = jnp.max(masked, axis=2, keepdims=True)
    raised = jnp.where(member[None], jnp.exp(masked - top), 0.0)
    absent = 1.0 - jnp.max(present, axis=1, keepdims=True)
    total = jnp.sum(raised, axis=2, keepdims=True) + absent[None]
    dispatch = raised * (1.0 / total)
    dispatch_ref[...] = dispatch
    saves[1].start()
    raised = jnp.exp(logits - jnp.max(logits, axis=0, keepdims=True))
    combine = raised * (1.0 / jnp.sum(raised, axis=0, keepdims=True))
    combine_ref[...] = combine
    saves[2].start()
    dispatch_low = dispatch.astype(low).reshape(-1, length)
    combine_low = jnp.where(member[None], combine, 0.0).astype(low).reshape(-1, length)
    block = (send_ref.shape[0], send_ref.shape[2], width)
    send_ref[:, 0] = dot(dispatch_low, second_in).astype(low).reshape(block)
    load.wait()
    send_ref[:, 1] = dot(combine_low, cotangent_ref[...]).astype(low).reshape(block)
    for save in saves:
        save.wait()


def route(second_in, slots, same, cotangent, groups):
    length, width = second_in.shape
    experts = slots.shape[0]
    own = experts // groups * IMG_ROW
    shape = (experts, IMG_ROW, length)
    return pl.pallas_call(
        route_kernel,
        in_specs=[whole_vmem] * 3 + [anywhere],
        out_specs=[anywhere] * 3 + [whole_vmem],
        out_shape=[kept((length, width), low)]
        + [kept(shape, full)] * 2
        + [shape_of((groups, 2, own, width), low)],
        scratch_shapes=[pltpu.VMEM((length, width), low)]
        + [pltpu.VMEM(shape, full)] * 2
        + [pltpu.SemaphoreType.DMA((4,))],
        compiler_params=params(14 + experts // 4),
        cost_estimate=cost(3),
        name="route",
    )(second_in, slots, same, *keep(cotangent))


def own_rows(received, expert):
    groups, _, width = received.shape
    rows = received[:, expert * IMG_ROW : (expert + 1) * IMG_ROW]
    return rows.reshape(groups * IMG_ROW, width).astype(low)


def expert_kernel(received_ref, up_ref, down_source, back_ref, down_ref, stage, semaphores):
    groups, _, own, width = received_ref.shape
    experts = own // IMG_ROW
    loads = copies_of(
        [down_source.at[index] for index in range(experts)],
        [down_ref.at[index] for index in range(experts)],
        semaphores,
    )
    for load in loads:
        load.start()
    slots = received_ref[:, 0].astype(full)
    grads = received_ref[:, 1].astype(full)
    for index in range(experts):
        up = up_ref[index]
        pre = dot(own_rows(slots, index), up)
        cdf, pdf = gelu_parts(pre)
        loads[index].wait()
        down = down_ref[index]
        out = dot((pre * cdf).astype(low), down)
        grad_hidden = dot(own_rows(grads, index), down, 1, 1)
        grad_pre = (grad_hidden * (cdf + pre * pdf)).astype(low)
        grad_slots = dot(grad_pre, up, 1, 1)
        rows = slice(index * IMG_ROW, (index + 1) * IMG_ROW)
        stage[0, :, rows] = out.reshape(groups, IMG_ROW, width)
        stage[1, :, rows] = grad_slots.reshape(groups, IMG_ROW, width)
    back_ref[:, 0] = stage[0].astype(low)
    back_ref[:, 1] = stage[1].astype(low)


def run_experts(received, up, down):
    groups, _, own, width = received.shape
    experts, _, hidden = up.shape
    return pl.pallas_call(
        expert_kernel,
        in_specs=[whole_vmem, whole_vmem, anywhere],
        out_specs=whole_vmem,
        out_shape=shape_of(received.shape, low),
        scratch_shapes=[
            pltpu.VMEM(down.shape, low),
            pltpu.VMEM((2, groups, own, width), full),
            pltpu.SemaphoreType.DMA((experts,)),
        ],
        compiler_params=params(12 + groups // 2),
        cost_estimate=cost(3),
        name="run_experts",
    )(received, up, *keep(down))


def backward_kernel(back_ref, *refs):
    sources, probs_source, refs = refs[:16], refs[16], refs[17:]
    (output_out, grad_resid_out, grads_out, sums_ref), refs = refs[:4], refs[4:]
    targets, refs = refs[:16], refs[16:]
    probs_ref, output_ref, grad_resid_ref, grads_ref, grad_attn, delta, grad_scores = refs[:7]
    turned_scores, turned_probs, semaphores, probs_semaphores, saves_semaphores = refs[7:]
    loads = copies_of(sources, targets, semaphores)
    ids_ref, cotangent_ref, combine_ref, second_ref, dispatch_ref, slots_ref = targets[:6]
    resid_ref, gain_ref, attn_ref, rest_ref, proj_ref, inverse_ref = targets[6:12]
    values_ref, keys_ref, queries_ref, first_ref = targets[12:]
    pairs = resid_ref.shape[1] // LANES

    def load_probs(pair):
        return pltpu.make_async_copy(
            probs_source.at[pl.ds(2 * pair, 2)],
            probs_ref.at[pl.ds(2 * pair, 2)],
            probs_semaphores.at[pair],
        )

    def save_grads(pair):
        return pltpu.make_async_copy(
            grads_ref.at[pair], grads_out.at[pair], saves_semaphores.at[2 + pair]
        )

    saves = copies_of(
        [output_ref, grad_resid_ref], [output_out, grad_resid_out], saves_semaphores
    )
    for load in loads[:12]:
        load.start()
    for load in loads[:6]:
        load.wait()
    for load in loads[12:]:
        load.start()
    load_probs(0).start()
    length, width = resid_ref.shape
    half = LANES // 2
    experts = slots_ref.shape[0]
    count = experts * IMG_ROW
    shape = (experts, IMG_ROW, length)
    slot_out = back_ref[:, 0].reshape(count, width)
    grad_slots = back_ref[:, 1].reshape(count, width)
    cotangent = cotangent_ref[...]
    second_in = second_ref[...]
    combine = combine_ref[...]
    dispatch = dispatch_ref[...]
    member = member_of(ids_ref[...])
    grad_combine = dot(slot_out, cotangent, 1, 1).reshape(shape)
    grad_own = jnp.sum(jnp.where(member[None], grad_combine, 0.0), axis=1, keepdims=True)
    inner = jnp.sum(combine * grad_own, axis=0, keepdims=True)
    grad_logits = combine * (grad_own - inner)
    grad_dispatch = dot(grad_slots, second_in, 1, 1).reshape(shape)
    weighted = jnp.sum(dispatch * grad_dispatch, axis=2, keepdims=True)
    routed = jnp.sum(dispatch * (grad_dispatch - weighted), axis=1, keepdims=True)
    grad_low = (grad_logits + routed).astype(low).reshape(count, length)
    row = lax.broadcasted_iota(jnp.int32, (experts, count), 0) * IMG_ROW
    column = lax.broadcasted_iota(jnp.int32, (experts, count), 1)
    grad_low = dot((row == column).astype(full).astype(low), grad_low).astype(low)
    slot_grad = dot(grad_low, second_in)
    mixing = jnp.concatenate([dispatch.astype(low).reshape(count, length), grad_low], axis=0)
    mixed = jnp.concatenate([grad_slots, slots_ref[...]], axis=0)
    grad_second = dot(mixing, mixed, 0, 0)
    for load in loads[6:12]:
        load.wait()
    resid = resid_ref[...]
    combine_low = jnp.where(member[None], combine, 0.0).astype(low).reshape(count, length)
    output_ref[...] = (resid + dot(combine_low, slot_out, 0, 0)).astype(low)
    saves[0].start()
    normed, factor = norm_parts(resid)
    second_grad = jnp.sum(grad_second * normed, axis=0, keepdims=True)
    gain = gain_ref[...].reshape(1, width)
    grad_resid = cotangent.astype(full) + norm_back(grad_second, normed, factor, gain)
    grad_resid_ref[...] = grad_resid
    saves[1].start()
    grad_branch = grad_resid.astype(low)
    attn = attn_ref[...]
    proj_grad = dot(attn.reshape(width, length), grad_branch).astype(low)
    scaled = dot(proj_ref[...], grad_branch, 1, 1).reshape(pairs, 2, half, length)
    scaled = (scaled * inverse_ref[...][:, :, None, :]).astype(low)
    exact = attn.astype(full) + rest_ref[...].astype(full)
    delta[...] = jnp.sum(scaled.astype(full) * exact.reshape(scaled.shape), axis=2)
    grad_attn[...] = scaled.reshape(grad_attn.shape)
    slot_low = slot_grad.astype(low)
    second_low = jnp.broadcast_to(second_grad, (16, width)).astype(low)
    early = pairs * (width + experts + 16)
    for index in range(pairs):
        lanes = slice(index * LANES, (index + 1) * LANES)
        sums_ref[index * width : (index + 1) * width] = proj_grad[:, lanes]
        base = width * pairs + index * experts
        sums_ref[base : base + experts] = slot_low[:, lanes]
        base = (width + experts) * pairs + index * 16
        sums_ref[base : base + 16] = second_low[:, lanes]
    used = early + pairs * 3 * width
    if used < sums_ref.shape[0]:
        sums_ref[used:] = jnp.zeros((sums_ref.shape[0] - used, LANES), low)

    for load in loads[12:]:
        load.wait()
    factor = half**-0.5
    none = jnp.zeros((half, TILE), low)

    def one_pair(pair, carry):
        load_probs(pair).wait()

        @pl.when(pair < pairs - 1)
        def _():
            load_probs(pair + 1).start()

        heads = [slice(head * half, (head + 1) * half) for head in range(2)]
        for head, rows in enumerate(heads):
            for start in range(0, length, TILE):
                span = slice(start, start + TILE)
                grad = grad_attn[pair, rows, span]
                parts = [grad, none] if head == 0 else [none, grad]
                grad_probs = dot(values_ref[pair], jnp.concatenate(parts, axis=0))
                grad_probs = grad_probs - delta[pair, head : head + 1, span]
                probs = probs_ref[2 * pair + head, :, span].astype(full)
                scores = (probs * grad_probs).astype(low)
                grad_scores[head, :, span] = scores
                turned_scores[head, span, :] = scores.T
            turned_probs[head] = probs_ref[2 * pair + head].T
        for head, rows in enumerate(heads):
            grads_ref[pair, 1, rows, :] = dot(
                queries_ref[pair, rows, :], turned_scores[head]
            ).astype(low)
        for head, rows in enumerate(heads):
            grads_ref[pair, 2, rows, :] = dot(
                grad_attn[pair, rows, :], turned_probs[head]
            ).astype(low)
        for head, rows in enumerate(heads):
            grads_ref[pair, 0, rows, :] = (
                dot(keys_ref[pair, rows, :], grad_scores[head]) * factor
            ).astype(low)
        sums = dot(first_ref[...], grads_ref[pair].reshape(3 * LANES, length), 1, 1).astype(low)

        for index in range(3):
            base = pl.multiple_of(early + (pair * 3 + index) * width, 16)
            sums_ref[pl.ds(base, width)] = sums[:, index * LANES : (index + 1) * LANES]
        save_grads(pair).start()
        return carry

    lax.fori_loop(0, pairs, one_pair, 0)
    for save in saves + [save_grads(pair) for pair in range(pairs)]:
        save.wait()


def padded(rows, parts):
    return -(-rows // (16 * parts)) * 16 * parts


def backward(back, arrays, probs):
    length, width = arrays[1].shape
    experts = arrays[5].shape[0]
    pairs = width // LANES
    rows = padded(pairs * (4 * width + experts + 16), 8)
    saved = [((length, width), low), ((length, width), full), ((pairs, 3, LANES, length), low)]
    return pl.pallas_call(
        backward_kernel,
        in_specs=[whole_vmem] + [anywhere] * (len(arrays) + 1),
        out_specs=[anywhere] * 3 + [whole_vmem],
        out_shape=[kept(*entry) for entry in saved] + [shape_of((rows, LANES), low)],
        scratch_shapes=[pltpu.VMEM(array.shape, array.dtype) for array in (*arrays, probs)]
        + [pltpu.VMEM(*entry) for entry in saved]
        + [
            pltpu.VMEM((pairs, LANES, length), low),
            pltpu.VMEM((pairs, 2, length), full),
            pltpu.VMEM((2, length, length), low),
            pltpu.VMEM((2, length, length), low),
            pltpu.VMEM((2, length, length), low),
            pltpu.SemaphoreType.DMA((len(arrays),)),
            pltpu.SemaphoreType.DMA((pairs,)),
            pltpu.SemaphoreType.DMA((2 + pairs,)),
        ],
        compiler_params=params(44 + experts // 8),
        cost_estimate=cost(20),
        name="backward",
    )(back, *keep(*arrays, probs))


def patch_back_kernel(x_ref, gain_ref, weight_ref, resid_ref, grads_ref, result_ref):
    length, width = x_ref.shape
    pairs = width // LANES
    grads = [grads_ref[pair, part] for part in range(3) for pair in range(pairs)]
    grad_first = dot(weight_ref[...], jnp.concatenate(grads, axis=0)).T
    normed, factor = norm_parts(x_ref[...].astype(full))
    gain = gain_ref[...].reshape(1, width)
    result_ref[...] = resid_ref[...] + norm_back(grad_first, normed, factor, gain)


def patch_back(patches, gain, weight, grad_resid, grads):
    return pl.pallas_call(
        patch_back_kernel,
        in_specs=[whole_vmem] * 5,
        out_specs=whole_vmem,
        out_shape=kept(patches.shape, full),
        compiler_params=params(20),
        cost_estimate=cost(3),
        name="patch_back",
    )(*keep(patches, gain, weight, grad_resid, grads))


def weights_kernel(copies, *refs):
    received = refs[:copies]
    up_ref, down_ref, up_grad_ref, down_grad_ref, slots, grads = refs[copies:]
    expert = pl.program_id(0)
    groups, _, own, width = received[0].shape
    count = groups * IMG_ROW
    for index in range(own // IMG_ROW):

        @pl.when(jnp.logical_and(expert == index, pl.program_id(1) == 0))
        def _():
            for copy, ref in enumerate(received):
                rows = slice(copy * count, (copy + 1) * count)
                slots[rows] = own_rows(ref[:, 0].astype(full), index)
                grads[rows] = own_rows(ref[:, 1].astype(full), index)

    pre = dot(slots[...], up_ref[0])
    cdf, pdf = gelu_parts(pre)
    down_grad_ref[0] = dot((pre * cdf).astype(low), grads[...], 0, 0)
    grad_hidden = dot(grads[...], down_ref[0], 1, 1)
    grad_pre = (grad_hidden * (cdf + pre * pdf)).astype(low)
    up_grad_ref[0] = dot(slots[...], grad_pre, 0, 0)


def weight_grads(received, up, down):
    groups, _, _, width = received[0].shape
    experts, _, hidden = up.shape
    copies = len(received)
    steps = 1 if copies * groups <= 64 else 3
    tile = hidden // steps
    up_spec = pl.BlockSpec((1, width, tile), lambda expert, step: (expert, 0, step))
    down_spec = pl.BlockSpec((1, tile, width), lambda expert, step: (expert, step, 0))
    rows = (copies * groups * IMG_ROW, width)

    def kernel(*refs):
        weights_kernel(copies, *refs)

    return pl.pallas_call(
        kernel,
        grid=(experts, steps),
        in_specs=[whole_vmem] * copies + [up_spec, down_spec],
        out_specs=[up_spec, down_spec],
        out_shape=[kept(up.shape, full), kept(down.shape, full)],
        scratch_shapes=[pltpu.VMEM(rows, low)] * 2,
        compiler_params=params(40),
        cost_estimate=cost(9),
        name="weight_grads",
    )(*keep(*received, up, down))


def position(place_ref):
    expert, row = place_ref[0], place_ref[1]
    return row % 2, row // 2 * 2 + expert % 2, expert // 2


def flipped(index, step):
    return jnp.bitwise_xor(index, step)


def rows_at(index, count):
    return pl.ds(pl.multiple_of(index * count, 16), count)


def small_call(kernel, out_shape, name, *arrays):
    return pl.pallas_call(
        kernel,
        in_specs=[pl.BlockSpec(memory_space=pltpu.SMEM)] + [whole_vmem] * (len(arrays) - 1),
        out_specs=jax.tree.map(lambda _: whole_vmem, out_shape),
        out_shape=out_shape,
        compiler_params=params(16),
        cost_estimate=cost(1),
        name=name,
    )(*arrays)


def core_kernel(place_ref, mine_ref, other_ref, *outs):
    core, quarter, _ = position(place_ref)
    count = outs[0].shape[0]
    for step, out in enumerate(outs):
        rows = rows_at(core * 4 + flipped(quarter, step), count)
        out[...] = (mine_ref[rows].astype(full) + other_ref[rows].astype(full)).astype(out.dtype)


def plane_kernel(place_ref, *refs):
    total = refs[0][...]
    for other in refs[1:-1]:
        total = total + other[...].astype(full)
    refs[-1][...] = total.astype(low)


def line_kernel(place_ref, mine_ref, other_ref, out_ref):
    out_ref[...] = (mine_ref[...].astype(full) + other_ref[...].astype(full)).astype(low)


def finish_parts(place_ref, parts, whole):
    core, quarter, _ = position(place_ref)
    for index, part in enumerate(parts):
        half = flipped(core, index // 4)
        whole[rows_at(half * 4 + flipped(quarter, index % 4), part.shape[0])] = part[...]


def finish_kernel(
    total, place_ref, weight_ref, gain_ref, *refs
):
    parts = refs[:8]
    first_ref, qkv_ref, proj_ref, second_ref, slot_ref, sums = refs[8:]
    finish_parts(place_ref, parts, sums)
    width = weight_ref.shape[0]
    pairs = width // LANES
    own = slot_ref.shape[0]
    base = (width + total + 16) * pairs
    seconds = []
    for index in range(pairs):
        lanes = slice(index * LANES, (index + 1) * LANES)
        proj_ref[:, lanes] = sums[index * width : (index + 1) * width].astype(full)
        start = (width + total) * pairs + index * 16
        seconds.append(sums[start : start + 16].astype(full)[0:1])
        start = width * pairs + index * total
        row = lax.broadcasted_iota(jnp.int32, (own, total), 0) + place_ref[0] * own
        column = lax.broadcasted_iota(jnp.int32, (own, total), 1)
        chosen = (row == column).astype(full).astype(low)
        slot_ref[:, lanes] = dot(chosen, sums[start : start + total])
    second_ref[...] = jnp.concatenate(seconds, axis=1).reshape(width)
    first = jnp.zeros((width, LANES), full)
    for pair in range(pairs):
        for part in range(3):
            lanes = slice(part * width + pair * LANES, part * width + (pair + 1) * LANES)
            start = base + (pair * 3 + part) * width
            grad = sums[start : start + width].astype(full)
            qkv_ref[:, lanes] = grad
            first = first + grad * weight_ref[:, lanes].astype(full)
    row = jnp.sum(first.T, axis=0, keepdims=True)
    first_ref[...] = (row / gain_ref[...].reshape(1, width)).reshape(width)


def finish(place, parts, weight, gain, experts, own):
    width = weight.shape[0]

    def kernel(*refs):
        finish_kernel(experts, *refs)

    return pl.pallas_call(
        kernel,
        in_specs=[pl.BlockSpec(memory_space=pltpu.SMEM)] + [whole_vmem] * (2 + len(parts)),
        out_specs=[whole_vmem] * 5,
        out_shape=[
            shape_of((width,), full),
            shape_of(weight.shape, full),
            shape_of((width, width), full),
            shape_of((width,), full),
            shape_of((own, width), full),
        ],
        scratch_shapes=[pltpu.VMEM((sum(part.shape[0] for part in parts), LANES), low)],
        compiler_params=params(20),
        cost_estimate=cost(3),
        name="finish",
    )(place, weight, gain, *parts)


def per_device(
    patches,
    image_ids,
    first_gain,
    qkv_weight,
    proj_weight,
    second_gain,
    slot_params,
    up_weight,
    down_weight,
    cotangent,
):
    groups = lax.axis_size("expert")
    copies = lax.axis_size("rows")
    devices = groups * copies
    _, length, width = patches.shape
    own = slot_params.shape[1]
    experts = own * groups
    spread = jnp.broadcast_to(slot_params.T[None], (groups, own, width))
    slots = lax.all_to_all(spread, "expert", 0, 0, tiled=True).reshape(experts, width)
    patches = patches[0]
    cotangent = cotangent[0]
    probs, queries, keys, values, first_in, attn, rest, inverse, resid, second_in, same = attend(
        patches, image_ids, first_gain, qkv_weight, proj_weight, second_gain
    )
    second_in, dispatch, combine, send = route(second_in, slots, same, cotangent, groups)
    received = lax.all_to_all(send, "expert", 0, 0, tiled=True)
    back = run_experts(received, up_weight, down_weight)
    back = lax.all_to_all(back, "expert", 0, 0, tiled=True)
    others = [
        lax.ppermute(received, "rows", [(index, index ^ step) for index in range(copies)])
        for step in range(1, copies)
    ]
    saved = [image_ids, cotangent, combine, second_in, dispatch, slots]
    saved += [resid, second_gain, attn, rest, proj_weight, inverse]
    saved += [values, keys, queries, first_in]
    output, grad_resid, grads, terms = backward(back, saved, probs)
    place = jnp.stack([lax.axis_index("expert"), lax.axis_index("rows")]).astype(jnp.int32)
    layers = groups // 2

    def flip(array, expert, row):
        pairs = [
            (index, (index // copies ^ expert) * copies + (index % copies ^ row))
            for index in range(devices)
        ]
        return lax.ppermute(array, both_axes, pairs)

    terms, others = lax.optimization_barrier((terms, others))
    quarter = (terms.shape[0] // 8, LANES)
    mine, *sends = small_call(
        core_kernel, [shape_of(quarter, full)] + [shape_of(quarter, low)] * 3, "add_core",
        place, terms, flip(terms, 0, 1),
    )
    arrived = [flip(send, step % 2, step // 2 * 2) for step, send in enumerate(sends, 1)]
    grads, _ = lax.optimization_barrier((grads, mine))
    patch_grad = patch_back(patches, first_gain, qkv_weight, grad_resid, grads)
    arrived, patch_grad = lax.optimization_barrier((arrived, patch_grad))
    mine = small_call(plane_kernel, shape_of(quarter, low), "add_plane", place, mine, *arrived)
    step = 1
    while step < layers:
        arrived = flip(mine, step * 2, 0)
        if step * 2 >= layers:
            others, _ = lax.optimization_barrier((others, mine))
            up_grad, down_grad = weight_grads([received] + others, up_weight, down_weight)
            arrived, up_grad, down_grad = lax.optimization_barrier((arrived, up_grad, down_grad))
        mine = small_call(
            line_kernel, shape_of(quarter, low), f"add_line_{step}", place, mine, arrived
        )
        step *= 2
    arrived = [flip(mine, step % 2, step // 2 * 2) for step in range(1, 4)]
    parts = [mine] + arrived
    parts = parts + [flip(part, 0, 1) for part in parts]
    first_grad, qkv_grad, proj_grad, second_grad, slot_grad = finish(
        place, parts, qkv_weight, first_gain, experts, own
    )
    return (
        output[None],
        patch_grad[None],
        first_grad,
        qkv_grad,
        proj_grad,
        second_grad,
        slot_grad.T,
        up_grad,
        down_grad,
    )


def solution(mesh):
    return jax.shard_map(
        per_device,
        mesh=mesh,
        in_specs=(
            P(("expert", "rows"), None, None),
            P(("expert", "rows"), None),
            P(),
            P(),
            P(),
            P(),
            P(None, "expert"),
            P("expert", None, None),
            P("expert", None, None),
            P(("expert", "rows"), None, None),
        ),
        out_specs=(
            P(("expert", "rows"), None, None),
            P(("expert", "rows"), None, None),
            P(),
            P(),
            P(),
            P(),
            P(None, "expert"),
            P("expert", None, None),
            P("expert", None, None),
        ),
        check_vma=False,
    )
```

```python
import jax
import jax.numpy as jnp
from jax import lax
from jax.experimental import pallas as pl
from jax.experimental.pallas import tpu as pltpu
from jax.sharding import PartitionSpec as P

HEADS = 6
IMG_ROW = 8
LANES = 128
TILE = 256

epsilon = 1e-06
masked_fill = -1e30
score_bound = 44.0
low = jnp.bfloat16
full = jnp.float32
whole_vmem = pl.BlockSpec(memory_space=pltpu.VMEM)
anywhere = pl.BlockSpec(memory_space=pl.ANY)
both_axes = ("expert", "rows")


def dot(left, right, left_dim=1, right_dim=0):
    return lax.dot_general(
        left, right, (((left_dim,), (right_dim,)), ((), ())), preferred_element_type=full
    )


def shape_of(shape, dtype):
    return jax.ShapeDtypeStruct(shape, dtype)


def kept(shape, dtype):
    return pltpu.HBM(shape, dtype)


def keep(*arrays):
    return [pltpu.with_memory_space_constraint(array, pltpu.HBM) for array in arrays]


def params(mib):
    return pltpu.CompilerParams(vmem_limit_bytes=mib << 20)


def cost(microseconds):
    return pl.CostEstimate(
        flops=0, transcendentals=0, bytes_accessed=int(microseconds * 3.6e6)
    )


def norm_parts(values):
    centred = values - jnp.mean(values, axis=-1, keepdims=True)
    factor = lax.rsqrt(jnp.mean(centred * centred, axis=-1, keepdims=True) + epsilon)
    return centred * factor, factor


def norm_back(grad_norm, normed, factor, gain):
    scaled = grad_norm * gain
    return factor * (
        scaled
        - jnp.mean(scaled, axis=-1, keepdims=True)
        - normed * jnp.mean(scaled * normed, axis=-1, keepdims=True)
    )


def member_of(ids):
    images = lax.broadcasted_iota(jnp.int32, (IMG_ROW, ids.shape[1]), 0)
    return images == ids


def gelu_parts(pre):
    cdf = 0.5 * (1.0 + lax.erf(pre * 0.7071067811865476))
    pdf = 0.3989422804014327 * jnp.exp(-0.5 * pre * pre)
    return cdf, pdf


def copies_of(sources, targets, semaphores):
    return [
        pltpu.make_async_copy(source, target, semaphores.at[index])
        for index, (source, target) in enumerate(zip(sources, targets, strict=True))
    ]


def attend_kernel(*refs):
    sources, refs = refs[:6], refs[6:]
    outs, second_ref, same, refs = refs[:9], refs[9], refs[10], refs[11:]
    probs_out, saved, refs = outs[0], refs[:8], refs[8:]
    queries_ref, keys_ref, value_rows_ref, first_ref = saved[:4]
    attn_ref, rest_ref, inverse_ref, resid_ref = saved[4:]
    probs_ref, key_rows, values, mask_rows, bound, semaphores, probs_semaphores = refs[:7]
    x_ref, gain_ref, weight_ref, ids_ref, proj_ref, second_gain_ref = refs[7:13]
    loads = copies_of(sources, refs[7:13], refs[13])
    for load in loads:
        load.start()
    length, width = x_ref.shape
    pairs = width // LANES
    half = LANES // 2
    saves = copies_of(saved, outs[1:], semaphores)

    def save_probs(head):
        return pltpu.make_async_copy(
            probs_ref.at[head], probs_out.at[head], probs_semaphores.at[head]
        )

    for load in loads[:2]:
        load.wait()
    gain = gain_ref[...].reshape(1, width)
    for start in range(0, length, length // 2):
        span = slice(start, start + length // 2)
        normed, _ = norm_parts(x_ref[span].astype(full))
        first_in = (normed * gain).astype(low)
        if start == 0:
            loads[2].wait()
            weight = weight_ref[...].T
        turned = dot(weight, first_in, 1, 1).astype(low).reshape(3, pairs, LANES, length // 2)
        queries_ref[:, :, span] = turned[0] * jnp.asarray(half**-0.5, low)
        keys_ref[:, :, span] = turned[1]
        values[:, :, span] = turned[2]
        first_ref[:, span] = first_in.T
    norms = []
    for part in (queries_ref, keys_ref):
        square = part[...].astype(full).reshape(2 * pairs, half, length)
        norms.append(jnp.max(jnp.sum(square * square, axis=1), axis=1, keepdims=True))
    bound[0] = jnp.max(norms[0] * norms[1])
    for index in range(pairs):
        key_rows[index] = keys_ref[index].T
        value_rows_ref[index] = values[index].T
    for save in saves[:4]:
        save.start()
    loads[3].wait()
    images = lax.broadcasted_iota(jnp.int32, (LANES, length), 0)
    matching = images == ids_ref[...]
    same[...] = matching.astype(full).astype(low)
    other = jnp.where(jnp.logical_or(matching, images >= IMG_ROW), 0.0, masked_fill)
    mask_rows[...] = other.T.astype(low)

    def attend_pair(pair, raise_scores):
        keys = jnp.concatenate([key_rows[pair], mask_rows[...]], axis=1)
        none = jnp.zeros((half, TILE), low)
        ones = jnp.ones((16, length), low)
        for head in range(2):
            rows = slice(head * half, (head + 1) * half)
            for start in range(0, length, TILE):
                span = slice(start, start + TILE)
                query = queries_ref[pair, rows, span]
                parts = [query, none] if head == 0 else [none, query]
                scores = dot(keys, jnp.concatenate(parts + [same[:, span]], axis=0))
                probs_ref[2 * pair + head, :, span] = raise_scores(scores).astype(low)
            save_probs(2 * pair + head).start()
        for head in range(2):
            rows = slice(head * half, (head + 1) * half)
            value = jnp.concatenate([values[pair, rows, :], ones], axis=0)
            mixed = dot(value, probs_ref[2 * pair + head])
            inverse = 1.0 / mixed[half : half + 1]
            inverse_ref[pair, head : head + 1] = inverse
            mixed = mixed[:half] * inverse
            attn = mixed.astype(low)
            attn_ref[pair, rows] = attn
            rest_ref[pair, rows] = (mixed - attn.astype(full)).astype(low)

    small = bound[0] < score_bound * score_bound

    def one_pair(pair, carry):
        @pl.when(small)
        def _():
            attend_pair(pair, jnp.exp)

        @pl.when(jnp.logical_not(small))
        def _():
            attend_pair(
                pair,
                lambda scores: jnp.exp(scores - jnp.max(scores, axis=0, keepdims=True)),
            )

        return carry

    lax.fori_loop(0, pairs, one_pair, 0)
    for save in saves[4:7]:
        save.start()
    for load in loads[4:]:
        load.wait()
    attn = attn_ref[...].reshape(width, length)
    resid = x_ref[...].astype(full) + dot(attn, proj_ref[...], 0, 0)
    resid_ref[...] = resid
    saves[7].start()
    normed, _ = norm_parts(resid)
    second_ref[...] = (normed * second_gain_ref[...].reshape(1, width)).astype(low)
    for save in saves:
        save.wait()
    for head in range(2 * pairs):
        save_probs(head).wait()


def attend(patches, ids, gain, weight, proj, second_gain):
    inputs = patches, gain, weight, ids, proj, second_gain
    length, width = patches.shape
    pairs = width // LANES
    stack = (pairs, LANES, length)
    rows = (pairs, length, LANES)
    probs = (2 * pairs, length, length)
    saved = [
        (stack, low),
        (stack, low),
        (rows, low),
        ((width, length), low),
        (stack, low),
        (stack, low),
        ((pairs, 2, length), full),
        ((length, width), full),
    ]
    return pl.pallas_call(
        attend_kernel,
        in_specs=[anywhere] * 6,
        out_specs=[anywhere] * 9 + [whole_vmem] * 2,
        out_shape=[kept(probs, low)]
        + [kept(*entry) for entry in saved]
        + [shape_of((length, width), low), shape_of((LANES, length), low)],
        scratch_shapes=[pltpu.VMEM(*entry) for entry in saved]
        + [
            pltpu.VMEM(probs, low),
            pltpu.VMEM(rows, low),
            pltpu.VMEM(stack, low),
            pltpu.VMEM((length, LANES), low),
            pltpu.SMEM((1,), full),
            pltpu.SemaphoreType.DMA((8,)),
            pltpu.SemaphoreType.DMA((2 * pairs,)),
        ]
        + [pltpu.VMEM(array.shape, array.dtype) for array in inputs]
        + [pltpu.SemaphoreType.DMA((6,))],
        compiler_params=params(30),
        cost_estimate=cost(12),
        name="attend",
    )(*keep(*inputs))


def slot_rows(slots):
    experts = slots.shape[0]
    row = lax.broadcasted_iota(jnp.int32, (experts * IMG_ROW, experts), 0) // IMG_ROW
    column = lax.broadcasted_iota(jnp.int32, (experts * IMG_ROW, experts), 1)
    return dot((row == column).astype(full).astype(low), slots).astype(low)


def route_kernel(
    second_ref, slots_ref, same_ref, cotangent_source,
    second_out, dispatch_out, combine_out, send_ref,
    cotangent_ref, dispatch_ref, combine_ref, semaphores,
):
    length, width = second_ref.shape
    experts = slots_ref.shape[0]
    shape = (experts, IMG_ROW, length)
    load, *saves = copies_of(
        [cotangent_source, second_ref, dispatch_ref, combine_ref],
        [cotangent_ref, second_out, dispatch_out, combine_out],
        semaphores,
    )
    load.start()
    saves[0].start()
    second_in = second_ref[...]
    logits = dot(slot_rows(slots_ref[...]), second_in, 1, 1).reshape(shape)
    present = same_ref[...].astype(full)[:IMG_ROW]
    member = present > 0.0
    masked = jnp.where(member[None], logits, masked_fill)
    top = jnp.max(masked, axis=2, keepdims=True)
    raised = jnp.where(member[None], jnp.exp(masked - top), 0.0)
    absent = 1.0 - jnp.max(present, axis=1, keepdims=True)
    total = jnp.sum(raised, axis=2, keepdims=True) + absent[None]
    dispatch = raised * (1.0 / total)
    dispatch_ref[...] = dispatch
    saves[1].start()
    raised = jnp.exp(logits - jnp.max(logits, axis=0, keepdims=True))
    combine = raised * (1.0 / jnp.sum(raised, axis=0, keepdims=True))
    combine_ref[...] = combine
    saves[2].start()
    dispatch_low = dispatch.astype(low).reshape(-1, length)
    combine_low = jnp.where(member[None], combine, 0.0).astype(low).reshape(-1, length)
    block = (send_ref.shape[0], send_ref.shape[2], width)
    send_ref[:, 0] = dot(dispatch_low, second_in).astype(low).reshape(block)
    load.wait()
    send_ref[:, 1] = dot(combine_low, cotangent_ref[...]).astype(low).reshape(block)
    for save in saves:
        save.wait()


def route(second_in, slots, same, cotangent, groups):
    length, width = second_in.shape
    experts = slots.shape[0]
    own = experts // groups * IMG_ROW
    shape = (experts, IMG_ROW, length)
    return pl.pallas_call(
        route_kernel,
        in_specs=[whole_vmem] * 3 + [anywhere],
        out_specs=[anywhere] * 3 + [whole_vmem],
        out_shape=[kept((length, width), low)]
        + [kept(shape, full)] * 2
        + [shape_of((groups, 2, own, width), low)],
        scratch_shapes=[pltpu.VMEM((length, width), low)]
        + [pltpu.VMEM(shape, full)] * 2
        + [pltpu.SemaphoreType.DMA((4,))],
        compiler_params=params(14 + experts // 4),
        cost_estimate=cost(3),
        name="route",
    )(second_in, slots, same, *keep(cotangent))


def own_rows(received, expert):
    groups, _, width = received.shape
    rows = received[:, expert * IMG_ROW : (expert + 1) * IMG_ROW]
    return rows.reshape(groups * IMG_ROW, width).astype(low)


def expert_kernel(received_ref, up_ref, down_source, back_ref, down_ref, stage, semaphores):
    groups, _, own, width = received_ref.shape
    experts = own // IMG_ROW
    loads = copies_of(
        [down_source.at[index] for index in range(experts)],
        [down_ref.at[index] for index in range(experts)],
        semaphores,
    )
    for load in loads:
        load.start()
    slots = received_ref[:, 0].astype(full)
    grads = received_ref[:, 1].astype(full)
    for index in range(experts):
        up = up_ref[index]
        pre = dot(own_rows(slots, index), up)
        cdf, pdf = gelu_parts(pre)
        loads[index].wait()
        down = down_ref[index]
        out = dot((pre * cdf).astype(low), down)
        grad_hidden = dot(own_rows(grads, index), down, 1, 1)
        grad_pre = (grad_hidden * (cdf + pre * pdf)).astype(low)
        grad_slots = dot(grad_pre, up, 1, 1)
        rows = slice(index * IMG_ROW, (index + 1) * IMG_ROW)
        stage[0, :, rows] = out.reshape(groups, IMG_ROW, width)
        stage[1, :, rows] = grad_slots.reshape(groups, IMG_ROW, width)
    back_ref[:, 0] = stage[0].astype(low)
    back_ref[:, 1] = stage[1].astype(low)


def run_experts(received, up, down):
    groups, _, own, width = received.shape
    experts, _, hidden = up.shape
    return pl.pallas_call(
        expert_kernel,
        in_specs=[whole_vmem, whole_vmem, anywhere],
        out_specs=whole_vmem,
        out_shape=shape_of(received.shape, low),
        scratch_shapes=[
            pltpu.VMEM(down.shape, low),
            pltpu.VMEM((2, groups, own, width), full),
            pltpu.SemaphoreType.DMA((experts,)),
        ],
        compiler_params=params(12 + groups // 2),
        cost_estimate=cost(3),
        name="run_experts",
    )(received, up, *keep(down))


def backward_kernel(back_ref, *refs):
    sources, probs_source, refs = refs[:16], refs[16], refs[17:]
    (output_out, grad_resid_out, grads_out, sums_ref, send_ref), refs = refs[:5], refs[5:]
    targets, refs = refs[:16], refs[16:]
    probs_ref, output_ref, grad_resid_ref, grads_ref, grad_attn, delta, grad_scores = refs[:7]
    turned_scores, turned_probs, semaphores, probs_semaphores, saves_semaphores = refs[7:]
    loads = copies_of(sources, targets, semaphores)
    ids_ref, cotangent_ref, combine_ref, second_ref, dispatch_ref, slots_ref = targets[:6]
    resid_ref, gain_ref, attn_ref, rest_ref, proj_ref, inverse_ref = targets[6:12]
    values_ref, keys_ref, queries_ref, first_ref = targets[12:]
    pairs = resid_ref.shape[1] // LANES

    def load_probs(pair):
        return pltpu.make_async_copy(
            probs_source.at[pl.ds(2 * pair, 2)],
            probs_ref.at[pl.ds(2 * pair, 2)],
            probs_semaphores.at[pair],
        )

    def save_grads(pair):
        return pltpu.make_async_copy(
            grads_ref.at[pair], grads_out.at[pair], saves_semaphores.at[2 + pair]
        )

    saves = copies_of(
        [output_ref, grad_resid_ref], [output_out, grad_resid_out], saves_semaphores
    )
    for load in loads[:12]:
        load.start()
    for load in loads[:6]:
        load.wait()
    for load in loads[12:]:
        load.start()
    load_probs(0).start()
    length, width = resid_ref.shape
    half = LANES // 2
    experts = slots_ref.shape[0]
    count = experts * IMG_ROW
    shape = (experts, IMG_ROW, length)
    slot_out = back_ref[:, 0].reshape(count, width)
    grad_slots = back_ref[:, 1].reshape(count, width)
    cotangent = cotangent_ref[...]
    second_in = second_ref[...]
    combine = combine_ref[...]
    dispatch = dispatch_ref[...]
    member = member_of(ids_ref[...])
    grad_combine = dot(slot_out, cotangent, 1, 1).reshape(shape)
    grad_own = jnp.sum(jnp.where(member[None], grad_combine, 0.0), axis=1, keepdims=True)
    inner = jnp.sum(combine * grad_own, axis=0, keepdims=True)
    grad_logits = combine * (grad_own - inner)
    grad_dispatch = dot(grad_slots, second_in, 1, 1).reshape(shape)
    weighted = jnp.sum(dispatch * grad_dispatch, axis=2, keepdims=True)
    routed = jnp.sum(dispatch * (grad_dispatch - weighted), axis=1, keepdims=True)
    grad_low = (grad_logits + routed).astype(low).reshape(count, length)
    row = lax.broadcasted_iota(jnp.int32, (experts, count), 0) * IMG_ROW
    column = lax.broadcasted_iota(jnp.int32, (experts, count), 1)
    grad_low = dot((row == column).astype(full).astype(low), grad_low).astype(low)
    slot_grad = dot(grad_low, second_in)
    mixing = jnp.concatenate([dispatch.astype(low).reshape(count, length), grad_low], axis=0)
    mixed = jnp.concatenate([grad_slots, slots_ref[...]], axis=0)
    grad_second = dot(mixing, mixed, 0, 0)
    for load in loads[6:12]:
        load.wait()
    resid = resid_ref[...]
    combine_low = jnp.where(member[None], combine, 0.0).astype(low).reshape(count, length)
    output_ref[...] = (resid + dot(combine_low, slot_out, 0, 0)).astype(low)
    saves[0].start()
    normed, factor = norm_parts(resid)
    second_grad = jnp.sum(grad_second * normed, axis=0, keepdims=True)
    gain = gain_ref[...].reshape(1, width)
    grad_resid = cotangent.astype(full) + norm_back(grad_second, normed, factor, gain)
    grad_resid_ref[...] = grad_resid
    saves[1].start()
    grad_branch = grad_resid.astype(low)
    attn = attn_ref[...]
    proj_grad = dot(attn.reshape(width, length), grad_branch).astype(low)
    scaled = dot(proj_ref[...], grad_branch, 1, 1).reshape(pairs, 2, half, length)
    scaled = (scaled * inverse_ref[...][:, :, None, :]).astype(low)
    exact = attn.astype(full) + rest_ref[...].astype(full)
    delta[...] = jnp.sum(scaled.astype(full) * exact.reshape(scaled.shape), axis=2)
    grad_attn[...] = scaled.reshape(grad_attn.shape)
    slot_low = slot_grad.astype(low)
    second_low = jnp.broadcast_to(second_grad, (16, width)).astype(low)
    early = pairs * (width + experts + 16)
    for index in range(pairs):
        lanes = slice(index * LANES, (index + 1) * LANES)
        sums_ref[index * width : (index + 1) * width] = proj_grad[:, lanes]
        base = width * pairs + index * experts
        sums_ref[base : base + experts] = slot_low[:, lanes]
        base = (width + experts) * pairs + index * 16
        sums_ref[base : base + 16] = second_low[:, lanes]
    used = early + pairs * 3 * width
    if used < sums_ref.shape[0]:
        sums_ref[used:] = jnp.zeros((sums_ref.shape[0] - used, LANES), low)

    for load in loads[12:]:
        load.wait()
    factor = half**-0.5
    none = jnp.zeros((half, TILE), low)

    def one_pair(pair, carry):
        load_probs(pair).wait()

        @pl.when(pair < pairs - 1)
        def _():
            load_probs(pair + 1).start()

        heads = [slice(head * half, (head + 1) * half) for head in range(2)]
        for head, rows in enumerate(heads):
            for start in range(0, length, TILE):
                span = slice(start, start + TILE)
                grad = grad_attn[pair, rows, span]
                parts = [grad, none] if head == 0 else [none, grad]
                grad_probs = dot(values_ref[pair], jnp.concatenate(parts, axis=0))
                grad_probs = grad_probs - delta[pair, head : head + 1, span]
                probs = probs_ref[2 * pair + head, :, span].astype(full)
                scores = (probs * grad_probs).astype(low)
                grad_scores[head, :, span] = scores
                turned_scores[head, span, :] = scores.T
            turned_probs[head] = probs_ref[2 * pair + head].T
        for head, rows in enumerate(heads):
            grads_ref[pair, 1, rows, :] = dot(
                queries_ref[pair, rows, :], turned_scores[head]
            ).astype(low)
        for head, rows in enumerate(heads):
            grads_ref[pair, 2, rows, :] = dot(
                grad_attn[pair, rows, :], turned_probs[head]
            ).astype(low)
        for head, rows in enumerate(heads):
            grads_ref[pair, 0, rows, :] = (
                dot(keys_ref[pair, rows, :], grad_scores[head]) * factor
            ).astype(low)
        sums = dot(first_ref[...], grads_ref[pair].reshape(3 * LANES, length), 1, 1).astype(low)

        for index in range(3):
            base = pl.multiple_of(early + (pair * 3 + index) * width, 16)
            sums_ref[pl.ds(base, width)] = sums[:, index * LANES : (index + 1) * LANES]
        save_grads(pair).start()
        return carry

    lax.fori_loop(0, pairs, one_pair, 0)
    core, _, _ = position()
    send_ref[...] = sums_ref[rows_at(1 - core, send_ref.shape[0])]
    for save in saves + [save_grads(pair) for pair in range(pairs)]:
        save.wait()


def padded(rows, parts):
    return -(-rows // (16 * parts)) * 16 * parts


def backward(back, arrays, probs):
    length, width = arrays[1].shape
    experts = arrays[5].shape[0]
    pairs = width // LANES
    rows = padded(pairs * (4 * width + experts + 16), 8)
    saved = [((length, width), low), ((length, width), full), ((pairs, 3, LANES, length), low)]
    return pl.pallas_call(
        backward_kernel,
        in_specs=[whole_vmem] + [anywhere] * (len(arrays) + 1),
        out_specs=[anywhere] * 3 + [whole_vmem] * 2,
        out_shape=[kept(*entry) for entry in saved]
        + [shape_of((count, LANES), low) for count in (rows, rows // 2)],
        scratch_shapes=[pltpu.VMEM(array.shape, array.dtype) for array in (*arrays, probs)]
        + [pltpu.VMEM(*entry) for entry in saved]
        + [
            pltpu.VMEM((pairs, LANES, length), low),
            pltpu.VMEM((pairs, 2, length), full),
            pltpu.VMEM((2, length, length), low),
            pltpu.VMEM((2, length, length), low),
            pltpu.VMEM((2, length, length), low),
            pltpu.SemaphoreType.DMA((len(arrays),)),
            pltpu.SemaphoreType.DMA((pairs,)),
            pltpu.SemaphoreType.DMA((2 + pairs,)),
        ],
        compiler_params=params(44 + experts // 8),
        cost_estimate=cost(20),
        name="backward",
    )(back, *keep(*arrays, probs))


def patch_back_kernel(x_ref, gain_ref, weight_ref, resid_ref, grads_ref, result_ref):
    length, width = x_ref.shape
    pairs = width // LANES
    grads = [grads_ref[pair, part] for part in range(3) for pair in range(pairs)]
    grad_first = dot(weight_ref[...], jnp.concatenate(grads, axis=0)).T
    normed, factor = norm_parts(x_ref[...].astype(full))
    gain = gain_ref[...].reshape(1, width)
    result_ref[...] = resid_ref[...] + norm_back(grad_first, normed, factor, gain)


def patch_back(patches, gain, weight, grad_resid, grads):
    return pl.pallas_call(
        patch_back_kernel,
        in_specs=[whole_vmem] * 5,
        out_specs=whole_vmem,
        out_shape=kept(patches.shape, full),
        compiler_params=params(20),
        cost_estimate=cost(3),
        name="patch_back",
    )(*keep(patches, gain, weight, grad_resid, grads))


def weights_kernel(copies, *refs):
    received = refs[:copies]
    up_ref, down_ref, up_grad_ref, down_grad_ref, slots, grads = refs[copies:]
    expert = pl.program_id(0)
    groups, _, own, width = received[0].shape
    count = groups * IMG_ROW
    for index in range(own // IMG_ROW):

        @pl.when(jnp.logical_and(expert == index, pl.program_id(1) == 0))
        def _():
            for copy, ref in enumerate(received):
                rows = slice(copy * count, (copy + 1) * count)
                slots[rows] = own_rows(ref[:, 0].astype(full), index)
                grads[rows] = own_rows(ref[:, 1].astype(full), index)

    pre = dot(slots[...], up_ref[0])
    cdf, pdf = gelu_parts(pre)
    down_grad_ref[0] = dot((pre * cdf).astype(low), grads[...], 0, 0)
    grad_hidden = dot(grads[...], down_ref[0], 1, 1)
    grad_pre = (grad_hidden * (cdf + pre * pdf)).astype(low)
    up_grad_ref[0] = dot(slots[...], grad_pre, 0, 0)


def weight_grads(received, up, down):
    groups, _, _, width = received[0].shape
    experts, _, hidden = up.shape
    copies = len(received)
    steps = 1 if copies * groups <= 64 else 3
    tile = hidden // steps
    up_spec = pl.BlockSpec((1, width, tile), lambda expert, step: (expert, 0, step))
    down_spec = pl.BlockSpec((1, tile, width), lambda expert, step: (expert, step, 0))
    rows = (copies * groups * IMG_ROW, width)

    def kernel(*refs):
        weights_kernel(copies, *refs)

    return pl.pallas_call(
        kernel,
        grid=(experts, steps),
        in_specs=[whole_vmem] * copies + [up_spec, down_spec],
        out_specs=[up_spec, down_spec],
        out_shape=[kept(up.shape, full), kept(down.shape, full)],
        scratch_shapes=[pltpu.VMEM(rows, low)] * 2,
        compiler_params=params(40),
        cost_estimate=cost(9),
        name="weight_grads",
    )(*keep(*received, up, down))


def position():
    expert, row = lax.axis_index("expert"), lax.axis_index("rows")
    return row % 2, row // 2 * 2 + expert % 2, expert // 2


def flipped(index, step):
    return jnp.bitwise_xor(index, step)


def rows_at(index, count):
    return pl.ds(pl.multiple_of(index * count, 16), count)


def small_call(kernel, out_shape, name, *arrays):
    return pl.pallas_call(
        kernel,
        in_specs=[whole_vmem] * len(arrays),
        out_specs=jax.tree.map(lambda _: whole_vmem, out_shape),
        out_shape=out_shape,
        compiler_params=params(16),
        cost_estimate=cost(1),
        name=name,
    )(*arrays)


def core_kernel(mine_ref, other_ref, *outs):
    core, quarter, _ = position()
    count = outs[0].shape[0]
    for step, out in enumerate(outs):
        mine = mine_ref[rows_at(core * 4 + flipped(quarter, step), count)].astype(full)
        other = other_ref[rows_at(flipped(quarter, step), count)].astype(full)
        out[...] = (mine + other).astype(out.dtype)


def plane_kernel(*refs):
    total = refs[0][...]
    for other in refs[1:-1]:
        total = total + other[...].astype(full)
    refs[-1][...] = total.astype(low)


def line_kernel(mine_ref, other_ref, out_ref):
    out_ref[...] = (mine_ref[...].astype(full) + other_ref[...].astype(full)).astype(low)


def finish_parts(parts, whole):
    core, quarter, _ = position()
    for index, part in enumerate(parts):
        half = flipped(core, index // 4)
        whole[rows_at(half * 4 + flipped(quarter, index % 4), part.shape[0])] = part[...]


def finish_kernel(
    total, weight_ref, gain_ref, *refs
):
    parts = refs[:8]
    first_ref, qkv_ref, proj_ref, second_ref, slot_ref, sums = refs[8:]
    finish_parts(parts, sums)
    width = weight_ref.shape[0]
    pairs = width // LANES
    own = slot_ref.shape[0]
    base = (width + total + 16) * pairs
    seconds = []
    for index in range(pairs):
        lanes = slice(index * LANES, (index + 1) * LANES)
        proj_ref[:, lanes] = sums[index * width : (index + 1) * width].astype(full)
        start = (width + total) * pairs + index * 16
        seconds.append(sums[start : start + 16].astype(full)[0:1])
        start = width * pairs + index * total
        row = lax.broadcasted_iota(jnp.int32, (own, total), 0) + lax.axis_index("expert") * own
        column = lax.broadcasted_iota(jnp.int32, (own, total), 1)
        chosen = (row == column).astype(full).astype(low)
        slot_ref[:, lanes] = dot(chosen, sums[start : start + total])
    second_ref[...] = jnp.concatenate(seconds, axis=1).reshape(width)
    first = jnp.zeros((width, LANES), full)
    for pair in range(pairs):
        for part in range(3):
            lanes = slice(part * width + pair * LANES, part * width + (pair + 1) * LANES)
            start = base + (pair * 3 + part) * width
            grad = sums[start : start + width].astype(full)
            qkv_ref[:, lanes] = grad
            first = first + grad * weight_ref[:, lanes].astype(full)
    row = jnp.sum(first.T, axis=0, keepdims=True)
    first_ref[...] = (row / gain_ref[...].reshape(1, width)).reshape(width)


def finish(parts, weight, gain, experts, own):
    width = weight.shape[0]

    def kernel(*refs):
        finish_kernel(experts, *refs)

    return pl.pallas_call(
        kernel,
        in_specs=[whole_vmem] * (2 + len(parts)),
        out_specs=[whole_vmem] * 5,
        out_shape=[
            shape_of((width,), full),
            shape_of(weight.shape, full),
            shape_of((width, width), full),
            shape_of((width,), full),
            shape_of((own, width), full),
        ],
        scratch_shapes=[pltpu.VMEM((sum(part.shape[0] for part in parts), LANES), low)],
        compiler_params=params(20),
        cost_estimate=cost(3),
        name="finish",
    )(weight, gain, *parts)


def per_device(
    patches,
    image_ids,
    first_gain,
    qkv_weight,
    proj_weight,
    second_gain,
    slot_params,
    up_weight,
    down_weight,
    cotangent,
):
    groups = lax.axis_size("expert")
    copies = lax.axis_size("rows")
    devices = groups * copies
    _, length, width = patches.shape
    own = slot_params.shape[1]
    experts = own * groups
    spread = jnp.broadcast_to(slot_params.T[None], (groups, own, width))
    slots = lax.all_to_all(spread, "expert", 0, 0, tiled=True).reshape(experts, width)
    patches = patches[0]
    cotangent = cotangent[0]
    probs, queries, keys, values, first_in, attn, rest, inverse, resid, second_in, same = attend(
        patches, image_ids, first_gain, qkv_weight, proj_weight, second_gain
    )
    second_in, dispatch, combine, send = route(second_in, slots, same, cotangent, groups)
    received = lax.all_to_all(send, "expert", 0, 0, tiled=True)
    back = run_experts(received, up_weight, down_weight)
    back = lax.all_to_all(back, "expert", 0, 0, tiled=True)
    others = [
        lax.ppermute(received, "rows", [(index, index ^ step) for index in range(copies)])
        for step in range(1, copies)
    ]
    saved = [image_ids, cotangent, combine, second_in, dispatch, slots]
    saved += [resid, second_gain, attn, rest, proj_weight, inverse]
    saved += [values, keys, queries, first_in]
    output, grad_resid, grads, terms, away = backward(back, saved, probs)
    layers = groups // 2

    def flip(array, expert, row):
        pairs = [
            (index, (index // copies ^ expert) * copies + (index % copies ^ row))
            for index in range(devices)
        ]
        return lax.ppermute(array, both_axes, pairs)

    away, others = lax.optimization_barrier((away, others))
    quarter = (terms.shape[0] // 8, LANES)
    mine, *sends = small_call(
        core_kernel, [shape_of(quarter, full)] + [shape_of(quarter, low)] * 3, "add_core",
        terms, flip(away, 0, 1),
    )
    arrived = [flip(send, step % 2, step // 2 * 2) for step, send in enumerate(sends, 1)]
    grads, _ = lax.optimization_barrier((grads, mine))
    patch_grad = patch_back(patches, first_gain, qkv_weight, grad_resid, grads)
    arrived, patch_grad = lax.optimization_barrier((arrived, patch_grad))
    mine = small_call(plane_kernel, shape_of(quarter, low), "add_plane", mine, *arrived)
    step = 1
    while step < layers:
        arrived = flip(mine, step * 2, 0)
        if step * 2 >= layers:
            others, _ = lax.optimization_barrier((others, mine))
            up_grad, down_grad = weight_grads([received] + others, up_weight, down_weight)
            arrived, up_grad, down_grad = lax.optimization_barrier((arrived, up_grad, down_grad))
        mine = small_call(
            line_kernel, shape_of(quarter, low), f"add_line_{step}", mine, arrived
        )
        step *= 2
    arrived = [flip(mine, step % 2, step // 2 * 2) for step in range(1, 4)]
    parts = [mine] + arrived
    parts = parts + [flip(part, 0, 1) for part in parts]
    first_grad, qkv_grad, proj_grad, second_grad, slot_grad = finish(
        parts, qkv_weight, first_gain, experts, own
    )
    return (
        output[None],
        patch_grad[None],
        first_grad,
        qkv_grad,
        proj_grad,
        second_grad,
        slot_grad.T,
        up_grad,
        down_grad,
    )


def solution(mesh):
    return jax.shard_map(
        per_device,
        mesh=mesh,
        in_specs=(
            P(("expert", "rows"), None, None),
            P(("expert", "rows"), None),
            P(),
            P(),
            P(),
            P(),
            P(None, "expert"),
            P("expert", None, None),
            P("expert", None, None),
            P(("expert", "rows"), None, None),
        ),
        out_specs=(
            P(("expert", "rows"), None, None),
            P(("expert", "rows"), None, None),
            P(),
            P(),
            P(),
            P(),
            P(None, "expert"),
            P("expert", None, None),
            P("expert", None, None),
        ),
        check_vma=False,
    )
```
